32 devices in a mesh: rep: 4 (over y, x), wide: 8 (over z, core).
Axes of the slice: x: 2, y: 2, z: 4, core: 2. Of those that a mesh axis runs over, the one named last changes fastest.
Arguments:
- tokens: bfloat16 [64, 576, 768], P(('rep', 'wide')), may hold values from -6 to 6
- live_count: int32 [32], P(('rep', 'wide')), may hold values from 1 to 2, as said below
- dataset_id: int32 [64], P(('rep', 'wide')), may hold values from 0 to 9
- shift_flag: int32 [64], P(('rep', 'wide')), may hold values 0 or 1
- norm_gains: bfloat16 [2, 768], P(None, 'wide'), may hold values from 0.099609375 to 1.8984375
- w_qkv: bfloat16 [768, 2304], P('wide'), may hold values from -0.21875 to 0.21875
- w_attn_out: bfloat16 [768, 768], P('wide'), may hold values from -0.625 to 0.625
- w_fc1: bfloat16 [768, 3072], P('wide'), may hold values from -0.21875 to 0.21875
- w_fc2: bfloat16 [3072, 768], P('wide'), may hold values from -0.109375 to 0.109375
- w_reassemble: bfloat16 [768, 256], P('wide'), may hold values from -0.21875 to 0.21875
- conv_kernels: bfloat16 [4, 2304, 256], P(None, 'wide'), may hold values from -0.125 to 0.125
- w_head: bfloat16 [256, 256], P('wide'), may hold values from -0.375 to 0.375
- scale_table: bfloat16 [10, 256], P(None, 'wide'), may hold values from 0.5 to 2
- shift_table: bfloat16 [10, 256], P(None, 'wide'), may hold values from -3 to 3
- d_tokens_out: bfloat16 [64, 576, 768], P(('rep', 'wide')), may hold values from -6 to 6
- d_joined: bfloat16 [64, 2304, 256], P(('rep', 'wide')), may hold values from -6 to 6
Outputs:
- tokens_out: bfloat16 [64, 576, 768], P(('rep', 'wide'))
- joined: bfloat16 [64, 2304, 256], P(('rep', 'wide'))
- d_tokens: bfloat16 [64, 576, 768], P(('rep', 'wide'))
- g_norm_gains: float32 [2, 768], P(None, 'wide')
- g_w_qkv: float32 [768, 2304], P('wide')
- g_w_attn_out: float32 [768, 768], P('wide')
- g_w_fc1: float32 [768, 3072], P('wide')
- g_w_fc2: float32 [3072, 768], P('wide')
- g_w_reassemble: float32 [768, 256], P('wide')
- g_conv_kernels: float32 [4, 2304, 256], P(None, 'wide')
- g_w_head: float32 [256, 256], P('wide')
- g_scale_table: float32 [10, 256], P(None, 'wide')
- g_shift_table: float32 [10, 256], P(None, 'wide')
The draws below stay inside these ranges and needn't reach their ends.
Inputs may be any that keep to these rules, and one draw needn't show every extreme that they name: `live_count`: each device's count of live slots; slots at or past it are left out of every output and sum; the first device holds 2, the last one 1.
All inputs are finite; a program needn't handle non-finite values. No bound on the sum of `shift_flag` on one device may be relied on, other than what follows from the above.
Results may differ from the reference program's by a relative error of at most 0.024.
Values may be sent and summed in bfloat16 or wider, within the bound.
No kernel may reach another device: no remote copies, remote signals or barrier semaphores. Data moves between devices by JAX's collectives and lax.ppermute only.
A program may use at most 320 MiB of HBM per device.

```python
import math
import jax
import jax.numpy as jnp
from jax import lax

D = 768
HEADS = 12
HD = 64
FF = 3072
CH = 256
GRID = 24
DATASETS = 10
IMG_DEV = 2
PATCH_TOKENS = 576
IMAGES = 64


def draw_live_count(key, part):
    counts = jax.random.randint(key, (IMAGES // IMG_DEV,), 1, IMG_DEV + 1, dtype=jnp.int32)
    return counts.at[0].set(IMG_DEV).at[-1].set(1)


def plant(array, rng, smallest, largest):
    longest = array.shape.index(max(array.shape))
    spots = []
    for shift in (0, 1):
        where = [jax.random.randint(jax.random.fold_in(rng, axis), (), 0, length) for axis, length in enumerate(array.shape)]
        where[longest] = (where[longest] + shift) % array.shape[longest]
        spots.append(tuple(where))
    return array.at[spots[0]].set(smallest).at[spots[1]].set(largest)


def block_scale(own_key, dims, split, least, largest):
    factor_of = 1.0
    for axis_at, blocks in split:
        steps = jax.random.uniform(jax.random.fold_in(jax.random.fold_in(own_key, 6), axis_at), (blocks,), jnp.float32, least / len(split), largest / len(split))
        factor_of = factor_of * jnp.repeat(jnp.exp(steps), dims[axis_at] // blocks).reshape((-1,) + (1,) * (len(dims) - 1 - axis_at))
    return factor_of


def noise(key, shape, deviation, bound, pieces=(), held_as=jnp.bfloat16):
    array = deviation * jax.random.normal(key, shape, jnp.float32)
    if pieces:
        array = array * block_scale(key, shape, pieces, -0.22, 0.18)
    return jnp.clip(array, -bound, bound).astype(held_as)


def setup_inputs(seed: int = 0) -> dict:
    arg_keys = jax.random.split(jax.random.key(seed), 17)
    return {
        "tokens": noise(arg_keys[0], (IMAGES, PATCH_TOKENS, D), 1.0, 6.0, ((0, 32),)),
        "live_count": draw_live_count(jax.random.fold_in(arg_keys[16], 71), 0),
        "dataset_id": plant(jax.random.randint(arg_keys[2], (IMAGES,), 0, DATASETS), jax.random.fold_in(arg_keys[2], 1), 0, DATASETS - 1).astype(jnp.int32),
        "shift_flag": plant((jax.random.randint(arg_keys[3], (IMAGES,), 0, 2) < 1).astype(jnp.int32), jax.random.fold_in(arg_keys[3], 1), 0, 1),
        "norm_gains": jnp.clip(1.0 + 0.18 * jax.random.normal(arg_keys[4], (2, D), jnp.float32), 0.099609375, 1.8984375).astype(jnp.bfloat16),
        "w_qkv": noise(arg_keys[5], (D, 3 * D), D ** -0.5, 0.21875, ((0, 8),)),
        "w_attn_out": noise(arg_keys[6], (D, D), (D // 8) ** -0.5, 0.625, ((0, 8),)),
        "w_fc1": noise(arg_keys[7], (D, FF), D ** -0.5, 0.21875, ((0, 8),)),
        "w_fc2": noise(arg_keys[8], (FF, D), FF ** -0.5, 0.109375, ((0, 8),)),
        "w_reassemble": noise(arg_keys[9], (D, CH), D ** -0.5, 0.21875, ((0, 8),)),
        "conv_kernels": noise(arg_keys[10], (4, 9 * CH, CH), (9 * CH) ** -0.5, 0.125, ((1, 8),)),
        "w_head": noise(arg_keys[11], (CH, CH), CH ** -0.5, 0.375, ((0, 8),)),
        "scale_table": jnp.clip(jnp.exp(math.log(2.0) - 1.3862944 * jax.random.uniform(arg_keys[12], (DATASETS, CH), jnp.float32) ** block_scale(arg_keys[12], (DATASETS, CH), ((1, 8),), -0.2, 0.2)), 0.5, 2.0).astype(jnp.bfloat16),
        "shift_table": noise(arg_keys[13], (DATASETS, CH), 0.5, 3.0, ((1, 8),)),
        "d_tokens_out": noise(arg_keys[14], (IMAGES, PATCH_TOKENS, D), 1.0, 6.0, ((0, 32),)),
        "d_joined": noise(arg_keys[15], (IMAGES, 4 * PATCH_TOKENS, CH), 1.0, 6.0, ((0, 32),)),
    }


HIGH = lax.Precision.HIGHEST

@jax.custom_vjp
def low(v):
    return lax.optimization_barrier(v.astype(jnp.bfloat16)).astype(jnp.float32)

@jax.custom_vjp
def low_back(v):
    return v

def low_keep(v):
    return (low(v), None)

def low_pass(kept, grad):
    return (grad,)

def back_keep(v):
    return (v, None)

def back_low(kept, grad):
    return (low(grad),)
low.defvjp(low_keep, low_pass)
low_back.defvjp(back_keep, back_low)

def matmul(left, right):
    return jnp.dot(left, right, precision=HIGH)

def normalize(values):
    centred = values - lax.optimization_barrier(jnp.mean(values, -1, keepdims=True))
    return centred * lax.rsqrt(lax.optimization_barrier(jnp.mean(centred * centred, -1, keepdims=True)) + 1e-06)

def upsample_table():
    target = jnp.arange(2 * GRID, dtype=jnp.int32)
    numer = target * (GRID - 1)
    lower = numer // (2 * GRID - 1)
    frac_part = (numer - lower * (2 * GRID - 1)).astype(jnp.float32) / (2 * GRID - 1)
    source = jnp.arange(GRID, dtype=jnp.int32)
    below = (source[None, :] == lower[:, None]).astype(jnp.float32) * (1.0 - frac_part[:, None])
    above = (source[None, :] == lower[:, None] + 1).astype(jnp.float32) * frac_part[:, None]
    return below + above

def upsample(field):
    grid_map = field.reshape(GRID, GRID, field.shape[-1])
    table = upsample_table()
    half_way = jnp.einsum('ay,yxc->axc', table, grid_map, precision=HIGH)
    return jnp.einsum('bx,axc->abc', table, half_way, precision=HIGH).reshape(4 * GRID * GRID, field.shape[-1])

def columns(field):
    grid_map = field.reshape(GRID, GRID, field.shape[-1])
    padded = jnp.pad(grid_map, ((1, 1), (1, 1), (0, 0)))
    parts = [padded[row_off:row_off + GRID, col_off:col_off + GRID, :] for row_off in range(3) for col_off in range(3)]
    return jnp.concatenate(parts, axis=-1).reshape(GRID * GRID, 9 * field.shape[-1])

def image_forward(params, image_rows, hot_row, flag_value, live_value):
    norm_gain, w_qkv, w_attn_out, w_fc1, w_fc2, w_reassemble, conv_kernels, w_head, scale_table, shift_table = params
    row_count = image_rows.shape[0]
    first_in = low(normalize(image_rows) * norm_gain[0])
    qkv_rows = low(low_back(matmul(first_in, w_qkv)))
    queries = qkv_rows[:, :D].reshape(row_count, HEADS, HD)
    key_rows = qkv_rows[:, D:2 * D].reshape(row_count, HEADS, HD)
    value_rows = qkv_rows[:, 2 * D:].reshape(row_count, HEADS, HD)
    scores = low_back(jnp.einsum('phd,qhd->hpq', queries, key_rows, precision=HIGH) * 0.125)
    attn_prob = low(jax.nn.softmax(scores, axis=-1))
    mixed = low(low_back(jnp.einsum('hpq,qhd->phd', attn_prob, value_rows, precision=HIGH).reshape(row_count, D)))
    middle = image_rows + low_back(matmul(mixed, w_attn_out))
    second_in = low(normalize(middle) * norm_gain[1])
    hidden = low_back(matmul(second_in, w_fc1))
    block_out = middle + low_back(matmul(low(jax.nn.gelu(hidden, approximate=False)), w_fc2))
    feature = low_back(matmul(low(block_out), w_reassemble))
    for unit in range(2):
        inner = low_back(matmul(columns(low(jax.nn.gelu(feature, approximate=False))), conv_kernels[2 * unit]))
        feature = feature + low_back(matmul(columns(low(jax.nn.gelu(inner, approximate=False))), conv_kernels[2 * unit + 1]))
    head_in = low(upsample(feature))
    head_out = low_back(matmul(head_in, w_head))
    scale_row = lax.optimization_barrier(jnp.sum(hot_row[:, None] * scale_table, 0))
    shift_row = flag_value * lax.optimization_barrier(jnp.sum(hot_row[:, None] * shift_table, 0))
    return (block_out * live_value, (head_out * scale_row[None, :] + shift_row[None, :]) * live_value)

def reference(tokens, live_count, dataset_id, shift_flag, norm_gains, w_qkv, w_attn_out, w_fc1, w_fc2, w_reassemble, conv_kernels, w_head, scale_table, shift_table, d_tokens_out, d_joined):
    slot_index = jnp.arange(IMAGES, dtype=jnp.int32)
    live_mask = (slot_index % IMG_DEV < jnp.repeat(live_count, IMG_DEV, total_repeat_length=IMAGES)).astype(jnp.float32)
    onehot = (dataset_id[:, None] == jnp.arange(DATASETS, dtype=jnp.int32)[None, :]).astype(jnp.float32)
    flag_values = shift_flag.astype(jnp.float32)
    params = tuple((weight.astype(jnp.float32) for weight in (norm_gains, w_qkv, w_attn_out, w_fc1, w_fc2, w_reassemble, conv_kernels, w_head, scale_table, shift_table)))
    group_count = IMAGES // IMG_DEV

    def whole(param_set, image_all):

        def per_group(packed):
            image_group, hot_group, flag_group, live_group = packed

            def one_image(image_rows, hot_row, flag_value, live_value):
                return image_forward(param_set, image_rows, hot_row, flag_value, live_value)
            return jax.vmap(one_image)(image_group, hot_group, flag_group, live_group)
        outputs = lax.map(jax.checkpoint(per_group), (image_all.reshape(group_count, IMG_DEV, PATCH_TOKENS, D), onehot.reshape(group_count, IMG_DEV, DATASETS), flag_values.reshape(group_count, IMG_DEV), live_mask.reshape(group_count, IMG_DEV)))
        return (outputs[0].reshape(IMAGES, PATCH_TOKENS, D), outputs[1].reshape(IMAGES, 4 * PATCH_TOKENS, CH))
    (block_all, joined_all), pullback = jax.vjp(whole, params, tokens.astype(jnp.float32))
    grad_params, grad_tokens = pullback((d_tokens_out.astype(jnp.float32), d_joined.astype(jnp.float32)))
    return (block_all.astype(jnp.bfloat16), joined_all.astype(jnp.bfloat16), grad_tokens.astype(jnp.bfloat16), grad_params[0], grad_params[1], grad_params[2], grad_params[3], grad_params[4], grad_params[5], grad_params[6], grad_params[7], grad_params[8], grad_params[9])
```

```python
import jax
import jax.numpy as jnp
from jax import lax
from jax.sharding import PartitionSpec as P

D = 768
HEADS = 12
HD = 64
GRID = 24
DATASETS = 10
F32 = jnp.float32
BF16 = jnp.bfloat16
BOTH = ("rep", "wide")


def mm(left, right):
    return jnp.dot(left, right, preferred_element_type=F32)


def mm_tn(left, right):
    return lax.dot_general(left, right, (((0,), (0,)), ((), ())), preferred_element_type=F32)


def mm_nt(left, right):
    return lax.dot_general(left, right, (((1,), (1,)), ((), ())), preferred_element_type=F32)


class Links:
    def __init__(self):
        rep = lax.axis_index("rep")
        wide = lax.axis_index("wide")
        self.bit = {
            "y": rep // 2,
            "x": rep % 2,
            "z1": wide // 4,
            "z0": (wide // 2) % 2,
            "c": wide % 2,
        }
        self.flip = {"y": 16, "x": 8, "z1": 4, "z0": 2, "c": 1}

    def swap(self, value, name):
        pairs = [(i, i ^ self.flip[name]) for i in range(32)]
        return lax.ppermute(value, BOTH, pairs)

    def both(self, value, name, axis):
        other = self.swap(value, name)
        first = self.bit[name] == 0
        return jnp.stack([jnp.where(first, value, other), jnp.where(first, other, value)], axis)

    def halve(self, value, name, axis):
        mine = lax.dynamic_index_in_dim(value, self.bit[name], axis, keepdims=False)
        theirs = lax.dynamic_index_in_dim(value, 1 - self.bit[name], axis, keepdims=False)
        got = self.swap(theirs, name)
        return (mine.astype(F32) + got.astype(F32)).astype(value.dtype)

    def gather_small(self, value):
        value = self.both(value, "z0", 0)
        value = self.both(value, "z1", 0)
        value = self.both(value, "c", 2)
        return value.reshape((8,) + value.shape[3:])

    def plane_gather(self, first, second):
        first = self.both(self.both(first, "x", 0), "y", 0)
        second = self.both(self.both(second, "y", 0), "x", 1)
        return first, second

    def gather(self, piece):
        piece = self.both(piece, "z0", 0)
        piece = self.both(piece, "z1", 0)
        first, second = self.plane_gather(piece[:, :, 0], piece[:, :, 1])
        value = jnp.stack([first, second], 4)
        value = self.both(value, "c", 4)
        return value

    def scatter(self, value):
        value = self.halve(value, "c", 0)
        first, second = value[:, :, :, 0], value[:, :, :, 1]
        first = self.halve(self.halve(first, "x", 2), "y", 1)
        second = self.halve(self.halve(second, "y", 1), "x", 1)
        value = jnp.stack([first, second], 1)
        value = value.reshape((2, 2) + value.shape[1:])
        value = self.halve(value, "z1", 0)
        value = self.halve(value, "z0", 0)
        first, second = self.plane_gather(value[0], value[1])
        return jnp.stack([first, second], 2)

    def quarter(self, shard):
        rows, cols = shard.shape[-2] // 2, shard.shape[-1] // 2
        shard = lax.dynamic_slice_in_dim(shard, self.bit["y"] * rows, rows, shard.ndim - 2)
        return lax.dynamic_slice_in_dim(shard, self.bit["x"] * cols, cols, shard.ndim - 1)


def gather_weight(links, shard):
    rows, cols = shard.shape
    piece = links.quarter(shard).reshape(2, rows // 4, cols // 2)
    value = links.gather(piece)
    return value.transpose(2, 3, 4, 0, 5, 6, 1, 7).reshape(8 * rows, cols)


def scatter_grad(links, grad):
    rows, cols = grad.shape[0] // 8, grad.shape[1]
    value = grad.astype(BF16).reshape(4, 2, 2, 2, rows // 4, 2, cols // 2)
    value = value.transpose(1, 0, 2, 5, 3, 4, 6)
    value = links.scatter(value)
    return value.transpose(0, 2, 3, 1, 4).reshape(rows, cols).astype(F32)


def sum_small(links, value):
    value = value.reshape((4, 2) + value.shape[1:])
    value = links.halve(value, "c", 1)
    value = value.reshape((2, 2) + value.shape[1:])
    value = links.halve(value, "z1", 0)
    value = links.halve(value, "z0", 0)
    value = value + links.swap(value, "x")
    return value + links.swap(value, "y")


def normalize(values):
    centred = values - jnp.mean(values, -1, keepdims=True)
    recip = lax.rsqrt(jnp.mean(centred * centred, -1, keepdims=True) + 1e-06)
    return centred * recip, recip


def norm_transpose(grad_normed, normed, recip):
    return recip * (
        grad_normed
        - jnp.mean(grad_normed, -1, keepdims=True)
        - normed * jnp.mean(grad_normed * normed, -1, keepdims=True)
    )


def gelu_pair(values):
    cdf = 0.5 * (1.0 + lax.erf(values * 0.7071067811865476))
    pdf = 0.3989422804014327 * jnp.exp(-0.5 * values * values)
    return values * cdf, cdf + values * pdf


def upsample_pair():
    target = jnp.arange(2 * GRID, dtype=jnp.int32)
    numer = target * (GRID - 1)
    lower = numer // (2 * GRID - 1)
    frac_part = (numer - lower * (2 * GRID - 1)).astype(F32) / (2 * GRID - 1)
    source = jnp.arange(GRID, dtype=jnp.int32)
    below = (source[None, :] == lower[:, None]).astype(F32) * (1.0 - frac_part[:, None])
    above = (source[None, :] == lower[:, None] + 1).astype(F32) * frac_part[:, None]
    table = below + above
    pair = table[:, None, :, None] * table[None, :, None, :]
    return pair.reshape(4 * GRID * GRID, GRID * GRID).astype(BF16)


def conv(maps, kernel):
    field = maps.reshape(-1, GRID, GRID, maps.shape[-1])
    out = lax.conv_general_dilated(
        field, kernel.reshape(3, 3, maps.shape[-1], -1), (1, 1), "SAME",
        dimension_numbers=("NHWC", "HWIO", "NHWC"), preferred_element_type=F32)
    return out.reshape(maps.shape[0], GRID * GRID, -1)


def conv_back(grads, kernel):
    flipped = kernel.reshape(3, 3, -1, kernel.shape[-1])[::-1, ::-1]
    field = grads.reshape(-1, GRID, GRID, grads.shape[-1])
    out = lax.conv_general_dilated(
        field, flipped, (1, 1), "SAME",
        dimension_numbers=("NHWC", "HWOI", "NHWC"), preferred_element_type=F32)
    return out.reshape(grads.shape[0], GRID * GRID, -1)


def columns(maps):
    field = maps.reshape(-1, GRID, GRID, maps.shape[-1])
    padded = jnp.pad(field, ((0, 0), (1, 1), (1, 1), (0, 0)))
    parts = [padded[:, r:r + GRID, c:c + GRID, :] for r in range(3) for c in range(3)]
    return jnp.concatenate(parts, -1).reshape(-1, 9 * maps.shape[-1])


def conv_weight_grad(maps, grads):
    return mm_tn(columns(maps), grads.reshape(-1, grads.shape[-1]))


def layer(weights, tokens, live, onehot, flags, d_tokens_out, d_joined):
    gains, w_qkv, w_out, w_fc1, w_fc2, w_re, w_conv, w_head, scale_table, shift_table = weights
    images, count = tokens.shape[0], tokens.shape[1]
    rows = images * count
    live_rows = jnp.repeat(live, count)[:, None]
    gains = gains.astype(F32)
    scale = jnp.sum(onehot[:, :, None] * scale_table.astype(F32)[None], 1)
    shift = flags[:, None] * jnp.sum(onehot[:, :, None] * shift_table.astype(F32)[None], 1)
    pair = upsample_pair()
    down = jnp.einsum("ts,itc->isc", pair, d_joined, preferred_element_type=F32) * live[:, None, None]
    g_shift_rows = flags[:, None] * jnp.sum(d_joined.astype(F32), 1) * live[:, None]

    x = tokens.reshape(rows, D).astype(F32)
    n1, rs1 = normalize(x)
    a1 = (n1 * gains[0]).astype(BF16)
    qkv = mm(a1, w_qkv).astype(BF16)
    heads = qkv.reshape(images, count, 3, HEADS, HD)
    query, key, value = heads[:, :, 0], heads[:, :, 1], heads[:, :, 2]
    scores = jnp.einsum("iphd,iqhd->ihpq", query, key, preferred_element_type=F32) * 0.125
    top = jnp.max(scores, -1, keepdims=True)
    powers = jnp.exp(scores - top)
    prob = (powers / jnp.sum(powers, -1, keepdims=True)).astype(BF16)
    mixed = jnp.einsum("ihpq,iqhd->iphd", prob, value, preferred_element_type=F32).astype(BF16)
    o = mixed.reshape(rows, D)
    x2 = x + mm(o, w_out)
    n2, rs2 = normalize(x2)
    a2 = (n2 * gains[1]).astype(BF16)
    gg, slope = gelu_pair(mm(a2, w_fc1))
    gg, slope = gg.astype(BF16), slope.astype(BF16)
    x3 = x2 + mm(gg, w_fc2)
    tokens_out = (x3 * live_rows).astype(BF16).reshape(tokens.shape)
    x3b = x3.astype(BF16)
    z = mm(x3b, w_re).reshape(images, count, -1)
    kept = []
    for unit in range(2):
        t1, s1 = gelu_pair(z)
        t1 = t1.astype(BF16)
        t2, s2 = gelu_pair(conv(t1, w_conv[2 * unit]))
        t2 = t2.astype(BF16)
        z = z + conv(t2, w_conv[2 * unit + 1])
        kept.append((t1, s1.astype(BF16), t2, s2.astype(BF16)))
    zb = z.astype(BF16).reshape(rows, -1)
    head = mm(zb, w_head).reshape(images, count, -1)
    hd = jnp.einsum("ts,isc->itc", pair, head.astype(BF16), preferred_element_type=F32)
    joined = ((hd * scale[:, None] + shift[:, None]) * live[:, None, None]).astype(BF16)

    g_scale_rows = jnp.sum(head * down, 1)
    g_scale = jnp.einsum("ik,ic->kc", onehot, g_scale_rows, precision=lax.Precision.HIGHEST)
    g_shift = jnp.einsum("ik,ic->kc", onehot, g_shift_rows, precision=lax.Precision.HIGHEST)
    dq_map = (down * scale[:, None]).astype(BF16).reshape(rows, -1)
    g_head = mm_tn(zb, dq_map)
    dz = mm_nt(dq_map, w_head).reshape(images, count, -1)
    g_conv = [None] * 4
    for unit in (1, 0):
        t1, s1, t2, s2 = kept[unit]
        dc2 = dz.astype(BF16)
        g_conv[2 * unit + 1] = conv_weight_grad(t2, dc2)
        dc1 = (conv_back(dc2, w_conv[2 * unit + 1]) * s2).astype(BF16)
        g_conv[2 * unit] = conv_weight_grad(t1, dc1)
        dz = dz + s1 * conv_back(dc1, w_conv[2 * unit])
    dr = dz.astype(BF16).reshape(rows, -1)
    g_re = mm_tn(x3b, dr)
    dx3 = d_tokens_out.reshape(rows, D).astype(F32) * live_rows + mm_nt(dr, w_re)
    dm = dx3.astype(BF16)
    g_fc2 = mm_tn(gg, dm)
    du = (mm_nt(dm, w_fc2) * slope).astype(BF16)
    g_fc1 = mm_tn(a2, du)
    da2 = mm_nt(du, w_fc1)
    g_gain2 = jnp.sum(da2 * n2, 0)
    dx2 = dx3 + norm_transpose(da2 * gains[1], n2, rs2)
    da = dx2.astype(BF16)
    g_out = mm_tn(o, da)
    do = mm_nt(da, w_out).astype(BF16).reshape(images, count, HEADS, HD)
    dv = jnp.einsum("ihpq,iphd->iqhd", prob, do, preferred_element_type=F32)
    dp = jnp.einsum("iphd,iqhd->ihpq", do, value, preferred_element_type=F32)
    probf = prob.astype(F32)
    ds = (probf * (dp - jnp.sum(probf * dp, -1, keepdims=True))).astype(BF16)
    dq = jnp.einsum("ihpq,iqhd->iphd", ds, key, preferred_element_type=F32) * 0.125
    dk = jnp.einsum("ihpq,iphd->iqhd", ds, query, preferred_element_type=F32) * 0.125
    dqkv = jnp.stack([dq, dk, dv], 2).astype(BF16).reshape(rows, 3 * D)
    g_qkv = mm_tn(a1, dqkv)
    da1 = mm_nt(dqkv, w_qkv)
    g_gain1 = jnp.sum(da1 * n1, 0)
    d_tokens = (dx2 + norm_transpose(da1 * gains[0], n1, rs1)).astype(BF16).reshape(tokens.shape)
    grads = (jnp.stack([g_gain1, g_gain2]), g_qkv, g_out, g_fc1, g_fc2, g_re, g_conv, g_head, g_scale, g_shift)
    return tokens_out, joined, d_tokens, grads


def shards(tokens, live_count, dataset_id, shift_flag, norm_gains, w_qkv, w_attn_out, w_fc1, w_fc2, w_reassemble,
           conv_kernels, w_head, scale_table, shift_table, d_tokens_out, d_joined):
    slots = tokens.shape[0]
    live = (jnp.arange(slots, dtype=jnp.int32) < live_count[0]).astype(F32)
    onehot = (dataset_id[:, None] == jnp.arange(DATASETS, dtype=jnp.int32)[None, :]).astype(F32)
    flags = shift_flag.astype(F32)
    neighbours = (lax.axis_size("rep"), lax.axis_size("wide")) == (4, 8)
    if neighbours:
        links = Links()
        small = jnp.concatenate([norm_gains.reshape(-1), scale_table.reshape(-1), shift_table.reshape(-1)])
        small = links.gather_small(small)
        g, t = norm_gains.shape[1], scale_table.shape[1]
        def wide_cols(part, lead):
            return part.reshape(8, lead, -1).transpose(1, 0, 2).reshape(lead, -1)
        gains = wide_cols(small[:, :2 * g], 2)
        scales = wide_cols(small[:, 2 * g:2 * g + DATASETS * t], DATASETS)
        shifts = wide_cols(small[:, 2 * g + DATASETS * t:], DATASETS)
        weights = (gains, gather_weight(links, w_qkv), gather_weight(links, w_attn_out), gather_weight(links, w_fc1),
                   gather_weight(links, w_fc2), gather_weight(links, w_reassemble),
                   [gather_weight(links, conv_kernels[j]) for j in range(4)], gather_weight(links, w_head), scales, shifts)
    else:
        def whole(part, axis):
            return lax.all_gather(part, "wide", axis=axis, tiled=True)
        weights = (whole(norm_gains, 1), whole(w_qkv, 0), whole(w_attn_out, 0), whole(w_fc1, 0), whole(w_fc2, 0),
                   whole(w_reassemble, 0), whole(conv_kernels, 1), whole(w_head, 0), whole(scale_table, 1),
                   whole(shift_table, 1))
    tokens_out, joined, d_tokens, grads = layer(weights, tokens, live, onehot, flags, d_tokens_out, d_joined)
    g_gains, g_qkv, g_out, g_fc1, g_fc2, g_re, g_conv, g_head, g_scale, g_shift = grads
    if neighbours:
        def by_shard(part):
            return part.reshape(part.shape[0], 8, -1).transpose(1, 0, 2).reshape(8, -1)
        small = jnp.concatenate([by_shard(g_gains), by_shard(g_scale), by_shard(g_shift)], 1)
        small = sum_small(links, small)
        g_gains = small[:2 * g].reshape(2, g)
        g_scale = small[2 * g:2 * g + DATASETS * t].reshape(DATASETS, t)
        g_shift = small[2 * g + DATASETS * t:].reshape(DATASETS, t)
        sums = (g_gains, scatter_grad(links, g_qkv), scatter_grad(links, g_out), scatter_grad(links, g_fc1),
                scatter_grad(links, g_fc2), scatter_grad(links, g_re),
                jnp.stack([scatter_grad(links, part) for part in g_conv]), scatter_grad(links, g_head), g_scale, g_shift)
    else:
        def share(part, axis):
            part = lax.psum_scatter(part.astype(BF16), "wide", scatter_dimension=axis, tiled=True)
            return lax.psum(part, "rep").astype(F32)
        sums = (share(g_gains, 1), share(g_qkv, 0), share(g_out, 0), share(g_fc1, 0), share(g_fc2, 0), share(g_re, 0),
                share(jnp.stack(g_conv), 1), share(g_head, 0), share(g_scale, 1), share(g_shift, 1))
    return (tokens_out, joined, d_tokens) + sums


def solution(mesh):
    images = P(BOTH, None, None)
    slots = P(BOTH)
    rows = P("wide", None)
    cols = P(None, "wide")
    kernels = P(None, "wide", None)
    return jax.shard_map(
        shards,
        mesh=mesh,
        in_specs=(images, slots, slots, slots, cols, rows, rows, rows, rows, rows, kernels, rows, cols, cols, images, images),
        out_specs=(images, images, images, cols, rows, rows, rows, rows, rows, kernels, rows, cols, cols),
        check_vma=False,
    )
```

```python
import math

import jax
import jax.numpy as jnp
from jax import lax
from jax.experimental import pallas as pl
from jax.experimental.pallas import tpu as pltpu
from jax.sharding import PartitionSpec as P

D = 768
HEADS = 12
HD = 64
GRID = 24
COUNT = GRID * GRID
DATASETS = 10
NH = 4
F32 = jnp.float32
BF16 = jnp.bfloat16
BOTH = ("rep", "wide")
VMEM = 60 << 20


def mm(left, right):
    return jnp.dot(left, right, preferred_element_type=F32)


def mm_tn(left, right):
    return lax.dot_general(left, right, (((0,), (0,)), ((), ())), preferred_element_type=F32)


def mm_nt(left, right):
    return lax.dot_general(left, right, (((1,), (1,)), ((), ())), preferred_element_type=F32)


def spec(shape, dtype=BF16):
    return jax.ShapeDtypeStruct(shape, dtype)


def whole(shape):
    return pl.BlockSpec(shape, lambda *_: (0,) * len(shape), pipeline_mode=pl.Buffered(1))


def params():
    return pltpu.CompilerParams(vmem_limit_bytes=VMEM)


def cost(macs, size):
    return pl.CostEstimate(flops=2 * int(macs), bytes_accessed=int(size), transcendentals=0)


FLIP = {"y": 16, "x": 8, "z1": 4, "z0": 2, "c": 1}


def swap(value, *names):
    flip = sum(FLIP[name] for name in names)
    return lax.ppermute(value, BOTH, [(i, i ^ flip) for i in range(32)])


def bits():
    rep, wide = lax.axis_index("rep"), lax.axis_index("wide")
    return {"y": rep // 2, "x": rep % 2, "z1": wide // 4, "z0": (wide // 2) % 2, "c": wide % 2}


def bit_vector():
    b = bits()
    return jnp.stack([b[k] for k in ("y", "x", "z1", "z0", "c")]).astype(jnp.int32)


def both(value, name):
    other = swap(value, name)
    first = bits()[name] == 0
    return jnp.stack([jnp.where(first, value, other), jnp.where(first, other, value)])


def gather(piece, order):
    value = jnp.stack([piece, swap(piece, "z0"), swap(piece, "z1"), swap(piece, "z1", "z0")])
    value = jnp.concatenate([value, swap(value, order[0])])
    other = swap(value, order[1])
    return value, other, swap(value, "c"), swap(other, "c")


def scatter(keep, send, order):
    def add(*terms):
        return sum(term.astype(F32) for term in terms).astype(BF16)

    got = swap(send, "c")
    for name, half in ((order[0], 8), (order[1], 4)):
        mine, theirs = add(keep[:half], got[:half]), add(keep[half:], got[half:])
        keep, got = mine, swap(theirs, name)
    terms = [add(keep[i], got[i]) for i in range(4)]
    total = add(terms[0], swap(terms[1], "z0"), swap(terms[2], "z1"), swap(terms[3], "z1", "z0"))
    return total, swap(total, order[1]), swap(total, order[0]), swap(total, *order)


def locate(me, order, plane, z, core):
    place = {order[0]: plane[0], order[1]: plane[1]}
    shard = ((me[2] ^ z[0]) * 2 + (me[3] ^ z[1])) * 2 + (me[4] ^ core)
    return shard, me[0] ^ place["y"], me[1] ^ place["x"]


def target(ref, lead, shard, y, x):
    rows, cols = ref.shape[-2] // 16, ref.shape[-1] // 2
    at = pl.ds(pl.multiple_of((shard * 2 + y) * rows, 16), rows), pl.ds(pl.multiple_of(x * cols, 128), cols)
    return ref.at[(lead,) + at] if lead is not None else ref.at[at]


def parts_of(shapes):
    entries = []
    for k, shape in enumerate(shapes):
        for lead in (range(shape[0]) if len(shape) == 3 else (None,)):
            entries.append((k, lead, shape[-2] // 16, shape[-1] // 2))
    beside = len({e[2] for e in entries}) == 1 and len({e[3] for e in entries}) > 1
    out, at = [], 0
    for k, lead, r, n in entries:
        out.append((k, lead, (0, r), (at, n)) if beside else (k, lead, (at, r), (0, n)))
        at += n if beside else r
    return out


def piece_shape(shapes):
    parts = parts_of(shapes)
    return max(p[2][0] + p[2][1] for p in parts), max(p[3][0] + p[3][1] for p in parts)


def cut(shards, shapes):
    b = bits()
    out = jnp.zeros(piece_shape(shapes), BF16)
    for k, lead, (r0, r), (c0, n) in parts_of(shapes):
        shard = shards[k] if lead is None else shards[k][lead]
        part = lax.dynamic_slice(shard, (b["y"] * r, b["x"] * n), (r, n))
        out = lax.dynamic_update_slice(out, part, (r0, c0))
    return out


def assemble(pieces, shapes, order, me):
    parts = parts_of(shapes)
    copies = 32 * len(parts)

    def body(me_ref, *refs):
        ins, outs, sem = refs[:4], refs[4:-1], refs[-1]
        started = []
        for a in range(4):
            second, core = a % 2, a // 2
            for s in range(8):
                shard, y, x = locate(me_ref, order, (s // 4, second), (s // 2 % 2, s % 2), core)
                for k, lead, (r0, r), (c0, n) in parts:
                    copy = pltpu.make_async_copy(
                        ins[a].at[s, pl.ds(r0, r), pl.ds(c0, n)], target(outs[k], lead, shard, y, x), sem.at[len(started)])
                    copy.start()
                    started.append(copy)
        for copy in started:
            copy.wait()

    return pl.pallas_call(
        body,
        grid=(1,),
        in_specs=[pl.BlockSpec(memory_space=pltpu.SMEM)] + [pl.BlockSpec(memory_space=pl.ANY)] * 4,
        out_specs=[whole(s) for s in shapes],
        out_shape=[spec(s) for s in shapes],
        scratch_shapes=[pltpu.SemaphoreType.DMA((copies,))],
        compiler_params=params(),
        cost_estimate=cost(0, 4 * sum(math.prod(s) for s in shapes)),
        name="assemble",
    )(me, *pieces)


def pack(grads, order, me):
    shapes = [g.shape for g in grads]
    parts = parts_of(shapes)
    copies = 32 * len(parts)

    def body(me_ref, *refs):
        ins, outs, sem = refs[:-3], refs[-3:-1], refs[-1]
        started = []
        for core in range(2):
            for s in range(16):
                shard, y, x = locate(me_ref, order, (s // 8, s // 4 % 2), (s // 2 % 2, s % 2), core)
                for k, lead, (r0, r), (c0, n) in parts:
                    copy = pltpu.make_async_copy(
                        target(ins[k], lead, shard, y, x), outs[core].at[s, pl.ds(r0, r), pl.ds(c0, n)], sem.at[len(started)])
                    copy.start()
                    started.append(copy)
        for copy in started:
            copy.wait()

    return pl.pallas_call(
        body,
        grid=(1,),
        in_specs=[pl.BlockSpec(memory_space=pltpu.SMEM)] + [whole(s) for s in shapes],
        out_specs=[pl.BlockSpec(memory_space=pl.ANY)] * 2,
        out_shape=[spec((16,) + piece_shape(shapes))] * 2,
        scratch_shapes=[pltpu.SemaphoreType.DMA((copies,))],
        compiler_params=params(),
        cost_estimate=cost(0, 4 * sum(math.prod(s) for s in shapes)),
        name="pack",
    )(me, *grads)


def shares(quarters, shapes, order):
    b = bits()
    first, second = b[order[0]] == 0, b[order[1]] == 0
    q = quarters
    ordered = {}
    for i in range(2):
        one = jnp.where(first, q[i], q[2 + i])
        two = jnp.where(first, q[2 + i], q[i])
        ordered[0, i], ordered[1, i] = one, two
    place = {}
    for i in range(2):
        place[i, 0] = jnp.where(second, ordered[i, 0], ordered[i, 1])
        place[i, 1] = jnp.where(second, ordered[i, 1], ordered[i, 0])

    def at(y, x):
        return place[(y, x) if order[0] == "y" else (x, y)]

    found = {}
    for k, lead, (r0, r), (c0, n) in parts_of(shapes):
        rows = [jnp.concatenate([at(y, x)[r0:r0 + r, c0:c0 + n] for x in range(2)], 1) for y in range(2)]
        found.setdefault(k, []).append(jnp.concatenate(rows, 0).astype(F32))
    return [found[k][0] if len(shapes[k]) == 2 else jnp.stack(found[k]) for k in range(len(shapes))]


def gather_small(value):
    value = both(value, "z0")
    value = both(value, "z1")
    value = jnp.moveaxis(both(value, "c"), 0, 2)
    return value.reshape((8,) + value.shape[3:])


def sum_small(value):
    b = bits()

    def halve(part, name, axis):
        mine = lax.dynamic_index_in_dim(part, b[name], axis, keepdims=False)
        theirs = lax.dynamic_index_in_dim(part, 1 - b[name], axis, keepdims=False)
        return mine + swap(theirs, name)

    value = value.reshape((2, 2, 2) + value.shape[1:])
    value = halve(value, "c", 2)
    value = halve(value, "z1", 0)
    value = halve(value, "z0", 0)
    value = value + swap(value, "x")
    return value + swap(value, "y")


def gelu_pair(values):
    cdf = 0.5 + 0.5 * lax.erf(values * 0.7071067811865476)
    pdf = 0.3989422804014327 * jnp.exp(-0.5 * values * values)
    return values * cdf, cdf + values * pdf


def normalize(values):
    centred = values - jnp.mean(values, -1, keepdims=True)
    recip = lax.rsqrt(jnp.mean(centred * centred, -1, keepdims=True) + 1e-06)
    return centred * recip, recip


def norm_transpose(grad_normed, normed, recip):
    return recip * (
        grad_normed
        - jnp.mean(grad_normed, -1, keepdims=True)
        - normed * jnp.mean(grad_normed * normed, -1, keepdims=True)
    )


def attention_body(q_ref, k_ref, v_ref, o_ref, e_ref, r_ref):
    for h in range(NH):
        c = slice(HD * h, HD * h + HD)
        s = mm_nt(k_ref[:, c], q_ref[:, c] * jnp.asarray(0.125, BF16))
        e = jnp.exp(s - jnp.max(s, 0, keepdims=True))
        r = 1.0 / jnp.sum(e, 0, keepdims=True)
        low = e.astype(BF16)
        e_ref[h] = low
        o_ref[:, c] = (mm_tn(v_ref[:, c], low) * r).T.astype(BF16)
        r_ref[0, h:h + 1, :] = r


def attention_specs():
    steps = HEADS // NH

    def cols(offset):
        return pl.BlockSpec((COUNT, NH * HD), lambda i, h: (i, offset + h))

    probs = pl.BlockSpec((NH, COUNT, COUNT), lambda i, h: (i * steps + h, 0, 0))
    sums = pl.BlockSpec((1, NH, COUNT), lambda i, h: (i * steps + h, 0, 0))
    return steps, cols, probs, sums


def attention(qkv):
    rows = qkv.shape[0]
    images = rows // COUNT
    steps, cols, probs, sums = attention_specs()
    return pl.pallas_call(
        attention_body,
        grid=(images, steps),
        in_specs=[cols(0), cols(steps), cols(2 * steps)],
        out_specs=[cols(0), probs, sums],
        out_shape=[spec((rows, D)), spec((images * HEADS, COUNT, COUNT)), spec((images * steps, NH, COUNT), F32)],
        compiler_params=params(),
        cost_estimate=cost(8 * images * HEADS * COUNT * COUNT * HD, images * HEADS * COUNT * COUNT * 2),
        name="attention",
    )(qkv, qkv, qkv)


def attention_back_body(q_ref, k_ref, v_ref, o_ref, e_ref, r_ref, do_ref, dq_ref, dk_ref, dv_ref):
    ones = jnp.ones((8, HD), BF16)
    for h in range(NH):
        c = slice(HD * h, HD * h + HD)
        do = do_ref[:, c]
        delta = mm_nt(ones, (do.astype(F32) * o_ref[:, c].astype(F32)).astype(BF16))[0:1]
        prob = e_ref[h].astype(F32) * r_ref[0, h:h + 1, :]
        dp = mm_nt(v_ref[:, c], do)
        ds = (prob * (dp - delta)).astype(BF16)
        dv_ref[:, c] = mm(prob.astype(BF16), do).astype(BF16)
        dk_ref[:, c] = (mm(ds, q_ref[:, c]) * 0.125).astype(BF16)
        dq_ref[:, c] = (mm_tn(ds, k_ref[:, c]) * 0.125).astype(BF16)


def attention_back(qkv, o, e, r, do):
    rows = qkv.shape[0]
    images = rows // COUNT
    steps, cols, probs, sums = attention_specs()
    return pl.pallas_call(
        attention_back_body,
        grid=(images, steps),
        in_specs=[cols(0), cols(steps), cols(2 * steps), cols(0), probs, sums, cols(0)],
        out_specs=[cols(0)] * 3,
        out_shape=[spec((rows, D))] * 3,
        compiler_params=params(),
        cost_estimate=cost(16 * images * HEADS * COUNT * COUNT * HD, images * HEADS * COUNT * COUNT * 2),
        name="attention_back",
    )(qkv, qkv, qkv, o, e, r, do)


def spread(value, out_ref, rows, sign):
    count, ch = value.shape
    at = lax.broadcasted_iota(jnp.int32, (count, 1), 0)
    col = at % GRID
    gap = jnp.zeros((GRID, ch), F32)
    for dx in (-1, 0, 1):
        step = sign * dx
        moved = value
        if step:
            moved = pltpu.roll(value, (-step) % count, 0)
            moved = jnp.where((col + step >= 0) & (col + step < GRID), moved, 0.0)
        for dy in (-1, 0, 1):
            block = 3 * (dy + 1) + dx + 1
            if sign * dy == 1:
                part = jnp.concatenate([moved[GRID:], gap], 0)
            elif sign * dy == -1:
                part = jnp.concatenate([gap, moved[:-GRID]], 0)
            else:
                part = moved
            out_ref[rows, block * ch:(block + 1) * ch] = part.astype(BF16)


def units_body(x_ref, wre_ref, w_ref, t1_ref, s1_ref, t2_ref, s2_ref, z_ref, cols):
    count = x_ref.shape[0]
    z = mm(x_ref[...], wre_ref[...])
    for unit in range(2):
        act, slope = gelu_pair(z)
        t1_ref[unit], s1_ref[unit] = act.astype(BF16), slope.astype(BF16)
        spread(act, cols, slice(0, count), 1)
        act, slope = gelu_pair(mm(cols[...], w_ref[2 * unit]))
        t2_ref[unit], s2_ref[unit] = act.astype(BF16), slope.astype(BF16)
        spread(act, cols, slice(0, count), 1)
        z = z + mm(cols[...], w_ref[2 * unit + 1])
    z_ref[...] = z.astype(BF16)


def units(x3b, w_re, w_conv):
    rows, ch = x3b.shape[0], w_re.shape[1]
    acts = pl.BlockSpec((2, COUNT, ch), lambda i: (0, i, 0))
    return pl.pallas_call(
        units_body,
        grid=(rows // COUNT,),
        in_specs=[pl.BlockSpec((COUNT, D), lambda i: (i, 0)), whole(w_re.shape), whole(w_conv.shape)],
        out_specs=[acts] * 4 + [pl.BlockSpec((COUNT, ch), lambda i: (i, 0))],
        out_shape=[spec((2, rows, ch))] * 4 + [spec((rows, ch))],
        scratch_shapes=[pltpu.VMEM((COUNT, 9 * ch), BF16)],
        compiler_params=params(),
        cost_estimate=cost(8 * rows * 9 * ch * ch, 12 << 20),
        name="units",
    )(x3b, w_re, w_conv)


def units_back_body(dq_ref, z_ref, x3b_ref, gt_ref, live_ref, whead_ref, w_ref, wre_ref, t1_ref, s1_ref, t2_ref, s2_ref,
                    gw_ref, ghead_ref, gre_ref, dx3_ref, moved, turned, dz_ref):
    rows, ch = dq_ref.shape
    images = rows // COUNT
    ghead_ref[...] = mm_tn(z_ref[...], dq_ref[...]).astype(BF16)
    dz_ref[...] = mm_nt(dq_ref[...], whead_ref[...])

    def back(index, grad, act_ref, unit):
        for i in range(images):
            at = slice(COUNT * i, COUNT * (i + 1))
            spread(grad[at], moved, at, -1)
        g = mm_tn(act_ref[unit], moved[...])
        for b in range(9):
            at = slice(ch * b, ch * (b + 1))
            gw_ref[index, at, :] = g[:, at].astype(BF16)
            turned[:, at] = w_ref[index, at, :]
        return mm_nt(moved[...], turned[...])

    for unit in (1, 0):
        grad = back(2 * unit + 1, dz_ref[...], t2_ref, unit) * s2_ref[unit].astype(F32)
        grad = back(2 * unit, grad, t1_ref, unit) * s1_ref[unit].astype(F32)
        dz_ref[...] += grad
    dr = dz_ref[...].astype(BF16)
    gre_ref[...] = mm_tn(x3b_ref[...], dr).astype(BF16)
    dx3_ref[...] = gt_ref[...].astype(F32) * live_ref[...] + mm_nt(dr, wre_ref[...])


def units_back(dq, z, x3b, gt, live, w_head, w_conv, w_re, t1, s1, t2, s2):
    rows, ch = dq.shape
    ins = (dq, z, x3b, gt, live, w_head, w_conv, w_re, t1, s1, t2, s2)
    outs = [spec(w_conv.shape), spec(w_head.shape), spec(w_re.shape), spec((rows, D), F32)]
    return pl.pallas_call(
        units_back_body,
        grid=(1,),
        in_specs=[whole(a.shape) for a in ins],
        out_specs=[whole(a.shape) for a in outs],
        out_shape=outs,
        scratch_shapes=[pltpu.VMEM((rows, 9 * ch), BF16), pltpu.VMEM((ch, 9 * ch), BF16), pltpu.VMEM((rows, ch), F32)],
        compiler_params=params(),
        cost_estimate=cost(14 * rows * 9 * ch * ch, 24 << 20),
        name="units_back",
    )(*ins)


def mlp_back_body(dx3_ref, a2_ref, gg_ref, slope_ref, w1_ref, w2_ref, x2_ref, gain_ref, g1_ref, g2_ref, dx2_ref, ggain_ref,
                  dm, total):
    step = pl.program_id(0)

    @pl.when(step == 0)
    def _():
        dm[...] = dx3_ref[...].astype(BF16)
        total[...] = jnp.zeros_like(total)

    g2_ref[...] = mm_tn(gg_ref[...], dm[...]).astype(BF16)
    du = (mm_nt(dm[...], w2_ref[...]) * slope_ref[...].astype(F32)).astype(BF16)
    g1_ref[...] = mm_tn(a2_ref[...], du).astype(BF16)
    total[...] += mm_nt(du, w1_ref[...])

    @pl.when(step == pl.num_programs(0) - 1)
    def _():
        rows = total.shape[0]
        chunk = rows // 6
        sums = jnp.zeros((1, D), F32)
        for p in range(0, rows, chunk):
            at = slice(p, p + chunk)
            da2 = total[at]
            n2, rs2 = normalize(x2_ref[at])
            sums = sums + jnp.sum(da2 * n2, 0, keepdims=True)
            dx2_ref[at] = dx3_ref[at] + norm_transpose(da2 * gain_ref[...], n2, rs2)
        ggain_ref[...] = sums


def mlp_back(dx3, a2, gg, slope, w1, w2, x2, gain, block=512):
    rows, ff = gg.shape
    cols = pl.BlockSpec((rows, block), lambda i: (0, i))
    one, two = pl.BlockSpec((D, block), lambda i: (0, i)), pl.BlockSpec((block, D), lambda i: (i, 0))
    full = whole((rows, D))
    return pl.pallas_call(
        mlp_back_body,
        grid=(ff // block,),
        in_specs=[full, full, cols, cols, one, two, full, whole((1, D))],
        out_specs=[one, two, full, whole((1, D))],
        out_shape=[spec(w1.shape), spec(w2.shape), spec((rows, D), F32), spec((1, D), F32)],
        scratch_shapes=[pltpu.VMEM((rows, D), BF16), pltpu.VMEM((rows, D), F32)],
        compiler_params=params(),
        cost_estimate=cost(4 * rows * D * ff, 40 << 20),
        name="mlp_back",
    )(dx3, a2, gg, slope, w1, w2, x2, gain)


def upsample_pair():
    size = 2 * GRID

    def weights(target, source):
        numer = target * (GRID - 1)
        lower = numer // (size - 1)
        frac = (numer - lower * (size - 1)).astype(F32) / (size - 1)
        return jnp.where(source == lower, 1.0 - frac, 0.0) + jnp.where(source == lower + 1, frac, 0.0)

    target = lax.broadcasted_iota(jnp.int32, (size * size, COUNT), 0)
    source = lax.broadcasted_iota(jnp.int32, (size * size, COUNT), 1)
    return (weights(target // size, source // GRID) * weights(target % size, source % GRID)).astype(BF16)


CHUNKS = (("x", "y"), ("y", "x"), ("x", "y"), ("y", "x"))


def shards(tokens, live_count, dataset_id, shift_flag, norm_gains, w_qkv, w_attn_out, w_fc1, w_fc2, w_reassemble,
           conv_kernels, w_head, scale_table, shift_table, d_tokens_out, d_joined):
    slots, count = tokens.shape[:2]
    rows = slots * count
    live = (jnp.arange(slots, dtype=jnp.int32) < live_count[0]).astype(F32)
    live_rows = jnp.repeat(live, count)[:, None]
    onehot = (dataset_id[:, None] == jnp.arange(DATASETS, dtype=jnp.int32)[None, :]).astype(F32)
    flags = shift_flag.astype(F32)
    neighbours = (lax.axis_size("rep"), lax.axis_size("wide")) == (4, 8)
    ch = w_head.shape[1]
    shard_sets = ((w_qkv,), (w_attn_out, w_fc1, w_reassemble), (w_fc2,), (conv_kernels, w_head))
    wide = lax.axis_size("wide")
    shape_sets = [[s.shape[:-2] + (s.shape[-2] * wide, s.shape[-1]) for s in group] for group in shard_sets]
    g, t = norm_gains.shape[1], scale_table.shape[1]
    if neighbours:
        me = bit_vector()
        small = jnp.concatenate([norm_gains.reshape(-1), scale_table.reshape(-1), shift_table.reshape(-1)])
        small = gather_small(small)

        def wide_cols(part, lead):
            return part.reshape(8, lead, -1).transpose(1, 0, 2).reshape(lead, -1)

        gains = wide_cols(small[:, :2 * g], 2)
        scales = wide_cols(small[:, 2 * g:2 * g + DATASETS * t], DATASETS)
        shifts = wide_cols(small[:, 2 * g + DATASETS * t:], DATASETS)
        full = []
        for group, shapes, order in zip(shard_sets, shape_sets, CHUNKS):
            full.append(assemble(gather(cut(group, shapes), order), shapes, order, me))
    else:
        def gathered(part, axis):
            return lax.all_gather(part, "wide", axis=axis, tiled=True)

        gains, scales, shifts = gathered(norm_gains, 1), gathered(scale_table, 1), gathered(shift_table, 1)
        full = [[gathered(s, s.ndim - 2) for s in group] for group in shard_sets]
    (f_qkv,), (f_out, f_fc1, f_re), (f_fc2,), (f_conv, f_head) = full

    gains = gains.astype(F32)
    scale = jnp.sum(onehot[:, :, None] * scales.astype(F32)[None], 1)
    shift = flags[:, None] * jnp.sum(onehot[:, :, None] * shifts.astype(F32)[None], 1)
    pair = upsample_pair()
    down = jnp.einsum("ts,itc->isc", pair, d_joined, preferred_element_type=F32) * live[:, None, None]
    g_shift_rows = flags[:, None] * jnp.sum(d_joined.astype(F32), 1) * live[:, None]
    x = tokens.reshape(rows, D).astype(F32)
    n1, rs1 = normalize(x)
    a1 = (n1 * gains[0]).astype(BF16)
    qkv = mm(a1, f_qkv).astype(BF16)
    o, e, r = attention(qkv)
    x2 = x + mm(o, f_out)
    n2, rs2 = normalize(x2)
    a2 = (n2 * gains[1]).astype(BF16)
    gg, slope = gelu_pair(mm(a2, f_fc1))
    gg, slope = gg.astype(BF16), slope.astype(BF16)
    x3 = x2 + mm(gg, f_fc2)
    tokens_out = (x3 * live_rows).astype(BF16).reshape(tokens.shape)
    x3b = x3.astype(BF16)
    t1, s1, t2, s2, zb = units(x3b, f_re, f_conv)
    head = mm(zb, f_head).reshape(slots, count, ch)
    hd = jnp.einsum("ts,isc->itc", pair, head.astype(BF16), preferred_element_type=F32)
    joined = ((hd * scale[:, None] + shift[:, None]) * live[:, None, None]).astype(BF16)

    g_scale_rows = jnp.sum(head * down, 1)
    g_scale = jnp.sum(onehot[:, :, None] * g_scale_rows[:, None, :], 0)
    g_shift = jnp.sum(onehot[:, :, None] * g_shift_rows[:, None, :], 0)
    dq_map = (down * scale[:, None]).astype(BF16).reshape(rows, ch)
    g_conv, g_head, g_re, dx3 = units_back(
        dq_map, zb, x3b, d_tokens_out.reshape(rows, D), live_rows, f_head, f_conv, f_re, t1, s1, t2, s2)
    g_fc1, g_fc2, dx2, g_gain2 = mlp_back(dx3, a2, gg, slope, f_fc1, f_fc2, x2, gains[1:2])
    da = dx2.astype(BF16)
    g_out = mm_tn(o, da).astype(BF16)
    do = mm_nt(da, f_out).astype(BF16)
    dqkv = attention_back(qkv, o, e, r, do)
    g_qkv = jnp.concatenate([mm_tn(a1, part).astype(BF16) for part in dqkv], 1)
    da1 = sum(mm_nt(part, f_qkv[:, D * i:D * (i + 1)]) for i, part in enumerate(dqkv))
    g_gain1 = jnp.sum(da1 * n1, 0)[None]
    d_tokens = (dx2 + norm_transpose(da1 * gains[0], n1, rs1)).astype(BF16).reshape(tokens.shape)

    grad_sets = ((g_qkv,), (g_out, g_fc1, g_re), (g_fc2,), (g_conv, g_head))
    g_gains = jnp.concatenate([g_gain1, g_gain2])
    if neighbours:
        sums = [None] * 4
        for i in (3, 2, 1, 0):
            keep, send = pack(grad_sets[i], CHUNKS[i], me)
            sums[i] = shares(scatter(keep, send, CHUNKS[i]), shape_sets[i], CHUNKS[i])

        def by_shard(part):
            return part.reshape(part.shape[0], 8, -1).transpose(1, 0, 2).reshape(8, -1)

        small = sum_small(jnp.concatenate([by_shard(g_gains), by_shard(g_scale), by_shard(g_shift)], 1))
        g_gains = small[:2 * g].reshape(2, g)
        g_scale = small[2 * g:2 * g + DATASETS * t].reshape(DATASETS, t)
        g_shift = small[2 * g + DATASETS * t:].reshape(DATASETS, t)
    else:
        def share(part, axis):
            part = lax.psum_scatter(part.astype(BF16), "wide", scatter_dimension=axis, tiled=True)
            return lax.psum(part, "rep").astype(F32)

        sums = [[share(part, part.ndim - 2) for part in group] for group in grad_sets]
        g_gains, g_scale, g_shift = share(g_gains, 1), share(g_scale, 1), share(g_shift, 1)
    (s_qkv,), (s_out, s_fc1, s_re), (s_fc2,), (s_conv, s_head) = sums
    return (tokens_out, joined, d_tokens, g_gains, s_qkv, s_out, s_fc1, s_fc2, s_re, s_conv, s_head, g_scale, g_shift)


def solution(mesh):
    images = P(BOTH, None, None)
    slots = P(BOTH)
    rows = P("wide", None)
    cols = P(None, "wide")
    kernels = P(None, "wide", None)
    return jax.shard_map(
        shards,
        mesh=mesh,
        in_specs=(images, slots, slots, slots, cols, rows, rows, rows, rows, rows, kernels, rows, cols, cols, images, images),
        out_specs=(images, images, images, cols, rows, rows, rows, rows, rows, kernels, rows, cols, cols),
        check_vma=False,
    )
```

```python
import math

import jax
import jax.numpy as jnp
from jax import lax
from jax.experimental import pallas as pl
from jax.experimental.pallas import tpu as pltpu
from jax.sharding import PartitionSpec as P

D = 768
HEADS = 12
HD = 64
GRID = 24
COUNT = GRID * GRID
DATASETS = 10
NH = 4
GROUPS = HEADS // NH
WIDTH = NH * HD
LANES = 128
F32 = jnp.float32
BF16 = jnp.bfloat16
BOTH = ("rep", "wide")
VMEM = 60 << 20


def mm(left, right):
    return jnp.dot(left, right, preferred_element_type=F32)


def mm_tn(left, right):
    return lax.dot_general(left, right, (((0,), (0,)), ((), ())), preferred_element_type=F32)


def mm_nt(left, right):
    return lax.dot_general(left, right, (((1,), (1,)), ((), ())), preferred_element_type=F32)


def spec(shape, dtype=BF16):
    return jax.ShapeDtypeStruct(shape, dtype)


def whole(shape):
    return pl.BlockSpec(shape, lambda *_: (0,) * len(shape), pipeline_mode=pl.Buffered(1))


def params():
    return pltpu.CompilerParams(vmem_limit_bytes=VMEM)


def cost(macs, size):
    return pl.CostEstimate(flops=2 * int(macs), bytes_accessed=int(size), transcendentals=0)


def lasts(microseconds):
    return pl.CostEstimate(flops=int(microseconds * 1.15e9), bytes_accessed=0, transcendentals=0)


FLIP = {"y": 16, "x": 8, "z1": 4, "z0": 2, "c": 1}
XY, YX = ("x", "y"), ("y", "x")


def swap(value, *names):
    flip = sum(FLIP[name] for name in names)
    return lax.ppermute(value, BOTH, [(i, i ^ flip) for i in range(32)])


def bits():
    rep, wide = lax.axis_index("rep"), lax.axis_index("wide")
    return {"y": rep // 2, "x": rep % 2, "z1": wide // 4, "z0": (wide // 2) % 2, "c": wide % 2}


def bit_vector():
    b = bits()
    return jnp.stack([b[k] for k in ("y", "x", "z1", "z0", "c")]).astype(jnp.int32)


class Line:
    def __init__(self):
        self.tokens = []

    def after(self, value):
        return lax.optimization_barrier((value, *self.tokens))[0] if self.tokens else value

    def run(self, call, first, *rest):
        out = call(self.after(first), *rest)
        self.tokens = jax.tree.leaves(out)[-1:]
        return out

    def run_all(self, call, *values):
        out = call(*(lax.optimization_barrier((*values, *self.tokens))[:len(values)]))
        self.tokens = jax.tree.leaves(out)
        return out


def locate(me, order, plane, z, core):
    place = {order[0]: plane[0], order[1]: plane[1]}
    shard = ((me[2] ^ z[0]) * 2 + (me[3] ^ z[1])) * 2 + (me[4] ^ core)
    return shard, me[0] ^ place["y"], me[1] ^ place["x"]


class Gather:
    def __init__(self, line, piece, at, axis):
        self.line, self.at, self.axis = line, at, axis
        self.got = [piece, swap(piece, "z0"), swap(piece, "z1"), swap(piece, "z1", "z0")]

    def over_first(self):
        def call(*parts):
            value = jnp.stack(parts)
            return [lax.slice_in_dim(value, 0, self.at, axis=self.axis + 1),
                    lax.slice_in_dim(value, self.at, value.shape[self.axis + 1], axis=self.axis + 1)]

        one, two = self.line.run_all(call, *self.got)
        self.got = [one, swap(one, "x"), two, swap(two, "y")]

    def over_second(self):
        def call(one, one_x, two, two_y):
            return [jnp.concatenate([one, one_x]), jnp.concatenate([two, two_y])]

        one, two = self.line.run_all(call, *self.got)
        self.pieces = []
        for value, name in ((one, "y"), (two, "x")):
            other = swap(value, name)
            self.pieces += [value, other, swap(value, "c"), swap(other, "c")]


PLANE = [[(s // 4, a % 2, s // 2 % 2, s % 2, a // 2) for s in range(8)] for a in range(4)]


def assemble(me, gathered, shapes, parts):
    at, axis = gathered.at, gathered.axis

    def halves(rows, cols):
        first, size = (rows, cols)[axis]
        out = []
        for low, high, shift in ((first, min(first + size, at), 0), (max(first, at), first + size, at)):
            span = (low - shift, high - low)
            out.append(None if high <= low else (span, cols, low - first, 0) if axis == 0 else (rows, span, 0, low - first))
        return out

    def body(me_ref, *refs):
        ins, outs, sem = refs[:8], refs[8:-1], refs[-1]
        started = []
        for half, order in enumerate((XY, YX)):
            for a, places in enumerate(PLANE):
                for s, (first, second, z1, z0, core) in enumerate(places):
                    shard, y, x = locate(me_ref, order, (first, second), (z1, z0), core)
                    for k, rows, cols, row, col in parts:
                        share = halves(rows, cols)[half]
                        if share is None or (row is None and (first or second)):
                            continue
                        (r0, r), (c0, n), down, across = share
                        source = ins[4 * half + a].at[s, pl.ds(r0, r), pl.ds(c0, n)]
                        if row is None:
                            place = outs[k].at[shard, pl.ds(down, r), pl.ds(across, n)]
                        else:
                            place = outs[k].at[pl.ds(pl.multiple_of(row(shard, y) + down, 16), r),
                                               pl.ds(pl.multiple_of(col(x) + across, LANES), n)]
                        copy = pltpu.make_async_copy(source, place, sem.at[len(started)])
                        copy.start()
                        started.append(copy)
        for copy in started:
            copy.wait()

    return pl.pallas_call(
        body,
        grid=(1,),
        in_specs=[pl.BlockSpec(memory_space=pltpu.SMEM)] + [pl.BlockSpec(memory_space=pl.ANY)] * 8,
        out_specs=[whole(s) for s in shapes],
        out_shape=[spec(s) for s in shapes],
        scratch_shapes=[pltpu.SemaphoreType.DMA((64 * len(parts),))],
        compiler_params=params(),
        cost_estimate=lasts(5),
        name="assemble",
    )(me, *gathered.pieces)


def total_of(terms):
    if len(terms) == 2:
        return terms[0] + terms[1]
    return sum(term.astype(F32) for term in terms).astype(BF16)


def in_four(total):
    size = total.shape[0] // 4
    return [total[size * i:size * (i + 1)] for i in range(4)]


def together(line, *jobs):
    counts = [len(job.terms) for job in jobs]

    def call(*terms):
        out = []
        for job, count in zip(jobs, counts):
            out.append(job.add(*terms[:count]))
            terms = terms[count:]
        return out

    for job, out in zip(jobs, line.run_all(call, *[term for job in jobs for term in job.terms])):
        job.send(out)


class Chunk:
    def __init__(self, line, keep, send, split):
        self.split, self.stage = split, 0
        self.terms = [keep, swap(line.after(send), "c")]

    def add(self, *terms):
        split = self.split
        if self.stage == 0 and split is None:
            return in_four(total_of(terms))
        if self.stage == 0:
            total = total_of(terms)
            return [total[:8, :split], total[8:, :split], total[:8, split:], total[8:, split:]]
        if split is None:
            return [total_of(terms)]
        one, two = terms[0] + terms[1], terms[2] + terms[3]
        if self.stage == 1:
            return [one[:4], one[4:], two[:4], two[4:]]
        return [jnp.concatenate([one, two], 1)]

    def send(self, out):
        if len(out) == 1:
            self.total = out[0]
        elif self.split is None:
            self.terms = [out[0], swap(out[1], "y"), swap(out[2], "x"), swap(out[3], "x", "y")]
        else:
            one, two = ("x", "y") if self.stage == 0 else ("y", "x")
            self.terms = [out[0], swap(out[1], one), out[2], swap(out[3], two)]
        self.stage += 1


class Along:
    def __init__(self, line, chunks):
        self.stage, self.rows = 0, [chunk.total.shape[1] for chunk in chunks]
        out = line.run_all(lambda *totals: in_four(jnp.concatenate(totals, 1)), *[chunk.total for chunk in chunks])
        self.terms = [out[0], swap(out[1], "z0"), swap(out[2], "z1"), swap(out[3], "z1", "z0")]

    def add(self, *terms):
        return [total_of(terms)[0]]

    def send(self, out):
        total = out[0]
        self.terms = [total, swap(total, "x"), swap(total, "y"), swap(total, "x", "y")]


class Whole:
    def __init__(self, value):
        self.terms, self.stage = [value, swap(value, "y")], 0

    def add(self, *terms):
        return [total_of(terms)]

    def send(self, out):
        self.terms = [out[0], swap(out[0], "x")]


def finish(me, alongs, places, shapes):
    ins = [t for along in alongs for t in along.terms]

    def body(me_ref, *refs):
        outs = refs[len(ins):len(ins) + len(shapes)]
        held = refs[len(ins) + len(shapes):]
        for c, parts in enumerate(places):
            for q in range(4):
                held[c][q] = refs[4 * c + q][...]
            for y in range(2):
                for x in range(2):
                    at = 2 * (me_ref[0] ^ y) + (me_ref[1] ^ x)
                    for k, r, r0, blocks, row, col in parts:
                        for b in range(blocks):
                            at_row = row(y) + (r * x if shapes[k][1] == LANES else 0)
                            outs[k][at_row:at_row + r, col(x, b):col(x, b) + LANES] = (
                                held[c][at, r0 + b * r:r0 + (b + 1) * r, :].astype(F32))

    return pl.pallas_call(
        body,
        grid=(1,),
        in_specs=[pl.BlockSpec(memory_space=pltpu.SMEM)] + [whole(a.shape) for a in ins],
        out_specs=[whole(s) for s in shapes],
        out_shape=[spec(s, F32) for s in shapes],
        scratch_shapes=[pltpu.VMEM((4,) + along.terms[0].shape, BF16) for along in alongs],
        compiler_params=params(),
        cost_estimate=lasts(3),
        name="finish",
    )(me, *ins)


PLAIN = "plain"


TABLE = 64


class Sink:
    def __init__(self, shapes, split, table=False):
        self.shapes, self.split, self.table = shapes, split, table
        rows = sum(k // 16 * (n // 2 // LANES) for k, n in shapes) + (TABLE // 4 if table else 0)
        if split == PLAIN:
            self.outs, self.scratch = [spec(s) for s in shapes], []
        else:
            self.outs = [spec((16, rows, LANES))] * 2
            self.scratch = [pltpu.VMEM((2, k, n // 2), BF16) for k, n in shapes]
            self.scratch += [pltpu.VMEM((TABLE, LANES), BF16)] if table else []

    def out_specs(self):
        return [whole(o.shape) for o in self.outs]

    def put(self, outs, held, k, rows, value):
        value = value.astype(BF16)
        half = self.shapes[k][1] // 2
        if self.split == PLAIN:
            outs[k][rows, :] = value
        else:
            held[k][0, rows, :] = value[:, :half]
            held[k][1, rows, :] = value[:, half:]

    def deliver(self, me_ref, outs, held):
        if self.split == PLAIN:
            return
        for core in range(2):
            for s in range(16):
                z = (s // 2 % 2, s % 2)
                places = [locate(me_ref, order, (s // 8, s // 4 % 2), z, core) for order in (XY, YX)]
                at = 0
                for k, (rows, cols) in enumerate(self.shapes):
                    r = rows // 16
                    for b in range(cols // 2 // LANES):
                        shard, y, x = places[0 if self.split is None or at < self.split else 1]
                        start = pl.multiple_of((shard * 2 + y) * r, 16)
                        outs[core][s, at:at + r, :] = held[k][x, pl.ds(start, r), b * LANES:(b + 1) * LANES]
                        at += r
                if self.table:
                    r = TABLE // 4
                    _, y, x = places[0 if self.split is None or at < self.split else 1]
                    outs[core][s, at:at + r, :] = held[-1][pl.ds(pl.multiple_of((2 * y + x) * r, 16), r), :]


def gelu_pair(values):
    cdf = 0.5 + 0.5 * lax.erf(values * 0.7071067811865476)
    pdf = 0.3989422804014327 * jnp.exp(-0.5 * values * values)
    return values * cdf, cdf + values * pdf


def normalize(values):
    centred = values - jnp.mean(values, -1, keepdims=True)
    recip = lax.rsqrt(jnp.mean(centred * centred, -1, keepdims=True) + 1e-06)
    return centred * recip, recip


def norm_transpose(grad_normed, normed, recip):
    return recip * (
        grad_normed
        - jnp.mean(grad_normed, -1, keepdims=True)
        - normed * jnp.mean(grad_normed * normed, -1, keepdims=True)
    )


SMALL = 16


def prepare(me, w_qkv, w_out, w_fc1, w_fc2, w_re, w_head, gains, scales, shifts):
    ff, ch = w_fc1.shape[1], w_re.shape[1]
    half = w_qkv.shape[0] // 2
    rows_two, rows_head = w_fc2.shape[0] // 2, w_head.shape[0] // 2
    n = w_qkv.shape[1] // 2

    def body(me_ref, qkv_ref, out_ref, fc1_ref, fc2_ref, re_ref, head_ref, gains_ref, scales_ref, shifts_ref,
             zero_ref, one_ref, two_ref):
        zero_ref[half:half + SMALL, :] = jnp.zeros((SMALL, n), BF16)
        zero_ref[half:half + DATASETS, 0:scales.shape[1]] = scales_ref[...]
        zero_ref[half:half + DATASETS, LANES:LANES + shifts.shape[1]] = shifts_ref[...]
        zero_ref[half:half + 2, 2 * LANES:2 * LANES + gains.shape[1]] = gains_ref[...]
        rows = pl.ds(pl.multiple_of(me_ref[0] * half, 16), half)
        rows_of_two = pl.ds(pl.multiple_of(me_ref[0] * rows_two, 16), rows_two)
        rows_of_head = pl.ds(pl.multiple_of(me_ref[0] * rows_head, 16), rows_head)
        for x in range(2):
            @pl.when(me_ref[1] == x)
            def _():
                zero_ref[0:half, :] = qkv_ref[rows, n * x:n * (x + 1)]
                one_ref[:, :D // 2] = out_ref[rows, D // 2 * x:D // 2 * (x + 1)]
                at = D // 2 + ff // 2
                one_ref[:, D // 2:at] = fc1_ref[rows, ff // 2 * x:ff // 2 * (x + 1)]
                one_ref[:, at:at + ch // 2] = re_ref[rows, ch // 2 * x:ch // 2 * (x + 1)]
                one_ref[0:rows_head, at + ch // 2:] = head_ref[rows_of_head, ch // 2 * x:ch // 2 * (x + 1)]
                two_ref[...] = fc2_ref[rows_of_two, D // 2 * x:D // 2 * (x + 1)]
        one_ref[rows_head:, D // 2 + ff // 2 + ch // 2:] = jnp.zeros((half - rows_head, LANES), BF16)

    ins = (w_qkv, w_out, w_fc1, w_fc2, w_re, w_head, gains, scales, shifts)
    outs = [spec((half + SMALL, n)), spec((half, D // 2 + ff // 2 + ch // 2 + LANES)), spec((rows_two, D // 2))]
    return pl.pallas_call(
        body,
        grid=(1,),
        in_specs=[pl.BlockSpec(memory_space=pltpu.SMEM)] + [whole(a.shape) for a in ins],
        out_specs=[whole(o.shape) for o in outs],
        out_shape=outs,
        compiler_params=params(),
        cost_estimate=lasts(2.4),
        name="prepare",
    )(me, *ins)


def norm_body(x_ref, out_ref):
    out_ref[...] = normalize(x_ref[...].astype(F32))[0]


def norm(x):
    rows = x.shape[0]
    block = pl.BlockSpec((rows // 4, D), lambda i: (i, 0))
    return pl.pallas_call(
        norm_body,
        grid=(4,),
        in_specs=[block],
        out_specs=block,
        out_shape=spec((rows, D), F32),
        compiler_params=params(),
        cost_estimate=lasts(4.4),
        name="norm",
    )(x)


def bilinear(targets, sources, first):
    size = 2 * GRID
    step = (GRID - 1) / (size - 1)

    def hat(target, source):
        return jnp.maximum(1.0 - jnp.abs(target.astype(F32) * step - source.astype(F32)), 0.0)

    target = lax.broadcasted_iota(jnp.int32, targets, targets.index(max(targets))) + first
    source = lax.broadcasted_iota(jnp.int32, sources, sources.index(max(sources)))
    return (hat(target // size, source // GRID) * hat(target % size, source % GRID)).astype(BF16)


def down_body(dj_ref, live_ref, flag_ref, down_ref, gshift_ref):
    step, images, size = pl.program_id(0), dj_ref.shape[0], dj_ref.shape[1]
    table = bilinear((1, size), (COUNT, 1), step * size)
    for i in range(images):
        part = mm(table, dj_ref[i])
        sums = jnp.sum(dj_ref[i].astype(F32), 0, keepdims=True)

        @pl.when(step == 0)
        def _():
            down_ref[i] = part
            gshift_ref[i] = sums

        @pl.when(step > 0)
        def _():
            down_ref[i] += part
            gshift_ref[i] += sums

        @pl.when(step == pl.num_programs(0) - 1)
        def _():
            down_ref[i] = down_ref[i] * live_ref[i]
            gshift_ref[i] = gshift_ref[i] * (live_ref[i] * flag_ref[i])


def bring_down(dj, live, flag):
    images, count, ch = dj.shape
    one = whole((images, 1, ch))
    return pl.pallas_call(
        down_body,
        grid=(4,),
        in_specs=[pl.BlockSpec((images, count // 4, ch), lambda i: (0, i, 0)), one, one],
        out_specs=[whole((images, COUNT, ch)), one],
        out_shape=[spec((images, COUNT, ch), F32), spec((images, 1, ch), F32)],
        compiler_params=params(),
        cost_estimate=lasts(8.9),
        name="bring_down",
    )(dj, live, flag)


def attention_body(a1_ref, wq_ref, wk_ref, wv_ref, qkv_ref, o_ref, e_ref, r_ref):
    for i, ref in enumerate((wq_ref, wk_ref, wv_ref)):
        qkv_ref[:, WIDTH * i:WIDTH * (i + 1)] = mm(a1_ref[...], ref[...]).astype(BF16)
    for h in range(NH):
        q, k, v = (slice(WIDTH * i + HD * h, WIDTH * i + HD * (h + 1)) for i in range(3))
        s = mm_nt(qkv_ref[:, k], qkv_ref[:, q] * jnp.asarray(0.125, BF16))
        e = jnp.exp(s - jnp.max(s, 0, keepdims=True))
        r = 1.0 / jnp.sum(e, 0, keepdims=True)
        low = e.astype(BF16)
        e_ref[h] = low
        o_ref[:, HD * h:HD * (h + 1)] = (mm_tn(qkv_ref[:, v], low) * r).T.astype(BF16)
        r_ref[0, h:h + 1, :] = r


def group_specs():
    def cols(n):
        return pl.BlockSpec((COUNT, n), lambda i: (i, 0))

    return cols, pl.BlockSpec((NH, COUNT, COUNT), lambda i: (i, 0, 0)), pl.BlockSpec((1, NH, COUNT), lambda i: (i, 0, 0))


def group_columns(group):
    return [pl.BlockSpec((D, WIDTH), lambda i, p=p: (0, GROUPS * p + group), pipeline_mode=pl.Buffered(1)) for p in range(3)]


def attention(a1, w, group):
    rows = a1.shape[0]
    images = rows // COUNT
    cols, probs, sums = group_specs()
    return pl.pallas_call(
        attention_body,
        grid=(images,),
        in_specs=[cols(D)] + group_columns(group),
        out_specs=[cols(3 * WIDTH), cols(WIDTH), probs, sums],
        out_shape=[spec((rows, 3 * WIDTH)), spec((rows, WIDTH)), spec((images * NH, COUNT, COUNT)),
                   spec((images, NH, COUNT), F32)],
        compiler_params=params(),
        cost_estimate=lasts(11),
        name="attention",
    )(a1, w, w, w)


def attention_back(da, me, group, qkv, o, e, r, a1, w_out, extra, split):
    rows = da.shape[0]
    images = rows // COUNT
    cols, probs, sums = group_specs()
    shape = (D, 3 * WIDTH)
    sink = Sink([shape], PLAIN) if extra is None else Sink([shape, (D, D)], split)
    n_out = len(sink.outs)
    extra = list(extra) if isinstance(extra, (list, tuple)) else [] if extra is None else [extra]

    def body(da_ref, me_ref, qkv_ref, o_ref, e_ref, r_ref, a1_ref, wout_ref, *refs):
        more, refs = refs[:len(extra)], refs[len(extra):]
        grads, dqkv, total, held = refs[:n_out], refs[n_out], refs[n_out + 1], refs[n_out + 2:]
        if len(extra) > 1:
            total_out, held = held[0], held[1:]
        step = pl.program_id(0)
        ones = jnp.ones((8, HD), BF16)
        do_all = mm_nt(da_ref[...], wout_ref[...]).astype(BF16)
        for h in range(NH):
            q, k, v = (slice(WIDTH * i + HD * h, WIDTH * i + HD * (h + 1)) for i in range(3))
            do = do_all[:, HD * h:HD * (h + 1)]
            delta = mm_nt(ones, (do.astype(F32) * o_ref[:, HD * h:HD * (h + 1)].astype(F32)).astype(BF16))[0:1]
            prob = e_ref[h].astype(F32) * r_ref[0, h:h + 1, :]
            dp = mm_nt(qkv_ref[:, v], do)
            ds = (prob * (dp - delta)).astype(BF16)
            dqkv[:, v] = mm(prob.astype(BF16), do).astype(BF16)
            dqkv[:, k] = (mm(ds, qkv_ref[:, q]) * 0.125).astype(BF16)
            dqkv[:, q] = (mm_tn(ds, qkv_ref[:, k]) * 0.125).astype(BF16)
        g = mm_tn(a1_ref[...], dqkv[...])
        g_out = [mm_tn(ref[...], da_ref[...]) for ref in more] if len(extra) > 1 else []

        @pl.when(step == 0)
        def _():
            total[...] = g
            for i, part in enumerate(g_out):
                total_out[WIDTH * i:WIDTH * (i + 1)] = part

        @pl.when(step > 0)
        def _():
            total[...] += g
            for i, part in enumerate(g_out):
                total_out[WIDTH * i:WIDTH * (i + 1)] += part

        @pl.when(step == images - 1)
        def _():
            sink.put(grads, held, 0, slice(0, D), total[...])
            if len(extra) > 1:
                sink.put(grads, held, 1, slice(0, D), total_out[...])
            elif extra:
                sink.put(grads, held, 1, slice(0, D), more[0][...])
            sink.deliver(me_ref, grads, held)

    more_specs = [cols(WIDTH)] * len(extra) if len(extra) > 1 else [whole(a.shape) for a in extra]
    out = pl.pallas_call(
        body,
        grid=(images,),
        in_specs=[cols(D), pl.BlockSpec(memory_space=pltpu.SMEM), cols(3 * WIDTH), cols(WIDTH), probs, sums, cols(D),
                  pl.BlockSpec((WIDTH, D), lambda i: (group, 0))] + more_specs,
        out_specs=sink.out_specs() + [cols(3 * WIDTH)],
        out_shape=sink.outs + [spec((rows, 3 * WIDTH))],
        scratch_shapes=[pltpu.VMEM(shape, F32)] + ([pltpu.VMEM((D, D), F32)] if len(extra) > 1 else []) + sink.scratch,
        compiler_params=params(),
        cost_estimate=lasts(18),
        name="attention_back",
    )(da, me, qkv, o, e, r, a1, w_out, *extra)
    return out[:n_out], out[n_out]


def input_back(dqkv, w, dx2, x, gains):
    rows = x.shape[0]
    block = rows // 4

    def body(*refs):
        (w_ref, dx2_ref, x_ref, gains_ref), out_ref = refs[GROUPS:-1], refs[-1]
        da1 = jnp.zeros((block, D), F32)
        for i, ref in enumerate(refs[:GROUPS]):
            for p in range(3):
                at = D * p + WIDTH * i
                da1 = da1 + mm_nt(ref[:, WIDTH * p:WIDTH * (p + 1)], w_ref[:, at:at + WIDTH])
        n1, rs1 = normalize(x_ref[...].astype(F32))
        out_ref[...] = (dx2_ref[...] + norm_transpose(da1 * gains_ref[0:1], n1, rs1)).astype(BF16)

    def cols(n):
        return pl.BlockSpec((block, n), lambda i: (i, 0))

    return pl.pallas_call(
        body,
        grid=(4,),
        in_specs=[cols(3 * WIDTH)] * GROUPS + [whole(w.shape), cols(D), cols(D), whole(gains.shape)],
        out_specs=cols(D),
        out_shape=spec((rows, D)),
        compiler_params=params(),
        cost_estimate=lasts(9),
        name="input_back",
    )(*dqkv, w, dx2, x, gains)


def mlp_up_body(x_ref, o0_ref, o1_ref, o2_ref, wout_ref, w1_ref, gains_ref, x2_ref, a2_ref, gg_ref, slope_ref):
    rows = x2_ref.shape[0]
    chunk = rows // 4

    @pl.when(pl.program_id(0) == 0)
    def _():
        for p in range(0, rows, chunk):
            at = slice(p, p + chunk)
            x2 = x_ref[at].astype(F32)
            for i, ref in enumerate((o0_ref, o1_ref, o2_ref)):
                x2 = x2 + mm(ref[at], wout_ref[WIDTH * i:WIDTH * (i + 1)])
            x2_ref[at] = x2
            a2_ref[at] = (normalize(x2)[0] * gains_ref[1:2]).astype(BF16)

    act, slope = gelu_pair(mm(a2_ref[...], w1_ref[...]))
    gg_ref[...], slope_ref[...] = act.astype(BF16), slope.astype(BF16)


def mlp_up(x, heads_out, w_out, w1, gains, block=512):
    rows, ff = x.shape[0], w1.shape[1]
    full, cols = whole((rows, D)), pl.BlockSpec((rows, block), lambda i: (0, i))
    return pl.pallas_call(
        mlp_up_body,
        grid=(ff // block,),
        in_specs=[full] + [whole((rows, WIDTH))] * 3 + [whole((D, D)), pl.BlockSpec((D, block), lambda i: (0, i)), whole((2, D))],
        out_specs=[full, full, cols, cols],
        out_shape=[spec((rows, D), F32), spec((rows, D)), spec((rows, ff)), spec((rows, ff))],
        compiler_params=params(),
        cost_estimate=lasts(18),
        name="mlp_up",
    )(x, *heads_out, w_out, w1, gains)


def mlp_down_body(gg_ref, w2_ref, x2_ref, count_ref, x3b_ref, out_ref):
    x3 = x2_ref[...] + mm(gg_ref[...], w2_ref[...])
    x3b_ref[...] = x3.astype(BF16)
    image = pl.program_id(0) * x3b_ref.shape[0] // COUNT
    out_ref[...] = (x3 * (image < count_ref[0]).astype(F32)).astype(BF16)


def mlp_down(gg, w2, x2, live_count):
    rows, ff = gg.shape
    block = rows // 4
    at = pl.BlockSpec((block, D), lambda i: (i, 0))
    return pl.pallas_call(
        mlp_down_body,
        grid=(4,),
        in_specs=[pl.BlockSpec((block, ff), lambda i: (i, 0)), whole(w2.shape), at, pl.BlockSpec(memory_space=pltpu.SMEM)],
        out_specs=[at, at],
        out_shape=[spec((rows, D))] * 2,
        compiler_params=params(),
        cost_estimate=lasts(11),
        name="mlp_down",
    )(gg, w2, x2, live_count)


def spread(value, out_ref, rows, sign):
    count, ch = value.shape
    at = lax.broadcasted_iota(jnp.int32, (count, 1), 0)
    col = at % GRID
    gap = jnp.zeros((GRID, ch), F32)
    for dx in (-1, 0, 1):
        step = sign * dx
        moved = value
        if step:
            moved = pltpu.roll(value, (-step) % count, 0)
            moved = jnp.where((col + step >= 0) & (col + step < GRID), moved, 0.0)
        for dy in (-1, 0, 1):
            block = 3 * (dy + 1) + dx + 1
            if sign * dy == 1:
                part = jnp.concatenate([moved[GRID:], gap], 0)
            elif sign * dy == -1:
                part = jnp.concatenate([gap, moved[:-GRID]], 0)
            else:
                part = moved
            out_ref[rows, block * ch:(block + 1) * ch] = part.astype(BF16)


def units_body(x_ref, wre_ref, w_ref, t1_ref, s1_ref, t2_ref, s2_ref, z_ref, cols):
    count = x_ref.shape[0]
    z = mm(x_ref[...], wre_ref[...])
    for unit in range(2):
        act, slope = gelu_pair(z)
        t1_ref[unit], s1_ref[unit] = act.astype(BF16), slope.astype(BF16)
        spread(act, cols, slice(0, count), 1)
        act, slope = gelu_pair(mm(cols[...], w_ref[2 * unit]))
        t2_ref[unit], s2_ref[unit] = act.astype(BF16), slope.astype(BF16)
        spread(act, cols, slice(0, count), 1)
        z = z + mm(cols[...], w_ref[2 * unit + 1])
    z_ref[...] = z.astype(BF16)


def units(x3b, w_re, w_conv):
    rows, ch = x3b.shape[0], w_re.shape[1]
    acts = pl.BlockSpec((2, COUNT, ch), lambda i: (0, i, 0))
    return pl.pallas_call(
        units_body,
        grid=(rows // COUNT,),
        in_specs=[pl.BlockSpec((COUNT, D), lambda i: (i, 0)), whole(w_re.shape), whole(w_conv.shape)],
        out_specs=[acts] * 4 + [pl.BlockSpec((COUNT, ch), lambda i: (i, 0))],
        out_shape=[spec((2, rows, ch))] * 4 + [spec((rows, ch))],
        scratch_shapes=[pltpu.VMEM((COUNT, 9 * ch), BF16)],
        compiler_params=params(),
        cost_estimate=lasts(18),
        name="units",
    )(x3b, w_re, w_conv)


def units_back_body(down_ref, scale_ref, gshift_ref, hot_ref, z_ref, x3b_ref, gt_ref, count_ref, whead_ref, w_ref, wre_ref, t1_ref, s1_ref, t2_ref, s2_ref,
                    gw_ref, ghead_ref, gre_ref, dx3_ref, dm_ref, table_ref, moved, turned, dz_ref):
    images, _, ch = down_ref.shape
    dq = jnp.concatenate([(down_ref[i] * scale_ref[i]).astype(BF16) for i in range(images)], 0)
    ghead_ref[...] = mm_tn(z_ref[...], dq).astype(BF16)
    dz_ref[...] = mm_nt(dq, whead_ref[...])
    table_ref[...] = jnp.zeros_like(table_ref)
    for i in range(images):
        head = mm(z_ref[COUNT * i:COUNT * (i + 1)], whead_ref[...])
        sums = (jnp.sum(head * down_ref[i], 0, keepdims=True), gshift_ref[i])
        for b in range(2 * ch // LANES):
            at, row = SMALL * b, sums[b // (ch // LANES)]
            cols = slice(LANES * (b % (ch // LANES)), LANES * (b % (ch // LANES) + 1))
            table_ref[at:at + SMALL] += hot_ref[i] * row[:, cols]

    def back(index, grad, act_ref, unit):
        for i in range(images):
            at = slice(COUNT * i, COUNT * (i + 1))
            spread(grad[at], moved, at, -1)
        g = mm_tn(act_ref[unit], moved[...])
        for b in range(9):
            at = slice(ch * b, ch * (b + 1))
            gw_ref[index, at, :] = g[:, at].astype(BF16)
            turned[:, at] = w_ref[index, at, :]
        return mm_nt(moved[...], turned[...])

    for unit in (1, 0):
        grad = back(2 * unit + 1, dz_ref[...], t2_ref, unit) * s2_ref[unit].astype(F32)
        grad = back(2 * unit, grad, t1_ref, unit) * s1_ref[unit].astype(F32)
        dz_ref[...] += grad
    dr = dz_ref[...].astype(BF16)
    gre_ref[...] = mm_tn(x3b_ref[...], dr).astype(BF16)
    dx3 = mm_nt(dr, wre_ref[...])
    for i in range(images):
        at = slice(COUNT * i, COUNT * (i + 1))
        part = gt_ref[at].astype(F32) * (i < count_ref[0]).astype(F32) + dx3[at]
        dx3_ref[at] = part
        dm_ref[at] = part.astype(BF16)


def units_back(down, scale, gshift, hot, z, x3b, gt, live_count, w_head, w_conv, w_re, t1, s1, t2, s2):
    rows, ch = z.shape
    ins = (down, scale, gshift, hot, z, x3b, gt, live_count, w_head, w_conv, w_re, t1, s1, t2, s2)
    outs = [spec(w_conv.shape), spec(w_head.shape), spec(w_re.shape), spec((rows, D), F32), spec((rows, D)),
            spec((2 * ch // LANES * SMALL, LANES), F32)]
    return pl.pallas_call(
        units_back_body,
        grid=(1,),
        in_specs=[pl.BlockSpec(memory_space=pltpu.SMEM) if a is live_count else whole(a.shape) for a in ins],
        out_specs=[whole(a.shape) for a in outs],
        out_shape=outs,
        scratch_shapes=[pltpu.VMEM((rows, 9 * ch), BF16), pltpu.VMEM((ch, 9 * ch), BF16), pltpu.VMEM((rows, ch), F32)],
        compiler_params=params(),
        cost_estimate=lasts(30),
        name="units_back",
    )(*ins)


def hidden_back(dm, me, gg, slope, w2, split, block=512):
    rows, ff = gg.shape
    sink = Sink([(ff, D)], split)
    n_out = len(sink.outs)

    def body(dm_ref, me_ref, gg_ref, slope_ref, w2_ref, *refs):
        grads, du_ref, held = refs[:n_out], refs[n_out], refs[n_out + 1:]
        step = pl.program_id(0)
        at = pl.ds(pl.multiple_of(step * block, block), block)
        sink.put(grads, held, 0, at, mm_tn(gg_ref[...], dm_ref[...]))
        du_ref[...] = (mm_nt(dm_ref[...], w2_ref[...]) * slope_ref[...].astype(F32)).astype(BF16)

        @pl.when(step == pl.num_programs(0) - 1)
        def _():
            sink.deliver(me_ref, grads, held)

    cols = pl.BlockSpec((rows, block), lambda i: (0, i))
    out = pl.pallas_call(
        body,
        grid=(ff // block,),
        in_specs=[whole((rows, D)), pl.BlockSpec(memory_space=pltpu.SMEM), cols, cols, pl.BlockSpec((block, D), lambda i: (i, 0))],
        out_specs=sink.out_specs() + [cols],
        out_shape=sink.outs + [spec((rows, ff))],
        scratch_shapes=sink.scratch,
        compiler_params=params(),
        cost_estimate=lasts(20),
        name="hidden_back",
    )(dm, me, gg, slope, w2)
    return out[:n_out], out[n_out]


def mlp_back(du, me, a2, w1, dx3, x2, gains, g_re, g_head, table, split, block=512):
    rows, ff = du.shape
    sink = Sink([(D, ff), g_re.shape, g_head.shape], split, True)
    n_out = len(sink.outs)
    half = ff // 2 // block

    def body(du_ref, me_ref, a2_ref, w1_ref, dx3_ref, x2_ref, gains_ref, gre_ref, ghead_ref, table_ref, *refs):
        step = pl.program_id(0)
        grads, (dx2_ref, da_ref, total), held = refs[:n_out], refs[n_out:n_out + 3], refs[n_out + 3:]
        g = mm_tn(a2_ref[...], du_ref[...]).astype(BF16)
        cols = pl.ds(pl.multiple_of(step % half * block, block), block)
        if split == PLAIN:
            grads[0][:, pl.ds(pl.multiple_of(step * block, block), block)] = g
        else:
            held[0][step // half, :, cols] = g
        da2 = mm_nt(du_ref[...], w1_ref[...])

        @pl.when(step == 0)
        def _():
            total[...] = da2

        @pl.when(step > 0)
        def _():
            total[...] += da2

        @pl.when(step == pl.num_programs(0) - 1)
        def _():
            sink.put(grads, held, 1, slice(0, g_re.shape[0]), gre_ref[...])
            sink.put(grads, held, 2, slice(0, g_head.shape[0]), ghead_ref[...])
            if split != PLAIN:
                held[-1][...] = table_ref[...].astype(BF16)
            sink.deliver(me_ref, grads, held)
            chunk = rows // 6
            for p in range(0, rows, chunk):
                at = slice(p, p + chunk)
                n2, rs2 = normalize(x2_ref[at])
                dx2 = dx3_ref[at] + norm_transpose(total[at] * gains_ref[1:2], n2, rs2)
                dx2_ref[at] = dx2
                da_ref[at] = dx2.astype(BF16)

    full = whole((rows, D))
    others = [spec((rows, D), F32), spec((rows, D))]
    out = pl.pallas_call(
        body,
        grid=(ff // block,),
        in_specs=[pl.BlockSpec((rows, block), lambda i: (0, i)), pl.BlockSpec(memory_space=pltpu.SMEM), full,
                  pl.BlockSpec((D, block), lambda i: (0, i)), full, full, whole((2, D)), whole(g_re.shape), whole(g_head.shape),
                  whole(table.shape)],
        out_specs=sink.out_specs() + [whole(o.shape) for o in others],
        out_shape=sink.outs + others,
        scratch_shapes=[pltpu.VMEM((rows, D), F32)] + sink.scratch,
        compiler_params=params(),
        cost_estimate=lasts(27),
        name="mlp_back",
    )(du, me, a2, w1, dx3, x2, gains, g_re, g_head, table)
    return out[:n_out], out[n_out:]


def join_body(z_ref, w_ref, scale_ref, shift_ref, live_ref, out_ref, head_ref):
    step, images, size = pl.program_id(0), out_ref.shape[0], out_ref.shape[1]

    @pl.when(step == 0)
    def _():
        for i in range(images):
            head = mm(z_ref[COUNT * i:COUNT * (i + 1)], w_ref[...])
            head_ref[i] = head.astype(BF16)

    table = bilinear((size, 1), (1, COUNT), step * size)
    for i in range(images):
        out_ref[i] = ((mm(table, head_ref[i]) * scale_ref[i] + shift_ref[i]) * live_ref[i]).astype(BF16)


def join(z, w_head, scale, shift, live):
    images, ch = scale.shape[0], w_head.shape[1]
    one = whole((images, 1, ch))
    return pl.pallas_call(
        join_body,
        grid=(4,),
        in_specs=[whole(z.shape), whole(w_head.shape), one, one, one],
        out_specs=pl.BlockSpec((images, COUNT, ch), lambda i: (0, i, 0)),
        out_shape=spec((images, 4 * COUNT, ch)),
        scratch_shapes=[pltpu.VMEM((images, COUNT, ch), BF16)],
        compiler_params=params(),
        cost_estimate=lasts(7),
        name="join",
    )(z, w_head, scale, shift, live)


def shards(tokens, live_count, dataset_id, shift_flag, norm_gains, w_qkv, w_attn_out, w_fc1, w_fc2, w_reassemble,
           conv_kernels, w_head, scale_table, shift_table, d_tokens_out, d_joined):
    slots, count = tokens.shape[:2]
    rows = slots * count
    neighbours = (lax.axis_size("rep"), lax.axis_size("wide")) == (4, 8)
    ch, ff = w_head.shape[1], w_fc1.shape[1]
    wide = lax.axis_size("wide")
    at_wide = lax.axis_index("wide")
    g, t = norm_gains.shape[1], scale_table.shape[1]
    me = bit_vector()
    line = Line()
    r = D // 16

    def gathered(part, axis):
        return lax.all_gather(part, "wide", axis=axis, tiled=True)

    def rows_of(size):
        return lambda shard, y: (shard * 2 + y) * size

    def cols_of(size):
        return lambda x: x * size

    def lanes(v):
        return jnp.broadcast_to(v[:, None, None], (slots, 1, ch))

    live = (jnp.arange(slots, dtype=jnp.int32) < live_count[0]).astype(F32)
    flags = shift_flag.astype(F32)
    x = tokens.reshape(rows, D)

    if neighbours:
        pieces = line.run(lambda v: prepare(me, v, w_attn_out, w_fc1, w_fc2, w_reassemble, w_head, norm_gains, scale_table,
                                            shift_table), w_qkv)
        zero = Gather(line, pieces[0], 5 * LANES, 1)
    n1 = line.run(norm, x)
    if neighbours:
        zero.over_first()
    down, g_shift_rows = line.run(bring_down, d_joined, lanes(live), lanes(flags))
    if neighbours:
        zero.over_second()
        f_qkv, small = line.run(lambda v: assemble(me, zero, [(D, 3 * D), (wide, SMALL, 3 * LANES)], [
            (0, (0, r), (0, 3 * D // 2), rows_of(r), cols_of(3 * D // 2)), (1, (r, SMALL), (0, 3 * LANES), None, None)]), zero.pieces[0])

        def table(lead, start, n):
            return small[:, :lead, start:start + n].transpose(1, 0, 2).reshape(lead, wide * n)

        gains, scales, shifts = table(2, 2 * LANES, g), table(DATASETS, 0, t), table(DATASETS, LANES, t)
    else:
        gains, scales, shifts = gathered(norm_gains, 1), gathered(scale_table, 1), gathered(shift_table, 1)
        f_qkv = gathered(w_qkv, 0)

    gains = gains.astype(F32)
    a1 = line.run(lambda n: (n * gains[0:1]).astype(BF16), n1)
    groups = []
    if neighbours:
        one = Gather(line, line.after(pieces[1]), 9 * LANES, 1)
    for i in range(GROUPS):
        groups.append(line.run(attention, a1, f_qkv, i))
        if i == 0:
            if neighbours:
                one.over_first()
                two = Gather(line, line.after(pieces[2]), ff // 32, 0)
            f_conv = gathered(line.after(conv_kernels), 1)
        if neighbours and i == 1:
            one.over_second()
            two.over_first()

    def weights_one():
        if not neighbours:
            return gathered(w_attn_out, 0), gathered(w_fc1, 0), gathered(w_reassemble, 0), gathered(w_head, 0)
        rh, at = ch // 16, D // 2 + ff // 2
        return line.run(lambda v: assemble(me, one, [(D, D), (D, ff), (D, ch), (ch, ch)], [
            (0, (0, r), (0, D // 2), rows_of(r), cols_of(D // 2)),
            (1, (0, r), (D // 2, ff // 2), rows_of(r), cols_of(ff // 2)),
            (2, (0, r), (at, ch // 2), rows_of(r), cols_of(ch // 2)),
            (3, (0, rh), (at + ch // 2, ch // 2), rows_of(rh), cols_of(ch // 2))]), one.pieces[0])

    def weights_two():
        if not neighbours:
            return gathered(w_fc2, 0)
        n = ff // 16
        return line.run(lambda v: assemble(me, two, [(ff, D)], [(0, (0, n), (0, D // 2), rows_of(n), cols_of(D // 2))])[0],
                        two.pieces[0])

    heads_out = [group[1] for group in groups]
    onehot = (dataset_id[:, None] == jnp.arange(DATASETS, dtype=jnp.int32)[None, :]).astype(F32)
    scale = jnp.sum(onehot[:, :, None] * scales.astype(F32)[None], 1)[:, None]
    shift = (flags[:, None] * jnp.sum(onehot[:, :, None] * shifts.astype(F32)[None], 1))[:, None]
    f_out, f_fc1, f_re, f_head = weights_one()
    if neighbours:
        two.over_second()
    x2, a2, gg, slope = line.run(lambda v: mlp_up(v, heads_out, f_out, f_fc1, gains), x)
    f_fc2 = weights_two()
    x3b, tokens_out = line.run(mlp_down, gg, f_fc2, x2, live_count)
    t1, s1, t2, s2, zb = line.run(units, x3b, f_re, f_conv)

    def packed(split):
        return split if neighbours else PLAIN

    def chunk(grads, split):
        return Chunk(line, grads[0], grads[1], split) if neighbours else grads

    def go(*jobs):
        if neighbours:
            together(line, *jobs)

    hot = jnp.pad(onehot, ((0, 0), (0, SMALL - DATASETS)))[:, :, None]
    g_conv, g_head, g_re, dx3, dm, small = line.run(
        lambda v: units_back(v, scale, g_shift_rows, hot, zb, x3b, d_tokens_out.reshape(rows, D), live_count, f_head, f_conv, f_re,
                             t1, s1, t2, s2), down)
    s_conv = lax.psum_scatter(g_conv, "wide", scatter_dimension=1, tiled=True)
    split_two = ff // 16
    grads, du = line.run(lambda v: hidden_back(v, me, gg, slope, f_fc2, packed(split_two)), dm)
    c_two = chunk(grads, split_two)
    split_one = 7 * r
    grads, (dx2, da) = line.run(
        lambda v: mlp_back(v, me, a2, f_fc1, dx3, x2, gains, g_re, g_head, small, packed(split_one)), du)
    go(c_two)
    c_one = chunk(grads, split_one)

    def attention_step(i, extra):
        qkv, o, e, rs = groups[i]
        return line.run(lambda v: attention_back(v, me, i, qkv, o, e, rs, a1, f_out, extra, packed(None)), da)

    grads, dqkv_0 = attention_step(0, heads_out)
    go(c_two, c_one)
    c_first = chunk(grads, None)
    (g_second,), dqkv_1 = attention_step(1, None)
    go(c_two, c_one, c_first)
    if neighbours:
        c_conv = Whole(s_conv)
    grads, dqkv_2 = attention_step(2, g_second)
    if neighbours:
        together(line, c_one, c_first, c_conv)
        early = Along(line, [c_two, c_one, c_first])
    c_last = chunk(grads, None)
    d_tokens = line.run(lambda v: input_back((dqkv_0, dqkv_1, v), f_qkv, dx2, x, gains), dqkv_2)
    go(c_last)
    joined = line.run(join, zb, f_head, scale, shift, lanes(live))

    if neighbours:
        together(line, c_last, early)
        late = Along(line, [c_last])
        s_conv = line.run_all(lambda p, q: p.astype(F32) + q.astype(F32), *c_conv.terms)
        rh, rows_two, half = ch // 16, ff // 16, D // 2
        blocks, n, quarter = half // LANES, ff // 2 // LANES, TABLE // 4

        def up_to(size):
            return lambda y: size * y

        def across(size):
            return lambda x, b: x * size + b * LANES

        def group_col(i):
            def col(x, b):
                at = blocks * x + b
                return at // 2 * D + WIDTH * i + at % 2 * LANES
            return col

        together(line, late)
        starts = [0, early.rows[0], early.rows[0] + early.rows[1]]
        s_fc2, s_fc1, s_re, s_head, small, s_out = line.run(lambda m: finish(m, [early], [[
            (0, rows_two, 0, blocks, up_to(rows_two), across(half)),
            (1, r, starts[1], n, up_to(r), across(ff // 2)),
            (2, r, starts[1] + r * n, 1, up_to(r), across(ch // 2)),
            (3, rh, starts[1] + r * (n + 1), 1, up_to(rh), across(ch // 2)),
            (4, quarter, starts[1] + r * (n + 1) + rh, 1, up_to(2 * quarter), lambda x, b: 0),
            (5, r, starts[2] + r * blocks, blocks, up_to(r), across(half))]],
            [w_fc2.shape, w_fc1.shape, w_reassemble.shape, w_head.shape, (TABLE, LANES), w_attn_out.shape]), me)
        (s_qkv,) = finish(me, [early, late], [
            [(0, r, starts[2], blocks, up_to(r), group_col(0))],
            [(0, r, 0, blocks, up_to(r), group_col(2)), (0, r, r * blocks, blocks, up_to(r), group_col(1))]], [w_qkv.shape])
        small = small.reshape(2, ch // LANES, SMALL, LANES).transpose(0, 2, 1, 3).reshape(2, SMALL, ch)
        small = lax.dynamic_slice(small, (0, 0, at_wide * t), (2, DATASETS, t))
        g_scale, g_shift = small[0], small[1]
    else:
        def share(part, axis):
            part = lax.psum_scatter(part.astype(BF16), "wide", scatter_dimension=axis, tiled=True)
            return lax.psum(part, "rep").astype(F32)

        s_conv = lax.psum(s_conv, "rep").astype(F32)
        small = small.reshape(2, ch // LANES, SMALL, LANES).transpose(0, 2, 1, 3).reshape(2, SMALL, ch)[:, :DATASETS]
        g_scale, g_shift = share(small[0], 1), share(small[1], 1)
        s_fc2, s_fc1, s_re, s_head = share(c_two[0], 0), share(c_one[0], 0), share(c_one[1], 0), share(c_one[2], 0)
        s_out = share(c_first[1], 0)
        by_group = (c_first[0], c_last[1], c_last[0])
        s_qkv = share(jnp.concatenate([c[:, WIDTH * p:WIDTH * (p + 1)] for p in range(3) for c in by_group], 1), 0)
    g_gains = jnp.stack([jnp.sum(w_qkv.astype(F32) * s_qkv, 1), jnp.sum(w_fc1.astype(F32) * s_fc1, 1)]) / norm_gains.astype(F32)
    return (tokens_out.reshape(tokens.shape), joined, d_tokens.reshape(tokens.shape), g_gains, s_qkv, s_out, s_fc1, s_fc2,
            s_re, s_conv, s_head, g_scale, g_shift)


def solution(mesh):
    images = P(BOTH, None, None)
    slots = P(BOTH)
    rows = P("wide", None)
    cols = P(None, "wide")
    kernels = P(None, "wide", None)
    return jax.shard_map(
        shards,
        mesh=mesh,
        in_specs=(images, slots, slots, slots, cols, rows, rows, rows, rows, rows, kernels, rows, cols, cols, images, images),
        out_specs=(images, images, images, cols, rows, rows, rows, rows, rows, kernels, rows, cols, cols),
        check_vma=False,
    )
```

```python
import math

import jax
import jax.numpy as jnp
from jax import lax
from jax.experimental import pallas as pl
from jax.experimental.pallas import tpu as pltpu
from jax.sharding import PartitionSpec as P

D = 768
HEADS = 12
HD = 64
GRID = 24
COUNT = GRID * GRID
DATASETS = 10
NH = 4
GROUPS = HEADS // NH
WIDTH = NH * HD
LANES = 128
F32 = jnp.float32
BF16 = jnp.bfloat16
BOTH = ("rep", "wide")
VMEM = 60 << 20


def mm(left, right):
    return jnp.dot(left, right, preferred_element_type=F32)


def mm_tn(left, right):
    return lax.dot_general(left, right, (((0,), (0,)), ((), ())), preferred_element_type=F32)


def mm_nt(left, right):
    return lax.dot_general(left, right, (((1,), (1,)), ((), ())), preferred_element_type=F32)


def spec(shape, dtype=BF16):
    return jax.ShapeDtypeStruct(shape, dtype)


def whole(shape):
    return pl.BlockSpec(shape, lambda *_: (0,) * len(shape), pipeline_mode=pl.Buffered(1))


def params():
    return pltpu.CompilerParams(vmem_limit_bytes=VMEM)


def cost(macs, size):
    return pl.CostEstimate(flops=2 * int(macs), bytes_accessed=int(size), transcendentals=0)


def lasts(microseconds):
    return pl.CostEstimate(flops=int(microseconds * 1.15e9), bytes_accessed=0, transcendentals=0)


FLIP = {"y": 16, "x": 8, "z1": 4, "z0": 2, "c": 1}
XY, YX = ("x", "y"), ("y", "x")


def swap(value, *names):
    flip = sum(FLIP[name] for name in names)
    return lax.ppermute(value, BOTH, [(i, i ^ flip) for i in range(32)])


def bits():
    rep, wide = lax.axis_index("rep"), lax.axis_index("wide")
    return {"y": rep // 2, "x": rep % 2, "z1": wide // 4, "z0": (wide // 2) % 2, "c": wide % 2}


def bit_vector():
    b = bits()
    return jnp.stack([b[k] for k in ("y", "x", "z1", "z0", "c")]).astype(jnp.int32)


def along_z(parts):
    size = lax.axis_size("wide") // 2
    groups = [[2 * z + core for z in range(size)] for core in range(2)]
    return lax.all_to_all(parts, "wide", 0, 0, tiled=True, axis_index_groups=groups)


class Line:
    def __init__(self):
        self.tokens = []

    def after(self, value):
        return lax.optimization_barrier((value, *self.tokens))[0] if self.tokens else value

    def run(self, call, first, *rest):
        out = call(self.after(first), *rest)
        self.tokens = jax.tree.leaves(out)[-1:]
        return out

    def touch(self, *values):
        out = lax.optimization_barrier((*values, *self.tokens))
        self.tokens = list(out[:len(values)])
        return self.tokens

    def run_all(self, call, *values):
        out = call(*(lax.optimization_barrier((*values, *self.tokens))[:len(values)]))
        self.tokens = jax.tree.leaves(out)
        return out


def locate(me, order, plane, z, core):
    place = {order[0]: plane[0], order[1]: plane[1]}
    shard = ((me[2] ^ z[0]) * 2 + (me[3] ^ z[1])) * 2 + (me[4] ^ core)
    return shard, me[0] ^ place["y"], me[1] ^ place["x"]


class Gather:
    def __init__(self, piece, at, axis, swaps=False):
        self.at, self.axis, self.stage = at, axis, 0
        if swaps:
            self.terms = [piece, swap(piece, "z0"), swap(piece, "z1"), swap(piece, "z1", "z0")]
        else:
            self.terms = [along_z(jnp.broadcast_to(piece[None], (4,) + piece.shape))]
        self.relative = swaps

    def add(self, *terms):
        if self.stage == 0:
            value = jnp.stack(terms) if self.relative else terms[0]
            return [lax.slice_in_dim(value, 0, self.at, axis=self.axis + 1),
                    lax.slice_in_dim(value, self.at, value.shape[self.axis + 1], axis=self.axis + 1)]
        return [jnp.concatenate(terms[:2]), jnp.concatenate(terms[2:])]

    def send(self, out):
        one, two = out
        if self.stage == 0:
            self.terms = [one, swap(one, "x"), two, swap(two, "y")]
        else:
            self.terms = [one, swap(one, "y"), two, swap(two, "x")]
        self.stage += 1

    def starting(self, first):
        self.pieces[0] = first
        return self

    def between_cores(self):
        one, one_y, two, two_x = self.terms
        self.pieces = [one, one_y, swap(one, "c"), swap(one_y, "c"), two, two_x, swap(two, "c"), swap(two_x, "c")]


PLANE = [[(s // 4, a % 2, s // 2 % 2, s % 2, a // 2) for s in range(8)] for a in range(4)]


def assemble(me, gathered, shapes, parts):
    at, axis = gathered.at, gathered.axis

    def halves(rows, cols):
        first, size = (rows, cols)[axis]
        out = []
        for low, high, shift in ((first, min(first + size, at), 0), (max(first, at), first + size, at)):
            span = (low - shift, high - low)
            out.append(None if high <= low else (span, cols, low - first, 0) if axis == 0 else (rows, span, 0, low - first))
        return out

    def body(me_ref, *refs):
        ins, outs, sem = refs[:8], refs[8:-1], refs[-1]
        started = []
        for half, order in enumerate((XY, YX)):
            for a, places in enumerate(PLANE):
                for s, (first, second, z1, z0, core) in enumerate(places):
                    z = (z1, z0) if gathered.relative else (me_ref[2] ^ z1, me_ref[3] ^ z0)
                    shard, y, x = locate(me_ref, order, (first, second), z, core)
                    for k, rows, cols, row, col in parts:
                        share = halves(rows, cols)[half]
                        if share is None or (row is None and (first or second)):
                            continue
                        (r0, r), (c0, n), down, across = share
                        source = ins[4 * half + a].at[s, pl.ds(r0, r), pl.ds(c0, n)]
                        if row is None:
                            place = outs[k].at[shard, pl.ds(down, r), pl.ds(across, n)]
                        else:
                            place = outs[k].at[pl.ds(pl.multiple_of(row(shard, y) + down, 16), r),
                                               pl.ds(pl.multiple_of(col(x) + across, LANES), n)]
                        copy = pltpu.make_async_copy(source, place, sem.at[len(started)])
                        copy.start()
                        started.append(copy)
        for copy in started:
            copy.wait()

    return pl.pallas_call(
        body,
        grid=(1,),
        in_specs=[pl.BlockSpec(memory_space=pltpu.SMEM)] + [pl.BlockSpec(memory_space=pl.ANY)] * 8,
        out_specs=[whole(s) for s in shapes],
        out_shape=[spec(s) for s in shapes],
        scratch_shapes=[pltpu.SemaphoreType.DMA((64 * len(parts),))],
        compiler_params=params(),
        cost_estimate=lasts(0),
        name="assemble",
    )(me, *gathered.pieces)


def together(line, *jobs):
    counts = [len(job.terms) for job in jobs]

    def call(*terms):
        out = []
        for job, count in zip(jobs, counts):
            out.append(job.add(*terms[:count]))
            terms = terms[count:]
        return out

    for job, out in zip(jobs, line.run_all(call, *[term for job in jobs for term in job.terms])):
        job.send(out)


class Chunk:
    def __init__(self, line, keep, send, split):
        self.split, self.stage = split, 0
        self.terms = [keep, swap(line.after(send), "c")]

    def add(self, *terms):
        if self.stage == 0:
            parts = [(slots, rows) for rows in (slice(0, self.split), slice(self.split, None)) for slots in (slice(0, 8), slice(8, 16))]
            return [terms[0][part] + terms[1][part] for part in parts]
        return [terms[i][part] + terms[i + 1][part] for i in (0, 2) for part in (slice(0, 4), slice(4, 8))]

    def send(self, out):
        one, two = ("x", "y") if self.stage == 0 else ("y", "x")
        self.terms = [out[0], swap(out[1], one), out[2], swap(out[3], two)]
        self.stage += 1


class Single(Chunk):
    def __init__(self, line, keep, send, order):
        super().__init__(line, keep, send, None)
        self.order = order

    def add(self, *terms):
        if self.stage == 2:
            return [terms[0] + terms[1]]
        half = terms[0].shape[0] // 2
        return [terms[0][part] + terms[1][part] for part in (slice(0, half), slice(half, None))]

    def send(self, out):
        self.terms = out if self.stage == 2 else [out[0], swap(out[1], self.order[self.stage])]
        self.stage += 1


class Along:
    def __init__(self, *chunks):
        self.stage, self.terms = 0, [term for chunk in chunks for term in chunk.terms]
        self.done = [len(chunk.terms) == 1 for chunk in chunks for _ in range(max(1, len(chunk.terms) // 2))]

    def add(self, *terms):
        if self.stage:
            return [sum(terms[0][i].astype(F32) for i in range(4)).astype(BF16)]
        terms = list(terms)
        sums = [terms.pop(0) if done else terms.pop(0) + terms.pop(0) for done in self.done]
        return [jnp.concatenate(sums, 1)]

    def send(self, out):
        if self.stage:
            self.total = out[0]
        else:
            self.terms = [along_z(out[0])]
        self.stage += 1


class Back:
    def __init__(self, line, *alongs):
        self.rows = [along.total.shape[0] for along in alongs]
        if len(alongs) > 1:
            (total,) = line.run_all(lambda *parts: [jnp.concatenate(parts)], *[along.total for along in alongs])
        else:
            total = alongs[0].total
        self.terms = [total, swap(total, "x"), swap(total, "y"), swap(total, "x", "y")]


class Whole:
    def __init__(self, value):
        self.terms = [value, swap(value, "y")]

    def add(self, *terms):
        return [terms[0] + terms[1]]

    def send(self, out):
        self.terms = [out[0], swap(out[0], "x")]


def finish(me, backs, places, shapes):
    ins = [t for back in backs for t in back.terms]

    def body(me_ref, *refs):
        outs = refs[len(ins):len(ins) + len(shapes)]
        held = refs[len(ins) + len(shapes):]
        for c, parts in enumerate(places):
            for q in range(4):
                held[c][q] = refs[4 * c + q][...]
            for y in range(2):
                for x in range(2):
                    at = 2 * (me_ref[0] ^ y) + (me_ref[1] ^ x)
                    for k, r, r0, blocks, row, col in parts:
                        for b in range(blocks):
                            at_row = row(y) + (r * x if shapes[k][1] == LANES else 0)
                            outs[k][at_row:at_row + r, col(x, b):col(x, b) + LANES] = (
                                held[c][at, r0 + b * r:r0 + (b + 1) * r, :].astype(F32))

    return pl.pallas_call(
        body,
        grid=(1,),
        in_specs=[pl.BlockSpec(memory_space=pltpu.SMEM)] + [whole(a.shape) for a in ins],
        out_specs=[whole(s) for s in shapes],
        out_shape=[spec(s, F32) for s in shapes],
        scratch_shapes=[pltpu.VMEM((4,) + back.terms[0].shape, BF16) for back in backs],
        compiler_params=params(),
        cost_estimate=lasts(3),
        name="finish",
    )(me, *ins)


PLAIN = "plain"
ALL_XY, ALL_YX = 1 << 30, 0


TABLE = 64


class Sink:
    def __init__(self, shapes, split, table=False):
        self.shapes, self.split, self.table = shapes, split, table
        rows = sum(k // 16 * (n // 2 // LANES) for k, n in shapes) + (TABLE // 4 if table else 0)
        if split == PLAIN:
            self.outs, self.scratch = [spec(s) for s in shapes], []
        else:
            self.outs = [spec((16, rows, LANES))] * 2
            self.scratch = [pltpu.VMEM((2, k, n // 2), BF16) for k, n in shapes]
            self.scratch += [pltpu.VMEM((TABLE, LANES), BF16)] if table else []

    def out_specs(self):
        return [whole(o.shape) for o in self.outs]

    def put(self, outs, held, k, rows, value):
        value = value.astype(BF16)
        half = self.shapes[k][1] // 2
        if self.split == PLAIN:
            outs[k][rows, :] = value
        else:
            held[k][0, rows, :] = value[:, :half]
            held[k][1, rows, :] = value[:, half:]

    def deliver(self, me_ref, outs, held):
        if self.split == PLAIN:
            return
        for core in range(2):
            for s in range(16):
                z = (me_ref[2] ^ (s // 2 % 2), me_ref[3] ^ (s % 2))
                places = [locate(me_ref, order, (s // 8, s // 4 % 2), z, core) for order in (XY, YX)]
                at = 0
                for k, (rows, cols) in enumerate(self.shapes):
                    r = rows // 16
                    for b in range(cols // 2 // LANES):
                        shard, y, x = places[0 if at < self.split else 1]
                        start = pl.multiple_of((shard * 2 + y) * r, 16)
                        outs[core][s, at:at + r, :] = held[k][x, pl.ds(start, r), b * LANES:(b + 1) * LANES]
                        at += r
                if self.table:
                    r = TABLE // 4
                    _, y, x = places[0 if at < self.split else 1]
                    outs[core][s, at:at + r, :] = held[-1][pl.ds(pl.multiple_of((2 * y + x) * r, 16), r), :]


def gelu_pair(values):
    cdf = 0.5 + 0.5 * lax.erf(values * 0.7071067811865476)
    pdf = 0.3989422804014327 * jnp.exp(-0.5 * values * values)
    return values * cdf, cdf + values * pdf


def gelu(values):
    return values * (0.5 + 0.5 * lax.erf(values * 0.7071067811865476))


def normalize(values):
    centred = values - jnp.mean(values, -1, keepdims=True)
    recip = lax.rsqrt(jnp.mean(centred * centred, -1, keepdims=True) + 1e-06)
    return centred * recip, recip


def norm_transpose(grad_normed, normed, recip):
    return recip * (
        grad_normed
        - jnp.mean(grad_normed, -1, keepdims=True)
        - normed * jnp.mean(grad_normed * normed, -1, keepdims=True)
    )


SMALL = 16


def prepare(me, w_qkv, w_out, w_fc1, w_fc2, w_re, w_head, gains, scales, shifts):
    ff, ch = w_fc1.shape[1], w_re.shape[1]
    half = w_qkv.shape[0] // 2
    rows_two, rows_head = w_fc2.shape[0] // 2, w_head.shape[0] // 2
    n = w_qkv.shape[1] // 2

    def body(me_ref, qkv_ref, out_ref, fc1_ref, fc2_ref, re_ref, head_ref, gains_ref, scales_ref, shifts_ref,
             zero_ref, one_ref, two_ref):
        zero_ref[half:half + SMALL, :] = jnp.zeros((SMALL, n), BF16)
        zero_ref[half:half + DATASETS, 0:scales.shape[1]] = scales_ref[...]
        zero_ref[half:half + DATASETS, LANES:LANES + shifts.shape[1]] = shifts_ref[...]
        zero_ref[half:half + 2, 2 * LANES:2 * LANES + gains.shape[1]] = gains_ref[...]
        rows = pl.ds(pl.multiple_of(me_ref[0] * half, 16), half)
        rows_of_two = pl.ds(pl.multiple_of(me_ref[0] * rows_two, 16), rows_two)
        rows_of_head = pl.ds(pl.multiple_of(me_ref[0] * rows_head, 16), rows_head)
        for x in range(2):
            @pl.when(me_ref[1] == x)
            def _():
                zero_ref[0:half, :] = qkv_ref[rows, n * x:n * (x + 1)]
                one_ref[:, :D // 2] = out_ref[rows, D // 2 * x:D // 2 * (x + 1)]
                at = D // 2 + ff // 2
                one_ref[:, D // 2:at] = fc1_ref[rows, ff // 2 * x:ff // 2 * (x + 1)]
                one_ref[:, at:at + ch // 2] = re_ref[rows, ch // 2 * x:ch // 2 * (x + 1)]
                one_ref[0:rows_head, at + ch // 2:] = head_ref[rows_of_head, ch // 2 * x:ch // 2 * (x + 1)]
                two_ref[...] = fc2_ref[rows_of_two, D // 2 * x:D // 2 * (x + 1)]
        one_ref[rows_head:, D // 2 + ff // 2 + ch // 2:] = jnp.zeros((half - rows_head, LANES), BF16)

    ins = (w_qkv, w_out, w_fc1, w_fc2, w_re, w_head, gains, scales, shifts)
    outs = [spec((half + SMALL, n)), spec((half, D // 2 + ff // 2 + ch // 2 + LANES)), spec((rows_two, D // 2))]
    return pl.pallas_call(
        body,
        grid=(1,),
        in_specs=[pl.BlockSpec(memory_space=pltpu.SMEM)] + [whole(a.shape) for a in ins],
        out_specs=[whole(o.shape) for o in outs],
        out_shape=outs,
        compiler_params=params(),
        cost_estimate=lasts(2.4),
        name="prepare",
    )(me, *ins)


def norm_body(x_ref, out_ref):
    out_ref[...] = normalize(x_ref[...].astype(F32))[0]


def norm(x):
    rows = x.shape[0]
    block = pl.BlockSpec((rows // 4, D), lambda i: (i, 0))
    return pl.pallas_call(
        norm_body,
        grid=(4,),
        in_specs=[block],
        out_specs=block,
        out_shape=spec((rows, D), F32),
        compiler_params=params(),
        cost_estimate=lasts(4.4),
        name="norm",
    )(x)


def bilinear(targets, sources, first):
    size = 2 * GRID
    step = (GRID - 1) / (size - 1)

    def hat(target, source):
        return jnp.maximum(1.0 - jnp.abs(target.astype(F32) * step - source.astype(F32)), 0.0)

    target = lax.broadcasted_iota(jnp.int32, targets, targets.index(max(targets))) + first
    source = lax.broadcasted_iota(jnp.int32, sources, sources.index(max(sources)))
    return (hat(target // size, source // GRID) * hat(target % size, source % GRID)).astype(BF16)


def down_body(dj_ref, live_ref, flag_ref, down_ref, gshift_ref):
    step, images, size = pl.program_id(0), dj_ref.shape[0], dj_ref.shape[1]
    table = bilinear((1, size), (COUNT, 1), step * size)
    for i in range(images):
        part = mm(table, dj_ref[i])
        sums = jnp.sum(dj_ref[i].astype(F32), 0, keepdims=True)

        @pl.when(step == 0)
        def _():
            down_ref[i] = part
            gshift_ref[i] = sums

        @pl.when(step > 0)
        def _():
            down_ref[i] += part
            gshift_ref[i] += sums

        @pl.when(step == pl.num_programs(0) - 1)
        def _():
            down_ref[i] = down_ref[i] * live_ref[i]
            gshift_ref[i] = gshift_ref[i] * (live_ref[i] * flag_ref[i])


def bring_down(dj, live, flag):
    images, count, ch = dj.shape
    one = whole((images, 1, ch))
    return pl.pallas_call(
        down_body,
        grid=(4,),
        in_specs=[pl.BlockSpec((images, count // 4, ch), lambda i: (0, i, 0)), one, one],
        out_specs=[whole((images, COUNT, ch)), one],
        out_shape=[spec((images, COUNT, ch), F32), spec((images, 1, ch), F32)],
        compiler_params=params(),
        cost_estimate=lasts(8.9),
        name="bring_down",
    )(dj, live, flag)


def attention_body(a1_ref, wq_ref, wk_ref, wv_ref, qkv_ref, o_ref, e_ref, r_ref):
    for i, ref in enumerate((wq_ref, wk_ref, wv_ref)):
        qkv_ref[:, WIDTH * i:WIDTH * (i + 1)] = mm(a1_ref[...], ref[...]).astype(BF16)
    for h in range(NH):
        q, k, v = (slice(WIDTH * i + HD * h, WIDTH * i + HD * (h + 1)) for i in range(3))
        s = mm_nt(qkv_ref[:, k], qkv_ref[:, q] * jnp.asarray(0.125, BF16))
        e = jnp.exp(s - jnp.max(s, 0, keepdims=True))
        r = 1.0 / jnp.sum(e, 0, keepdims=True)
        low = e.astype(BF16)
        e_ref[h] = low
        o_ref[:, HD * h:HD * (h + 1)] = (mm_tn(qkv_ref[:, v], low) * r).T.astype(BF16)
        r_ref[0, h:h + 1, :] = r


def group_specs():
    def cols(n):
        return pl.BlockSpec((COUNT, n), lambda i: (i, 0))

    return cols, pl.BlockSpec((NH, COUNT, COUNT), lambda i: (i, 0, 0)), pl.BlockSpec((1, NH, COUNT), lambda i: (i, 0, 0))


def group_columns(group):
    return [pl.BlockSpec((D, WIDTH), lambda i, p=p: (0, GROUPS * p + group), pipeline_mode=pl.Buffered(1)) for p in range(3)]


def attention(a1, w, group):
    rows = a1.shape[0]
    images = rows // COUNT
    cols, probs, sums = group_specs()
    return pl.pallas_call(
        attention_body,
        grid=(images,),
        in_specs=[cols(D)] + group_columns(group),
        out_specs=[cols(3 * WIDTH), cols(WIDTH), probs, sums],
        out_shape=[spec((rows, 3 * WIDTH)), spec((rows, WIDTH)), spec((images * NH, COUNT, COUNT)),
                   spec((images, NH, COUNT), F32)],
        compiler_params=params(),
        cost_estimate=lasts(11),
        name="attention",
    )(a1, w, w, w)


def attention_back(da, me, group, qkv, o, e, r, a1, w_out, extra, split):
    rows = da.shape[0]
    images = rows // COUNT
    cols, probs, sums = group_specs()
    shape = (D, 3 * WIDTH)
    sink = Sink([shape], PLAIN) if extra is None else Sink([shape, (D, D)], split)
    n_out = len(sink.outs)
    extra = list(extra) if isinstance(extra, (list, tuple)) else [] if extra is None else [extra]

    def body(da_ref, me_ref, qkv_ref, o_ref, e_ref, r_ref, a1_ref, wout_ref, *refs):
        more, refs = refs[:len(extra)], refs[len(extra):]
        grads, dqkv, total, held = refs[:n_out], refs[n_out], refs[n_out + 1], refs[n_out + 2:]
        if len(extra) > 1:
            total_out, held = held[0], held[1:]
        step = pl.program_id(0)
        ones = jnp.ones((8, HD), BF16)
        do_all = mm_nt(da_ref[...], wout_ref[...]).astype(BF16)
        for h in range(NH):
            q, k, v = (slice(WIDTH * i + HD * h, WIDTH * i + HD * (h + 1)) for i in range(3))
            do = do_all[:, HD * h:HD * (h + 1)]
            delta = mm_nt(ones, (do.astype(F32) * o_ref[:, HD * h:HD * (h + 1)].astype(F32)).astype(BF16))[0:1]
            prob = e_ref[h].astype(F32) * r_ref[0, h:h + 1, :]
            dp = mm_nt(qkv_ref[:, v], do)
            ds = (prob * (dp - delta)).astype(BF16)
            dqkv[:, v] = mm(prob.astype(BF16), do).astype(BF16)
            dqkv[:, k] = (mm(ds, qkv_ref[:, q]) * 0.125).astype(BF16)
            dqkv[:, q] = (mm_tn(ds, qkv_ref[:, k]) * 0.125).astype(BF16)
        g = mm_tn(a1_ref[...], dqkv[...])
        g_out = [mm_tn(ref[...], da_ref[...]) for ref in more] if len(extra) > 1 else []

        @pl.when(step == 0)
        def _():
            total[...] = g
            for i, part in enumerate(g_out):
                total_out[WIDTH * i:WIDTH * (i + 1)] = part

        @pl.when(step > 0)
        def _():
            total[...] += g
            for i, part in enumerate(g_out):
                total_out[WIDTH * i:WIDTH * (i + 1)] += part

        @pl.when(step == images - 1)
        def _():
            sink.put(grads, held, 0, slice(0, D), total[...])
            if len(extra) > 1:
                sink.put(grads, held, 1, slice(0, D), total_out[...])
            elif extra:
                sink.put(grads, held, 1, slice(0, D), more[0][...])
            sink.deliver(me_ref, grads, held)

    more_specs = [cols(WIDTH)] * len(extra) if len(extra) > 1 else [whole(a.shape) for a in extra]
    out = pl.pallas_call(
        body,
        grid=(images,),
        in_specs=[cols(D), pl.BlockSpec(memory_space=pltpu.SMEM), cols(3 * WIDTH), cols(WIDTH), probs, sums, cols(D),
                  pl.BlockSpec((WIDTH, D), lambda i: (group, 0))] + more_specs,
        out_specs=sink.out_specs() + [cols(3 * WIDTH)],
        out_shape=sink.outs + [spec((rows, 3 * WIDTH))],
        scratch_shapes=[pltpu.VMEM(shape, F32)] + ([pltpu.VMEM((D, D), F32)] if len(extra) > 1 else []) + sink.scratch,
        compiler_params=params(),
        cost_estimate=lasts(18),
        name="attention_back",
    )(da, me, qkv, o, e, r, a1, w_out, *extra)
    return out[:n_out], out[n_out]


def input_back(dqkv, w, dx2, x, gains):
    rows = x.shape[0]
    block = rows // 4

    def body(*refs):
        (w_ref, dx2_ref, x_ref, gains_ref), out_ref = refs[GROUPS:-1], refs[-1]
        da1 = jnp.zeros((block, D), F32)
        for i, ref in enumerate(refs[:GROUPS]):
            for p in range(3):
                at = D * p + WIDTH * i
                da1 = da1 + mm_nt(ref[:, WIDTH * p:WIDTH * (p + 1)], w_ref[:, at:at + WIDTH])
        n1, rs1 = normalize(x_ref[...].astype(F32))
        out_ref[...] = (dx2_ref[...].astype(F32) + norm_transpose(da1 * gains_ref[0:1], n1, rs1)).astype(BF16)

    def cols(n):
        return pl.BlockSpec((block, n), lambda i: (i, 0))

    return pl.pallas_call(
        body,
        grid=(4,),
        in_specs=[cols(3 * WIDTH)] * GROUPS + [whole(w.shape), cols(D), cols(D), whole(gains.shape)],
        out_specs=cols(D),
        out_shape=spec((rows, D)),
        compiler_params=params(),
        cost_estimate=lasts(9),
        name="input_back",
    )(*dqkv, w, dx2, x, gains)


def mlp_up_body(x_ref, o0_ref, o1_ref, o2_ref, wout_ref, w1_ref, gains_ref, x2_ref, a2_ref, u_ref):
    rows = x2_ref.shape[0]
    chunk = rows // 4

    @pl.when(pl.program_id(0) == 0)
    def _():
        for p in range(0, rows, chunk):
            at = slice(p, p + chunk)
            x2 = x_ref[at].astype(F32)
            for i, ref in enumerate((o0_ref, o1_ref, o2_ref)):
                x2 = x2 + mm(ref[at], wout_ref[WIDTH * i:WIDTH * (i + 1)])
            x2_ref[at] = x2.astype(BF16)
            a2_ref[at] = (normalize(x2)[0] * gains_ref[1:2]).astype(BF16)

    u_ref[...] = mm(a2_ref[...], w1_ref[...]).astype(BF16)


def mlp_up(x, heads_out, w_out, w1, gains, block=1024):
    rows, ff = x.shape[0], w1.shape[1]
    full, cols = whole((rows, D)), pl.BlockSpec((rows, block), lambda i: (0, i))
    return pl.pallas_call(
        mlp_up_body,
        grid=(ff // block,),
        in_specs=[full] + [whole((rows, WIDTH))] * 3 + [whole((D, D)), pl.BlockSpec((D, block), lambda i: (0, i)), whole((2, D))],
        out_specs=[full, full, cols],
        out_shape=[spec((rows, D)), spec((rows, D)), spec((rows, ff))],
        compiler_params=params(),
        cost_estimate=lasts(18),
        name="mlp_up",
    )(x, *heads_out, w_out, w1, gains)


def mlp_down_body(u_ref, w2_ref, x2_ref, count_ref, x3b_ref, out_ref):
    x3 = x2_ref[...].astype(F32)
    size = u_ref.shape[1] // 6
    for k in range(6):
        at = slice(size * k, size * (k + 1))
        act = gelu(u_ref[:, at].astype(F32)).astype(BF16)
        x3 = x3 + mm(act, w2_ref[at, :])
    x3b_ref[...] = x3.astype(BF16)
    image = pl.program_id(0) * x3b_ref.shape[0] // COUNT
    out_ref[...] = (x3 * (image < count_ref[0]).astype(F32)).astype(BF16)


def mlp_down(gg, w2, x2, live_count):
    rows, ff = gg.shape
    block = rows // 4
    at = pl.BlockSpec((block, D), lambda i: (i, 0))
    return pl.pallas_call(
        mlp_down_body,
        grid=(4,),
        in_specs=[pl.BlockSpec((block, ff), lambda i: (i, 0)), whole(w2.shape), at, pl.BlockSpec(memory_space=pltpu.SMEM)],
        out_specs=[at, at],
        out_shape=[spec((rows, D))] * 2,
        compiler_params=params(),
        cost_estimate=lasts(11),
        name="mlp_down",
    )(gg, w2, x2, live_count)


def spread(value, out_ref, rows, sign):
    count, ch = value.shape
    at = lax.broadcasted_iota(jnp.int32, (count, 1), 0)
    col = at % GRID
    gap = jnp.zeros((GRID, ch), F32)
    for dx in (-1, 0, 1):
        step = sign * dx
        moved = value
        if step:
            moved = pltpu.roll(value, (-step) % count, 0)
            moved = jnp.where((col + step >= 0) & (col + step < GRID), moved, 0.0)
        for dy in (-1, 0, 1):
            block = 3 * (dy + 1) + dx + 1
            if sign * dy == 1:
                part = jnp.concatenate([moved[GRID:], gap], 0)
            elif sign * dy == -1:
                part = jnp.concatenate([gap, moved[:-GRID]], 0)
            else:
                part = moved
            out_ref[rows, block * ch:(block + 1) * ch] = part.astype(BF16)


def units_body(x_ref, wre_ref, w_ref, t1_ref, s1_ref, t2_ref, s2_ref, zb_ref, cols, z_ref):
    unit, count = pl.program_id(1), x_ref.shape[0]

    @pl.when(unit == 0)
    def _():
        z_ref[...] = mm(x_ref[...], wre_ref[...])

    act, slope = gelu_pair(z_ref[...])
    t1_ref[0], s1_ref[0] = act.astype(BF16), slope.astype(BF16)
    spread(act, cols, slice(0, count), 1)
    act, slope = gelu_pair(mm(cols[...], w_ref[0]))
    t2_ref[0], s2_ref[0] = act.astype(BF16), slope.astype(BF16)
    spread(act, cols, slice(0, count), 1)
    z_ref[...] += mm(cols[...], w_ref[1])

    @pl.when(unit == 1)
    def _():
        zb_ref[...] = z_ref[...].astype(BF16)


def units(x3b, w_re, w_conv):
    rows, ch = x3b.shape[0], w_re.shape[1]
    acts = pl.BlockSpec((1, COUNT, ch), lambda i, j: (j, i, 0))
    return pl.pallas_call(
        units_body,
        grid=(rows // COUNT, 2),
        in_specs=[pl.BlockSpec((COUNT, D), lambda i, j: (i, 0)), whole(w_re.shape),
                  pl.BlockSpec((2,) + w_conv.shape[1:], lambda i, j: (j, 0, 0))],
        out_specs=[acts] * 4 + [pl.BlockSpec((COUNT, ch), lambda i, j: (i, 0))],
        out_shape=[spec((2, rows, ch))] * 4 + [spec((rows, ch))],
        scratch_shapes=[pltpu.VMEM((COUNT, 9 * ch), BF16), pltpu.VMEM((COUNT, ch), F32)],
        compiler_params=params(),
        cost_estimate=lasts(18),
        name="units",
    )(x3b, w_re, w_conv)


def units_back_body(down_ref, scale_ref, gshift_ref, hot_ref, z_ref, x3b_ref, gt_ref, count_ref, whead_ref, wre_ref,
                    w_ref, t1_ref, s1_ref, t2_ref, s2_ref,
                    gw_ref, ghead_ref, gre_ref, dm_ref, table_ref, moved, turned, dz_ref):
    images, _, ch = down_ref.shape

    @pl.when(pl.program_id(0) == 0)
    def _():
        dq = jnp.concatenate([(down_ref[i] * scale_ref[i]).astype(BF16) for i in range(images)], 0)
        ghead_ref[...] = mm_tn(z_ref[...], dq).astype(BF16)
        dz_ref[...] = mm_nt(dq, whead_ref[...])
        table_ref[...] = jnp.zeros_like(table_ref)
        for i in range(images):
            head = mm(z_ref[COUNT * i:COUNT * (i + 1)], whead_ref[...])
            sums = (jnp.sum(head * down_ref[i], 0, keepdims=True), gshift_ref[i])
            for b in range(2 * ch // LANES):
                at, row = SMALL * b, sums[b // (ch // LANES)]
                cols = slice(LANES * (b % (ch // LANES)), LANES * (b % (ch // LANES) + 1))
                table_ref[at:at + SMALL] += hot_ref[i] * row[:, cols]

    def back(index, grad, act_ref):
        for i in range(images):
            at = slice(COUNT * i, COUNT * (i + 1))
            spread(grad[at], moved, at, -1)
        g = mm_tn(act_ref[0], moved[...])
        for b in range(9):
            at = slice(ch * b, ch * (b + 1))
            gw_ref[index, at, :] = g[:, at].astype(BF16)
            turned[:, at] = w_ref[index, at, :]
        return mm_nt(moved[...], turned[...])

    grad = back(1, dz_ref[...], t2_ref) * s2_ref[0].astype(F32)
    grad = back(0, grad, t1_ref) * s1_ref[0].astype(F32)
    dz_ref[...] += grad

    @pl.when(pl.program_id(0) == 1)
    def _():
        dr = dz_ref[...].astype(BF16)
        gre_ref[...] = mm_tn(x3b_ref[...], dr).astype(BF16)
        dx3 = mm_nt(dr, wre_ref[...])
        for i in range(images):
            at = slice(COUNT * i, COUNT * (i + 1))
            part = gt_ref[at].astype(F32) * (i < count_ref[0]).astype(F32) + dx3[at]
            dm_ref[at] = part.astype(BF16)


def units_back(down, scale, gshift, hot, z, x3b, gt, live_count, w_head, w_conv, w_re, t1, s1, t2, s2):
    rows, ch = z.shape
    ins = (down, scale, gshift, hot, z, x3b, gt, live_count, w_head, w_re)
    outs = [spec(w_conv.shape), spec(w_head.shape), spec(w_re.shape), spec((rows, D)),
            spec((2 * ch // LANES * SMALL, LANES), F32)]
    kernels = pl.BlockSpec((2,) + w_conv.shape[1:], lambda i: (1 - i, 0, 0))
    act = pl.BlockSpec((1, rows, ch), lambda i: (1 - i, 0, 0))
    return pl.pallas_call(
        units_back_body,
        grid=(2,),
        in_specs=[pl.BlockSpec(memory_space=pltpu.SMEM) if a is live_count else whole(a.shape) for a in ins] + [kernels] + [act] * 4,
        out_specs=[kernels] + [whole(a.shape) for a in outs[1:]],
        out_shape=outs,
        scratch_shapes=[pltpu.VMEM((rows, 9 * ch), BF16), pltpu.VMEM((ch, 9 * ch), BF16), pltpu.VMEM((rows, ch), F32)],
        compiler_params=params(),
        cost_estimate=lasts(30),
        name="units_back",
    )(*ins, w_conv, t1, s1, t2, s2)


def hidden_back(dm, me, u, w2, split, block=512):
    rows, ff = u.shape
    sink = Sink([(ff, D)], split)
    n_out = len(sink.outs)

    def body(dm_ref, me_ref, u_ref, w2_ref, *refs):
        grads, du_ref, held = refs[:n_out], refs[n_out], refs[n_out + 1:]
        step = pl.program_id(0)
        at = pl.ds(pl.multiple_of(step * block, block), block)
        act, slope = gelu_pair(u_ref[...].astype(F32))
        sink.put(grads, held, 0, at, mm_tn(act.astype(BF16), dm_ref[...]))
        du_ref[...] = (mm_nt(dm_ref[...], w2_ref[...]) * slope).astype(BF16)

        @pl.when(step == pl.num_programs(0) - 1)
        def _():
            sink.deliver(me_ref, grads, held)

    cols = pl.BlockSpec((rows, block), lambda i: (0, i))
    out = pl.pallas_call(
        body,
        grid=(ff // block,),
        in_specs=[whole((rows, D)), pl.BlockSpec(memory_space=pltpu.SMEM), cols, pl.BlockSpec((block, D), lambda i: (i, 0))],
        out_specs=sink.out_specs() + [cols],
        out_shape=sink.outs + [spec((rows, ff))],
        scratch_shapes=sink.scratch,
        compiler_params=params(),
        cost_estimate=lasts(20),
        name="hidden_back",
    )(dm, me, u, w2)
    return out[:n_out], out[n_out]


def first_weight_back(du, me, a2, g_re, g_head, table, split, block=512):
    rows, ff = du.shape
    sink = Sink([(D, ff), g_re.shape, g_head.shape], split, True)
    n_out = len(sink.outs)
    half = ff // 2 // block

    def body(du_ref, me_ref, a2_ref, gre_ref, ghead_ref, table_ref, *refs):
        step = pl.program_id(0)
        grads, held = refs[:n_out], refs[n_out:]
        g = mm_tn(a2_ref[...], du_ref[...]).astype(BF16)
        cols = pl.ds(pl.multiple_of(step % half * block, block), block)
        if split == PLAIN:
            grads[0][:, pl.ds(pl.multiple_of(step * block, block), block)] = g
        else:
            held[0][step // half, :, cols] = g

        @pl.when(step == pl.num_programs(0) - 1)
        def _():
            sink.put(grads, held, 1, slice(0, g_re.shape[0]), gre_ref[...])
            sink.put(grads, held, 2, slice(0, g_head.shape[0]), ghead_ref[...])
            if split != PLAIN:
                held[-1][...] = table_ref[...].astype(BF16)
            sink.deliver(me_ref, grads, held)

    return pl.pallas_call(
        body,
        grid=(ff // block,),
        in_specs=[pl.BlockSpec((rows, block), lambda i: (0, i)), pl.BlockSpec(memory_space=pltpu.SMEM), whole((rows, D)),
                  whole(g_re.shape), whole(g_head.shape), whole(table.shape)],
        out_specs=sink.out_specs(),
        out_shape=sink.outs,
        scratch_shapes=sink.scratch,
        compiler_params=params(),
        cost_estimate=lasts(13),
        name="first_weight_back",
    )(du, me, a2, g_re, g_head, table)


def mlp_back_body(du_ref, w1_ref, dm_ref, x2_ref, gains_ref, da_ref):
    n2, rs2 = normalize(x2_ref[...].astype(F32))
    da2 = mm_nt(du_ref[...], w1_ref[...])
    da_ref[...] = (dm_ref[...].astype(F32) + norm_transpose(da2 * gains_ref[1:2], n2, rs2)).astype(BF16)


def mlp_back(du, w1, dm, x2, gains):
    rows, ff = du.shape
    block = rows // 4

    def cols(n):
        return pl.BlockSpec((block, n), lambda i: (i, 0))

    return pl.pallas_call(
        mlp_back_body,
        grid=(4,),
        in_specs=[cols(ff), whole(w1.shape), cols(D), cols(D), whole((2, D))],
        out_specs=cols(D),
        out_shape=spec((rows, D)),
        compiler_params=params(),
        cost_estimate=lasts(13),
        name="mlp_back",
    )(du, w1, dm, x2, gains)


def join_body(z_ref, w_ref, scale_ref, shift_ref, live_ref, out_ref, head_ref):
    step, images, size = pl.program_id(0), out_ref.shape[0], out_ref.shape[1]

    @pl.when(step == 0)
    def _():
        for i in range(images):
            head = mm(z_ref[COUNT * i:COUNT * (i + 1)], w_ref[...])
            head_ref[i] = head.astype(BF16)

    table = bilinear((size, 1), (1, COUNT), step * size)
    for i in range(images):
        out_ref[i] = ((mm(table, head_ref[i]) * scale_ref[i] + shift_ref[i]) * live_ref[i]).astype(BF16)


def join(z, w_head, scale, shift, live):
    images, ch = scale.shape[0], w_head.shape[1]
    one = whole((images, 1, ch))
    return pl.pallas_call(
        join_body,
        grid=(4,),
        in_specs=[whole(z.shape), whole(w_head.shape), one, one, one],
        out_specs=pl.BlockSpec((images, COUNT, ch), lambda i: (0, i, 0)),
        out_shape=spec((images, 4 * COUNT, ch)),
        scratch_shapes=[pltpu.VMEM((images, COUNT, ch), BF16)],
        compiler_params=params(),
        cost_estimate=lasts(7),
        name="join",
    )(z, w_head, scale, shift, live)


def shards(tokens, live_count, dataset_id, shift_flag, norm_gains, w_qkv, w_attn_out, w_fc1, w_fc2, w_reassemble,
           conv_kernels, w_head, scale_table, shift_table, d_tokens_out, d_joined):
    slots, count = tokens.shape[:2]
    rows = slots * count
    neighbours = (lax.axis_size("rep"), lax.axis_size("wide")) == (4, 8)
    ch, ff = w_head.shape[1], w_fc1.shape[1]
    wide = lax.axis_size("wide")
    at_wide = lax.axis_index("wide")
    g, t = norm_gains.shape[1], scale_table.shape[1]
    me = bit_vector()
    line = Line()
    r = D // 16

    def gathered(part, axis):
        return lax.all_gather(part, "wide", axis=axis, tiled=True)

    def rows_of(size):
        return lambda shard, y: (shard * 2 + y) * size

    def cols_of(size):
        return lambda x: x * size

    def lanes(v):
        return jnp.broadcast_to(v[:, None, None], (slots, 1, ch))

    live = (jnp.arange(slots, dtype=jnp.int32) < live_count[0]).astype(F32)
    flags = shift_flag.astype(F32)
    x = tokens.reshape(rows, D)

    if neighbours:
        pieces = line.run(lambda v: prepare(me, v, w_attn_out, w_fc1, w_fc2, w_reassemble, w_head, norm_gains, scale_table,
                                            shift_table), w_qkv)
        zero = Gather(pieces[0], 5 * LANES, 1, True)
    n1 = line.run(norm, x)
    if neighbours:
        together(line, zero)
        together(line, zero)
        zero.between_cores()
        one = Gather(line.after(pieces[1]), 9 * LANES, 1)
    down, g_shift_rows = line.run(bring_down, d_joined, lanes(live), lanes(flags))
    if neighbours:
        f_qkv, small = line.run(lambda v: assemble(me, zero.starting(v), [(D, 3 * D), (wide, SMALL, 3 * LANES)], [
            (0, (0, r), (0, 3 * D // 2), rows_of(r), cols_of(3 * D // 2)), (1, (r, SMALL), (0, 3 * LANES), None, None)]), zero.pieces[0])
        together(line, one)

        def table(lead, start, n):
            return small[:, :lead, start:start + n].transpose(1, 0, 2).reshape(lead, wide * n)

        gains, scales, shifts = table(2, 2 * LANES, g), table(DATASETS, 0, t), table(DATASETS, LANES, t)
    else:
        gains, scales, shifts = gathered(norm_gains, 1), gathered(scale_table, 1), gathered(shift_table, 1)
        f_qkv = gathered(w_qkv, 0)

    gains = gains.astype(F32)
    a1 = line.run(lambda n: (n * gains[0:1]).astype(BF16), n1)
    groups = []
    for i in range(GROUPS):
        groups.append(line.run(attention, a1, f_qkv, i))
        if neighbours and i == 0:
            together(line, one)
            two = Gather(line.after(pieces[2]), ff // 32, 0)
        if neighbours and i == 1:
            one.terms = line.touch(*one.terms)
            one.between_cores()
            together(line, two)
        if neighbours and i == 2:
            together(line, two)
        if i == 1:
            f_conv = gathered(line.after(conv_kernels), 1)

    def weights_one():
        if not neighbours:
            return gathered(w_attn_out, 0), gathered(w_fc1, 0), gathered(w_reassemble, 0), gathered(w_head, 0)
        rh, at = ch // 16, D // 2 + ff // 2
        return line.run(lambda v: assemble(me, one.starting(v), [(D, D), (D, ff), (D, ch), (ch, ch)], [
            (0, (0, r), (0, D // 2), rows_of(r), cols_of(D // 2)),
            (1, (0, r), (D // 2, ff // 2), rows_of(r), cols_of(ff // 2)),
            (2, (0, r), (at, ch // 2), rows_of(r), cols_of(ch // 2)),
            (3, (0, rh), (at + ch // 2, ch // 2), rows_of(rh), cols_of(ch // 2))]), one.pieces[0])

    def weights_two():
        if not neighbours:
            return gathered(w_fc2, 0)
        n = ff // 16
        return line.run(lambda v: assemble(me, two.starting(v), [(ff, D)], [(0, (0, n), (0, D // 2), rows_of(n), cols_of(D // 2))])[0],
                        two.pieces[0])

    heads_out = [group[1] for group in groups]
    onehot = (dataset_id[:, None] == jnp.arange(DATASETS, dtype=jnp.int32)[None, :]).astype(F32)
    scale = jnp.sum(onehot[:, :, None] * scales.astype(F32)[None], 1)[:, None]
    shift = (flags[:, None] * jnp.sum(onehot[:, :, None] * shifts.astype(F32)[None], 1))[:, None]
    f_out, f_fc1, f_re, f_head = weights_one()
    x2, a2, u = line.run(lambda v: mlp_up(v, heads_out, f_out, f_fc1, gains), x)
    if neighbours:
        two.terms = line.touch(*two.terms)
        two.between_cores()
    f_fc2 = weights_two()
    x3b, tokens_out = line.run(mlp_down, u, f_fc2, x2, live_count)
    t1, s1, t2, s2, zb = line.run(units, x3b, f_re, f_conv)

    def packed(split):
        return split if neighbours else PLAIN

    def chunk(grads, split):
        return Chunk(line, grads[0], grads[1], split) if neighbours else grads

    def go(*jobs):
        if neighbours:
            together(line, *jobs)

    hot = jnp.pad(onehot, ((0, 0), (0, SMALL - DATASETS)))[:, :, None]
    g_conv, g_head, g_re, dm, small = line.run(
        lambda v: units_back(v, scale, g_shift_rows, hot, zb, x3b, d_tokens_out.reshape(rows, D), live_count, f_head, f_conv, f_re,
                             t1, s1, t2, s2), down)
    s_conv = lax.psum_scatter(g_conv, "wide", scatter_dimension=1, tiled=True)
    split_two, split_one = ff // 16, 7 * r
    grads, du = line.run(lambda v: hidden_back(v, me, u, f_fc2, packed(split_two)), dm)
    c_two = chunk(grads, split_two)
    grads = line.run(lambda v: first_weight_back(v, me, a2, g_re, g_head, small, packed(split_one)), du)
    go(c_two)
    c_one = chunk(grads, split_one)
    da = line.run(lambda v: mlp_back(v, f_fc1, dm, x2, gains), du)
    go(c_two, c_one)

    def attention_step(i, extra, split):
        qkv, o, e, rs = groups[i]
        return line.run(lambda v: attention_back(v, me, i, qkv, o, e, rs, a1, f_out, extra, packed(split)), da)

    grads, dqkv_0 = attention_step(0, heads_out, ALL_XY)
    if neighbours:
        z_two = Along(c_two)
        together(line, z_two, c_one)
        c_first = Single(line, grads[0], grads[1], XY)
    else:
        c_first = grads
    (g_second,), dqkv_1 = attention_step(1, None, PLAIN)
    split_last = 3 * r
    if neighbours:
        z_one = Along(c_one)
        together(line, z_two, z_one, c_first)
        c_conv = Whole(s_conv)
        b_two = Back(line, z_two)
    grads, dqkv_2 = attention_step(2, g_second, split_last)
    if neighbours:
        together(line, z_one, c_first, c_conv)
        b_one = Back(line, z_one)
        c_last = Chunk(line, grads[0], grads[1], split_last)
    else:
        c_last = grads
    joined = line.run(join, zb, f_head, scale, shift, lanes(live))
    if neighbours:
        together(line, c_last)
    d_tokens = line.run(lambda v: input_back((dqkv_0, dqkv_1, v), f_qkv, da, x, gains), dqkv_2)

    if neighbours:
        together(line, c_last, c_first)
        s_conv = line.run_all(lambda p, q: p.astype(F32) + q.astype(F32), *c_conv.terms)
        rh, rows_two, half = ch // 16, ff // 16, D // 2
        blocks, n, quarter = half // LANES, ff // 2 // LANES, TABLE // 4

        def up_to(size):
            return lambda y: size * y

        def across(size):
            return lambda x, b: x * size + b * LANES

        def group_col(i):
            def col(x, b):
                at = blocks * x + b
                return at // 2 * D + WIDTH * i + at % 2 * LANES
            return col

        (s_fc2,) = line.run(lambda m: finish(m, [b_two], [[(0, rows_two, 0, blocks, up_to(rows_two), across(half))]],
                                             [w_fc2.shape]), me)
        z_last = Along(c_first, c_last)
        together(line, z_last)
        s_fc1, s_re, s_head, small = line.run(lambda m: finish(m, [b_one], [[
            (0, r, 0, n, up_to(r), across(ff // 2)),
            (1, r, r * n, 1, up_to(r), across(ch // 2)),
            (2, rh, r * (n + 1), 1, up_to(rh), across(ch // 2)),
            (3, quarter, r * (n + 1) + rh, 1, up_to(2 * quarter), lambda x, b: 0)]],
            [w_fc1.shape, w_reassemble.shape, w_head.shape, (TABLE, LANES)]), me)
        together(line, z_last)
        late = Back(line, z_last)
        s_qkv, s_out = finish(me, [late], [
            [(0, r, 0, blocks, up_to(r), group_col(0)), (1, r, r * blocks, blocks, up_to(r), across(half)),
             (0, r, 2 * r * blocks, blocks, up_to(r), group_col(2)), (0, r, 3 * r * blocks, blocks, up_to(r), group_col(1))]],
            [w_qkv.shape, w_attn_out.shape])
        small = small.reshape(2, ch // LANES, SMALL, LANES).transpose(0, 2, 1, 3).reshape(2, SMALL, ch)
        small = lax.dynamic_slice(small, (0, 0, at_wide * t), (2, DATASETS, t))
        g_scale, g_shift = small[0], small[1]
    else:
        def share(part, axis):
            part = lax.psum_scatter(part.astype(BF16), "wide", scatter_dimension=axis, tiled=True)
            return lax.psum(part, "rep").astype(F32)

        s_conv = lax.psum(s_conv, "rep").astype(F32)
        small = small.reshape(2, ch // LANES, SMALL, LANES).transpose(0, 2, 1, 3).reshape(2, SMALL, ch)[:, :DATASETS]
        g_scale, g_shift = share(small[0], 1), share(small[1], 1)
        s_fc2, s_fc1, s_re, s_head = share(c_two[0], 0), share(c_one[0], 0), share(c_one[1], 0), share(c_one[2], 0)
        s_out = share(c_first[1], 0)
        by_group = (c_first[0], c_last[1], c_last[0])
        s_qkv = share(jnp.concatenate([c[:, WIDTH * p:WIDTH * (p + 1)] for p in range(3) for c in by_group], 1), 0)
    g_gains = jnp.stack([jnp.sum(w_qkv.astype(F32) * s_qkv, 1), jnp.sum(w_fc1.astype(F32) * s_fc1, 1)]) / norm_gains.astype(F32)
    return (tokens_out.reshape(tokens.shape), joined, d_tokens.reshape(tokens.shape), g_gains, s_qkv, s_out, s_fc1, s_fc2,
            s_re, s_conv, s_head, g_scale, g_shift)


def solution(mesh):
    images = P(BOTH, None, None)
    slots = P(BOTH)
    rows = P("wide", None)
    cols = P(None, "wide")
    kernels = P(None, "wide", None)
    return jax.shard_map(
        shards,
        mesh=mesh,
        in_specs=(images, slots, slots, slots, cols, rows, rows, rows, rows, rows, kernels, rows, cols, cols, images, images),
        out_specs=(images, images, images, cols, rows, rows, rows, rows, rows, kernels, rows, cols, cols),
        check_vma=False,
    )
```

```python
import math

import jax
import jax.numpy as jnp
from jax import lax
from jax.experimental import pallas as pl
from jax.experimental.pallas import tpu as pltpu
from jax.sharding import PartitionSpec as P

D = 768
HEADS = 12
HD = 64
GRID = 24
COUNT = GRID * GRID
DATASETS = 10
NH = 4
GROUPS = HEADS // NH
WIDTH = NH * HD
LANES = 128
F32 = jnp.float32
BF16 = jnp.bfloat16
BOTH = ("rep", "wide")
VMEM = 60 << 20


def mm(left, right):
    return jnp.dot(left, right, preferred_element_type=F32)


def mm_tn(left, right):
    return lax.dot_general(left, right, (((0,), (0,)), ((), ())), preferred_element_type=F32)


def mm_nt(left, right):
    return lax.dot_general(left, right, (((1,), (1,)), ((), ())), preferred_element_type=F32)


def spec(shape, dtype=BF16):
    return jax.ShapeDtypeStruct(shape, dtype)


def whole(shape):
    return pl.BlockSpec(shape, lambda *_: (0,) * len(shape), pipeline_mode=pl.Buffered(1))


def params():
    return pltpu.CompilerParams(vmem_limit_bytes=VMEM)


def cost(macs, size):
    return pl.CostEstimate(flops=2 * int(macs), bytes_accessed=int(size), transcendentals=0)


def lasts(microseconds):
    return pl.CostEstimate(flops=int(microseconds * 1.15e9), bytes_accessed=0, transcendentals=0)


FLIP = {"y": 16, "x": 8, "z1": 4, "z0": 2, "c": 1}
XY, YX = ("x", "y"), ("y", "x")


def swap(value, *names):
    flip = sum(FLIP[name] for name in names)
    return lax.ppermute(value, BOTH, [(i, i ^ flip) for i in range(32)])


def bits():
    rep, wide = lax.axis_index("rep"), lax.axis_index("wide")
    return {"y": rep // 2, "x": rep % 2, "z1": wide // 4, "z0": (wide // 2) % 2, "c": wide % 2}


def bit_vector():
    b = bits()
    return jnp.stack([b[k] for k in ("y", "x", "z1", "z0", "c")]).astype(jnp.int32)


def along_z(parts):
    size = lax.axis_size("wide") // 2
    groups = [[2 * z + core for z in range(size)] for core in range(2)]
    return lax.all_to_all(parts, "wide", 0, 0, tiled=True, axis_index_groups=groups)


class Line:
    def __init__(self):
        self.tokens = []

    def after(self, value):
        return lax.optimization_barrier((value, *self.tokens))[0] if self.tokens else value

    def run(self, call, first, *rest):
        out = call(self.after(first), *rest)
        self.tokens = jax.tree.leaves(out)[-1:]
        return out

    def touch(self, *values):
        out = lax.optimization_barrier((*values, *self.tokens))
        self.tokens = list(out[:len(values)])
        return self.tokens

    def run_all(self, call, *values):
        out = call(*(lax.optimization_barrier((*values, *self.tokens))[:len(values)]))
        self.tokens = jax.tree.leaves(out)
        return out


def locate(me, order, plane, z, core):
    place = {order[0]: plane[0], order[1]: plane[1]}
    shard = ((me[2] ^ z[0]) * 2 + (me[3] ^ z[1])) * 2 + (me[4] ^ core)
    return shard, me[0] ^ place["y"], me[1] ^ place["x"]


class Gather:
    def __init__(self, piece, at, axis, swaps=False):
        self.at, self.axis, self.stage = at, axis, 0
        if swaps:
            self.terms = [piece, swap(piece, "z0"), swap(piece, "z1"), swap(piece, "z1", "z0")]
        else:
            self.terms = [along_z(jnp.broadcast_to(piece[None], (4,) + piece.shape))]
        self.relative = swaps

    def add(self, *terms):
        if self.stage == 0:
            value = jnp.stack(terms) if self.relative else terms[0]
            return [lax.slice_in_dim(value, 0, self.at, axis=self.axis + 1),
                    lax.slice_in_dim(value, self.at, value.shape[self.axis + 1], axis=self.axis + 1)]
        return [jnp.concatenate(terms[:2]), jnp.concatenate(terms[2:])]

    def send(self, out):
        one, two = out
        if self.stage == 0:
            self.terms = [one, swap(one, "x"), two, swap(two, "y")]
        else:
            self.terms = [one, swap(one, "y"), two, swap(two, "x")]
        self.stage += 1

    def starting(self, first):
        self.pieces[0] = first
        return self

    def between_cores(self, own=None):
        one, one_y, two, two_x = self.terms
        own = own or (swap(one, "c"), swap(two, "c"))
        self.pieces = [one, one_y, own[0], swap(one_y, "c"), two, two_x, own[1], swap(two_x, "c")]


PLANE = [[(s // 4, a % 2, s // 2 % 2, s % 2, a // 2) for s in range(8)] for a in range(4)]


def assemble(me, gathered, shapes, parts):
    at, axis = gathered.at, gathered.axis

    def halves(rows, cols):
        first, size = (rows, cols)[axis]
        out = []
        for low, high, shift in ((first, min(first + size, at), 0), (max(first, at), first + size, at)):
            span = (low - shift, high - low)
            out.append(None if high <= low else (span, cols, low - first, 0) if axis == 0 else (rows, span, 0, low - first))
        return out

    def body(me_ref, *refs):
        ins, outs, sem = refs[:8], refs[8:-1], refs[-1]
        started = []
        for half, order in enumerate((XY, YX)):
            for a, places in enumerate(PLANE):
                for s, (first, second, z1, z0, core) in enumerate(places):
                    z = (z1, z0) if gathered.relative else (me_ref[2] ^ z1, me_ref[3] ^ z0)
                    shard, y, x = locate(me_ref, order, (first, second), z, core)
                    for k, rows, cols, row, col in parts:
                        share = halves(rows, cols)[half]
                        if share is None or (row is None and (first or second)):
                            continue
                        (r0, r), (c0, n), down, across = share
                        source = ins[4 * half + a].at[s, pl.ds(r0, r), pl.ds(c0, n)]
                        if row is None:
                            place = outs[k].at[shard, pl.ds(down, r), pl.ds(across, n)]
                        else:
                            place = outs[k].at[pl.ds(pl.multiple_of(row(shard, y) + down, 16), r),
                                               pl.ds(pl.multiple_of(col(x) + across, LANES), n)]
                        copy = pltpu.make_async_copy(source, place, sem.at[len(started)])
                        copy.start()
                        started.append(copy)
        for copy in started:
            copy.wait()

    return pl.pallas_call(
        body,
        grid=(1,),
        in_specs=[pl.BlockSpec(memory_space=pltpu.SMEM)] + [pl.BlockSpec(memory_space=pl.ANY)] * 8,
        out_specs=[whole(s) for s in shapes],
        out_shape=[spec(s) for s in shapes],
        scratch_shapes=[pltpu.SemaphoreType.DMA((64 * len(parts),))],
        compiler_params=params(),
        cost_estimate=lasts(0),
        name="assemble",
    )(me, *gathered.pieces)


def together(line, *jobs):
    counts = [len(job.terms) for job in jobs]

    def call(*terms):
        out = []
        for job, count in zip(jobs, counts):
            out.append(job.add(*terms[:count]))
            terms = terms[count:]
        return out

    for job, out in zip(jobs, line.run_all(call, *[term for job in jobs for term in job.terms])):
        job.send(out)


class Chunk:
    def __init__(self, line, keep, send, split):
        self.split, self.stage = split, 0
        self.terms = [keep, swap(line.after(send), "c")]

    def add(self, *terms):
        if self.stage == 0:
            parts = [(slots, rows) for rows in (slice(0, self.split), slice(self.split, None)) for slots in (slice(0, 8), slice(8, 16))]
            return [terms[0][part] + terms[1][part] for part in parts]
        return [terms[i][part] + terms[i + 1][part] for i in (0, 2) for part in (slice(0, 4), slice(4, 8))]

    def send(self, out):
        one, two = ("x", "y") if self.stage == 0 else ("y", "x")
        self.terms = [out[0], swap(out[1], one), out[2], swap(out[3], two)]
        self.stage += 1


class Single(Chunk):
    def __init__(self, line, keep, send, order):
        super().__init__(line, keep, send, None)
        self.order = order

    def add(self, *terms):
        if self.stage == 2:
            return [terms[0] + terms[1]]
        half = terms[0].shape[0] // 2
        return [terms[0][part] + terms[1][part] for part in (slice(0, half), slice(half, None))]

    def send(self, out):
        self.terms = out if self.stage == 2 else [out[0], swap(out[1], self.order[self.stage])]
        self.stage += 1


class Along:
    def __init__(self, *chunks):
        self.stage, self.terms = 0, [term for chunk in chunks for term in chunk.terms]
        self.done = [len(chunk.terms) == 1 for chunk in chunks for _ in range(max(1, len(chunk.terms) // 2))]

    def add(self, *terms):
        if self.stage:
            return [sum(terms[0][i].astype(F32) for i in range(4)).astype(BF16)]
        terms = list(terms)
        sums = [terms.pop(0) if done else terms.pop(0) + terms.pop(0) for done in self.done]
        return [jnp.concatenate(sums, 1)]

    def send(self, out):
        if self.stage:
            self.total = out[0]
        else:
            self.terms = [along_z(out[0])]
        self.stage += 1


class Back:
    def __init__(self, line, *alongs):
        self.rows = [along.total.shape[0] for along in alongs]
        if len(alongs) > 1:
            (total,) = line.run_all(lambda *parts: [jnp.concatenate(parts)], *[along.total for along in alongs])
        else:
            total = alongs[0].total
        self.terms = [total, swap(total, "x"), swap(total, "y"), swap(total, "x", "y")]


class Whole:
    def __init__(self, value):
        self.terms = [value, swap(value, "x")]

    def add(self, *terms):
        return [terms[0] + terms[1]]

    def send(self, out):
        self.terms = [out[0], swap(out[0], "y")]


def finish(me, backs, places, shapes):
    ins = [t for back in backs for t in back.terms]

    def body(me_ref, *refs):
        outs = refs[len(ins):len(ins) + len(shapes)]
        held = refs[len(ins) + len(shapes):]
        for c, parts in enumerate(places):
            for q in range(4):
                held[c][q] = refs[4 * c + q][...]
            for y in range(2):
                for x in range(2):
                    at = 2 * (me_ref[0] ^ y) + (me_ref[1] ^ x)
                    for k, r, r0, blocks, row, col in parts:
                        for b in range(blocks):
                            at_row = row(y) + (r * x if shapes[k][1] == LANES else 0)
                            outs[k][at_row:at_row + r, col(x, b):col(x, b) + LANES] = (
                                held[c][at, r0 + b * r:r0 + (b + 1) * r, :].astype(F32))

    return pl.pallas_call(
        body,
        grid=(1,),
        in_specs=[pl.BlockSpec(memory_space=pltpu.SMEM)] + [whole(a.shape) for a in ins],
        out_specs=[whole(s) for s in shapes],
        out_shape=[spec(s, F32) for s in shapes],
        scratch_shapes=[pltpu.VMEM((4,) + back.terms[0].shape, BF16) for back in backs],
        compiler_params=params(),
        cost_estimate=lasts(3),
        name="finish",
    )(me, *ins)


PLAIN = "plain"
ALL_XY, ALL_YX = 1 << 30, 0


TABLE = 64


class Sink:
    def __init__(self, shapes, split, table=False):
        self.shapes, self.split, self.table = shapes, split, table
        rows = sum(k // 16 * (n // 2 // LANES) for k, n in shapes) + (TABLE // 4 if table else 0)
        if split == PLAIN:
            self.outs, self.scratch = [spec(s) for s in shapes], []
        else:
            self.outs = [spec((16, rows, LANES))] * 2
            self.scratch = [pltpu.VMEM((2, k, n // 2), BF16) for k, n in shapes]
            self.scratch += [pltpu.VMEM((TABLE, LANES), BF16)] if table else []

    def out_specs(self):
        return [whole(o.shape) for o in self.outs]

    def put(self, outs, held, k, rows, value):
        value = value.astype(BF16)
        half = self.shapes[k][1] // 2
        if self.split == PLAIN:
            outs[k][rows, :] = value
        else:
            held[k][0, rows, :] = value[:, :half]
            held[k][1, rows, :] = value[:, half:]

    def deliver(self, me_ref, outs, held):
        if self.split == PLAIN:
            return
        for core in range(2):
            for s in range(16):
                z = (me_ref[2] ^ (s // 2 % 2), me_ref[3] ^ (s % 2))
                places = [locate(me_ref, order, (s // 8, s // 4 % 2), z, core) for order in (XY, YX)]
                at = 0
                for k, (rows, cols) in enumerate(self.shapes):
                    r = rows // 16
                    size = r // 2 if r > 144 and r % 32 == 0 else r
                    for b in range(cols // 2 // LANES):
                        for part in range(0, r, size):
                            shard, y, x = places[0 if at < self.split else 1]
                            start = pl.multiple_of((shard * 2 + y) * r + part, 16)
                            outs[core][s, at:at + size, :] = held[k][x, pl.ds(start, size), b * LANES:(b + 1) * LANES]
                            at += size
                if self.table:
                    r = TABLE // 4
                    _, y, x = places[0 if at < self.split else 1]
                    outs[core][s, at:at + r, :] = held[-1][pl.ds(pl.multiple_of((2 * y + x) * r, 16), r), :]


def gelu_pair(values):
    cdf = 0.5 + 0.5 * lax.erf(values * 0.7071067811865476)
    pdf = 0.3989422804014327 * jnp.exp(-0.5 * values * values)
    return values * cdf, cdf + values * pdf


def gelu(values):
    return values * (0.5 + 0.5 * lax.erf(values * 0.7071067811865476))


def normalize(values):
    centred = values - jnp.mean(values, -1, keepdims=True)
    recip = lax.rsqrt(jnp.mean(centred * centred, -1, keepdims=True) + 1e-06)
    return centred * recip, recip


def norm_transpose(grad_normed, normed, recip):
    return recip * (
        grad_normed
        - jnp.mean(grad_normed, -1, keepdims=True)
        - normed * jnp.mean(grad_normed * normed, -1, keepdims=True)
    )


SMALL = 16


def prepare(me, w_qkv, w_out, w_fc1, w_fc2, w_re, w_head, gains, scales, shifts):
    ff, ch = w_fc1.shape[1], w_re.shape[1]
    half = w_qkv.shape[0] // 2
    rows_two, rows_head = w_fc2.shape[0] // 2, w_head.shape[0] // 2
    n = w_qkv.shape[1] // 2

    def body(me_ref, qkv_ref, out_ref, fc1_ref, fc2_ref, re_ref, head_ref, gains_ref, scales_ref, shifts_ref,
             zero_ref, one_ref, two_ref):
        zero_ref[half:half + SMALL, :] = jnp.zeros((SMALL, n), BF16)
        zero_ref[half:half + DATASETS, 0:scales.shape[1]] = scales_ref[...]
        zero_ref[half:half + DATASETS, LANES:LANES + shifts.shape[1]] = shifts_ref[...]
        zero_ref[half:half + 2, 2 * LANES:2 * LANES + gains.shape[1]] = gains_ref[...]
        rows = pl.ds(pl.multiple_of(me_ref[0] * half, 16), half)
        rows_of_two = pl.ds(pl.multiple_of(me_ref[0] * rows_two, 16), rows_two)
        rows_of_head = pl.ds(pl.multiple_of(me_ref[0] * rows_head, 16), rows_head)
        for x in range(2):
            @pl.when(me_ref[1] == x)
            def _():
                zero_ref[0:half, :] = qkv_ref[rows, n * x:n * (x + 1)]
                one_ref[:, :D // 2] = out_ref[rows, D // 2 * x:D // 2 * (x + 1)]
                at = D // 2 + ff // 2
                one_ref[:, D // 2:at] = fc1_ref[rows, ff // 2 * x:ff // 2 * (x + 1)]
                one_ref[:, at:at + ch // 2] = re_ref[rows, ch // 2 * x:ch // 2 * (x + 1)]
                one_ref[0:rows_head, at + ch // 2:] = head_ref[rows_of_head, ch // 2 * x:ch // 2 * (x + 1)]
                two_ref[...] = fc2_ref[rows_of_two, D // 2 * x:D // 2 * (x + 1)]
        one_ref[rows_head:, D // 2 + ff // 2 + ch // 2:] = jnp.zeros((half - rows_head, LANES), BF16)

    ins = (w_qkv, w_out, w_fc1, w_fc2, w_re, w_head, gains, scales, shifts)
    outs = [spec((half + SMALL, n)), spec((half, D // 2 + ff // 2 + ch // 2 + LANES)), spec((rows_two, D // 2))]
    return pl.pallas_call(
        body,
        grid=(1,),
        in_specs=[pl.BlockSpec(memory_space=pltpu.SMEM)] + [whole(a.shape) for a in ins],
        out_specs=[whole(o.shape) for o in outs],
        out_shape=outs,
        compiler_params=params(),
        cost_estimate=lasts(2.4),
        name="prepare",
    )(me, *ins)


def norm_body(x_ref, out_ref):
    out_ref[...] = normalize(x_ref[...].astype(F32))[0]


def norm(x):
    rows = x.shape[0]
    block = pl.BlockSpec((rows // 4, D), lambda i: (i, 0))
    return pl.pallas_call(
        norm_body,
        grid=(4,),
        in_specs=[block],
        out_specs=block,
        out_shape=spec((rows, D), F32),
        compiler_params=params(),
        cost_estimate=lasts(4.4),
        name="norm",
    )(x)


def bilinear(targets, sources, first):
    size = 2 * GRID
    step = (GRID - 1) / (size - 1)

    def hat(target, source):
        return jnp.maximum(1.0 - jnp.abs(target.astype(F32) * step - source.astype(F32)), 0.0)

    target = lax.broadcasted_iota(jnp.int32, targets, targets.index(max(targets))) + first
    source = lax.broadcasted_iota(jnp.int32, sources, sources.index(max(sources)))
    return (hat(target // size, source // GRID) * hat(target % size, source % GRID)).astype(BF16)


def is_live(count_ref, image):
    return (image < count_ref[0]).astype(F32)


def down_body(dj_ref, count_ref, flag_ref, down_ref, gshift_ref):
    step, images, size = pl.program_id(0), dj_ref.shape[0], dj_ref.shape[1]
    table = bilinear((1, size), (COUNT, 1), step * size)
    for i in range(images):
        part = mm(table, dj_ref[i])
        sums = jnp.sum(dj_ref[i].astype(F32), 0, keepdims=True)

        @pl.when(step == 0)
        def _():
            down_ref[i] = part
            gshift_ref[i] = sums

        @pl.when(step > 0)
        def _():
            down_ref[i] += part
            gshift_ref[i] += sums

        @pl.when(step == pl.num_programs(0) - 1)
        def _():
            down_ref[i] = down_ref[i] * is_live(count_ref, i)
            gshift_ref[i] = gshift_ref[i] * (is_live(count_ref, i) * flag_ref[i].astype(F32))


def bring_down(dj, live_count, flag):
    images, count, ch = dj.shape
    one = whole((images, 1, ch))
    return pl.pallas_call(
        down_body,
        grid=(4,),
        in_specs=[pl.BlockSpec((images, count // 4, ch), lambda i: (0, i, 0))] + [pl.BlockSpec(memory_space=pltpu.SMEM)] * 2,
        out_specs=[whole((images, COUNT, ch)), one],
        out_shape=[spec((images, COUNT, ch), F32), spec((images, 1, ch), F32)],
        compiler_params=params(),
        cost_estimate=lasts(8.9),
        name="bring_down",
    )(dj, live_count, flag)


def tables_body(small_ref, id_ref, flag_ref, scale_ref, shift_ref):
    shards, rows, _ = small_ref.shape
    ch = scale_ref.shape[2]
    width = ch // shards
    whole_tables = [jnp.zeros((rows, ch), F32), jnp.zeros((rows, ch), F32)]
    lane = lax.broadcasted_iota(jnp.int32, (LANES, ch), 0)
    col = lax.broadcasted_iota(jnp.int32, (LANES, ch), 1)
    for w in range(shards):
        place = ((col == lane + width * w) & (lane < width)).astype(BF16)
        for k in range(2):
            whole_tables[k] = whole_tables[k] + mm(small_ref[w, :, LANES * k:LANES * (k + 1)], place)
    row = lax.broadcasted_iota(jnp.int32, (rows, 1), 0)
    for i in range(scale_ref.shape[0]):
        mask = row == id_ref[i]
        scale_ref[i] = jnp.sum(jnp.where(mask, whole_tables[0], 0.0), 0, keepdims=True)
        shift_ref[i] = jnp.sum(jnp.where(mask, whole_tables[1], 0.0), 0, keepdims=True) * flag_ref[i].astype(F32)


def tables(small, ids, flags, ch):
    out = spec((ids.shape[0], 1, ch), F32)
    return pl.pallas_call(
        tables_body,
        grid=(1,),
        in_specs=[whole(small.shape)] + [pl.BlockSpec(memory_space=pltpu.SMEM)] * 2,
        out_specs=[whole(out.shape)] * 2,
        out_shape=[out] * 2,
        compiler_params=params(),
        cost_estimate=lasts(2),
        name="tables",
    )(small, ids, flags)


def attention_body(a1_ref, wq_ref, wk_ref, wv_ref, qkv_ref, o_ref, e_ref, r_ref):
    for i, ref in enumerate((wq_ref, wk_ref, wv_ref)):
        qkv_ref[:, WIDTH * i:WIDTH * (i + 1)] = mm(a1_ref[...], ref[...]).astype(BF16)
    def part(kind, h):
        return slice(WIDTH * kind + HD * h, WIDTH * kind + HD * (h + 1))

    def scores(h):
        return mm_nt(qkv_ref[:, part(1, h)], qkv_ref[:, part(0, h)] * jnp.asarray(0.125, BF16))

    following = scores(0)
    for h in range(NH):
        s, following = following, scores(h + 1) if h + 1 < NH else None
        e = jnp.exp(s - jnp.max(s, 0, keepdims=True))
        r = 1.0 / jnp.sum(e, 0, keepdims=True)
        low = e.astype(BF16)
        e_ref[h] = low
        o_ref[:, HD * h:HD * (h + 1)] = (mm_tn(qkv_ref[:, part(2, h)], low) * r).T.astype(BF16)
        r_ref[0, h:h + 1, :] = r


def group_specs():
    def cols(n):
        return pl.BlockSpec((COUNT, n), lambda i: (i, 0))

    return cols, pl.BlockSpec((NH, COUNT, COUNT), lambda i: (i, 0, 0)), pl.BlockSpec((1, NH, COUNT), lambda i: (i, 0, 0))


def group_columns(group):
    return [pl.BlockSpec((D, WIDTH), lambda i, p=p: (0, GROUPS * p + group), pipeline_mode=pl.Buffered(1)) for p in range(3)]


def attention(a1, w, group):
    rows = a1.shape[0]
    images = rows // COUNT
    cols, probs, sums = group_specs()
    return pl.pallas_call(
        attention_body,
        grid=(images,),
        in_specs=[cols(D)] + group_columns(group),
        out_specs=[cols(3 * WIDTH), cols(WIDTH), probs, sums],
        out_shape=[spec((rows, 3 * WIDTH)), spec((rows, WIDTH)), spec((images * NH, COUNT, COUNT)),
                   spec((images, NH, COUNT), F32)],
        compiler_params=params(),
        cost_estimate=lasts(11),
        name="attention",
    )(a1, w, w, w)


def attention_back(da, me, group, qkv, o, e, r, a1, w_out, extra, split):
    rows = da.shape[0]
    images = rows // COUNT
    cols, probs, sums = group_specs()
    shape = (D, 3 * WIDTH)
    sink = Sink([shape], PLAIN) if extra is None else Sink([shape, (D, D)], split)
    n_out = len(sink.outs)
    extra = list(extra) if isinstance(extra, (list, tuple)) else [] if extra is None else [extra]

    def body(da_ref, me_ref, qkv_ref, o_ref, e_ref, r_ref, a1_ref, wout_ref, *refs):
        more, refs = refs[:len(extra)], refs[len(extra):]
        grads, dqkv, total, held = refs[:n_out], refs[n_out], refs[n_out + 1], refs[n_out + 2:]
        if len(extra) > 1:
            total_out, held = held[0], held[1:]
        step = pl.program_id(0)
        ones = jnp.ones((8, HD), BF16)
        do_all = mm_nt(da_ref[...], wout_ref[...]).astype(BF16)
        for h in range(NH):
            q, k, v = (slice(WIDTH * i + HD * h, WIDTH * i + HD * (h + 1)) for i in range(3))
            do = do_all[:, HD * h:HD * (h + 1)]
            delta = mm_nt(ones, (do.astype(F32) * o_ref[:, HD * h:HD * (h + 1)].astype(F32)).astype(BF16))[0:1]
            prob = e_ref[h].astype(F32) * r_ref[0, h:h + 1, :]
            dp = mm_nt(qkv_ref[:, v], do)
            ds = (prob * (dp - delta)).astype(BF16)
            dqkv[:, v] = mm(prob.astype(BF16), do).astype(BF16)
            dqkv[:, k] = (mm(ds, qkv_ref[:, q]) * 0.125).astype(BF16)
            dqkv[:, q] = (mm_tn(ds, qkv_ref[:, k]) * 0.125).astype(BF16)
        g = mm_tn(a1_ref[...], dqkv[...])
        g_out = [mm_tn(ref[...], da_ref[...]) for ref in more] if len(extra) > 1 else []

        @pl.when(step == 0)
        def _():
            total[...] = g
            for i, part in enumerate(g_out):
                total_out[WIDTH * i:WIDTH * (i + 1)] = part

        @pl.when(step > 0)
        def _():
            total[...] += g
            for i, part in enumerate(g_out):
                total_out[WIDTH * i:WIDTH * (i + 1)] += part

        @pl.when(step == images - 1)
        def _():
            sink.put(grads, held, 0, slice(0, D), total[...])
            if len(extra) > 1:
                sink.put(grads, held, 1, slice(0, D), total_out[...])
            elif extra:
                sink.put(grads, held, 1, slice(0, D), more[0][...])
            sink.deliver(me_ref, grads, held)

    more_specs = [cols(WIDTH)] * len(extra) if len(extra) > 1 else [whole(a.shape) for a in extra]
    out = pl.pallas_call(
        body,
        grid=(images,),
        in_specs=[cols(D), pl.BlockSpec(memory_space=pltpu.SMEM), cols(3 * WIDTH), cols(WIDTH), probs, sums, cols(D),
                  pl.BlockSpec((WIDTH, D), lambda i: (group, 0))] + more_specs,
        out_specs=sink.out_specs() + [cols(3 * WIDTH)],
        out_shape=sink.outs + [spec((rows, 3 * WIDTH))],
        scratch_shapes=[pltpu.VMEM(shape, F32)] + ([pltpu.VMEM((D, D), F32)] if len(extra) > 1 else []) + sink.scratch,
        compiler_params=params(),
        cost_estimate=lasts(18),
        name="attention_back",
    )(da, me, qkv, o, e, r, a1, w_out, *extra)
    return out[:n_out], out[n_out]


def input_back(dqkv, w, dx2, x, gains):
    rows = x.shape[0]
    block = rows // 4

    def body(*refs):
        (w_ref, dx2_ref, x_ref, gains_ref), out_ref = refs[GROUPS:-1], refs[-1]
        da1 = jnp.zeros((block, D), F32)
        for i, ref in enumerate(refs[:GROUPS]):
            for p in range(3):
                at = D * p + WIDTH * i
                da1 = da1 + mm_nt(ref[:, WIDTH * p:WIDTH * (p + 1)], w_ref[:, at:at + WIDTH])
        n1, rs1 = normalize(x_ref[...].astype(F32))
        out_ref[...] = (dx2_ref[...].astype(F32) + norm_transpose(da1 * gains_ref[0:1], n1, rs1)).astype(BF16)

    def cols(n):
        return pl.BlockSpec((block, n), lambda i: (i, 0))

    return pl.pallas_call(
        body,
        grid=(4,),
        in_specs=[cols(3 * WIDTH)] * GROUPS + [whole(w.shape), cols(D), cols(D), whole(gains.shape)],
        out_specs=cols(D),
        out_shape=spec((rows, D)),
        compiler_params=params(),
        cost_estimate=lasts(9),
        name="input_back",
    )(*dqkv, w, dx2, x, gains)


def mlp_up_body(x_ref, o0_ref, o1_ref, o2_ref, wout_ref, w1_ref, gains_ref, x2_ref, a2_ref, u_ref):
    rows = x2_ref.shape[0]
    chunk = rows // 4

    @pl.when(pl.program_id(0) == 0)
    def _():
        for p in range(0, rows, chunk):
            at = slice(p, p + chunk)
            x2 = x_ref[at].astype(F32)
            for i, ref in enumerate((o0_ref, o1_ref, o2_ref)):
                x2 = x2 + mm(ref[at], wout_ref[WIDTH * i:WIDTH * (i + 1)])
            x2_ref[at] = x2.astype(BF16)
            a2_ref[at] = (normalize(x2)[0] * gains_ref[1:2]).astype(BF16)

    u_ref[...] = mm(a2_ref[...], w1_ref[...]).astype(BF16)


def mlp_up(x, heads_out, w_out, w1, gains, block=1024):
    rows, ff = x.shape[0], w1.shape[1]
    full, cols = whole((rows, D)), pl.BlockSpec((rows, block), lambda i: (0, i))
    return pl.pallas_call(
        mlp_up_body,
        grid=(ff // block,),
        in_specs=[full] + [whole((rows, WIDTH))] * 3 + [whole((D, D)), pl.BlockSpec((D, block), lambda i: (0, i)), whole((2, D))],
        out_specs=[full, full, cols],
        out_shape=[spec((rows, D)), spec((rows, D)), spec((rows, ff))],
        compiler_params=params(),
        cost_estimate=lasts(18),
        name="mlp_up",
    )(x, *heads_out, w_out, w1, gains)


def mlp_down_body(u_ref, w2_ref, x2_ref, count_ref, x3b_ref, out_ref):
    x3 = x2_ref[...].astype(F32)
    size = u_ref.shape[1] // 6
    for k in range(6):
        at = slice(size * k, size * (k + 1))
        act = gelu(u_ref[:, at].astype(F32)).astype(BF16)
        x3 = x3 + mm(act, w2_ref[at, :])
    x3b_ref[...] = x3.astype(BF16)
    image = pl.program_id(0) * x3b_ref.shape[0] // COUNT
    out_ref[...] = (x3 * (image < count_ref[0]).astype(F32)).astype(BF16)


def mlp_down(gg, w2, x2, live_count):
    rows, ff = gg.shape
    block = rows // 4
    at = pl.BlockSpec((block, D), lambda i: (i, 0))
    return pl.pallas_call(
        mlp_down_body,
        grid=(4,),
        in_specs=[pl.BlockSpec((block, ff), lambda i: (i, 0)), whole(w2.shape), at, pl.BlockSpec(memory_space=pltpu.SMEM)],
        out_specs=[at, at],
        out_shape=[spec((rows, D))] * 2,
        compiler_params=params(),
        cost_estimate=lasts(11),
        name="mlp_down",
    )(gg, w2, x2, live_count)


def spread(value, out_ref, rows, sign):
    count, ch = value.shape
    at = lax.broadcasted_iota(jnp.int32, (count, 1), 0)
    col = at % GRID
    gap = jnp.zeros((GRID, ch), F32)
    for dx in (-1, 0, 1):
        step = sign * dx
        moved = value
        if step:
            moved = pltpu.roll(value, (-step) % count, 0)
            moved = jnp.where((col + step >= 0) & (col + step < GRID), moved, 0.0)
        for dy in (-1, 0, 1):
            block = 3 * (dy + 1) + dx + 1
            if sign * dy == 1:
                part = jnp.concatenate([moved[GRID:], gap], 0)
            elif sign * dy == -1:
                part = jnp.concatenate([gap, moved[:-GRID]], 0)
            else:
                part = moved
            out_ref[rows, block * ch:(block + 1) * ch] = part.astype(BF16)


def units_body(x_ref, wre_ref, w_ref, t1_ref, s1_ref, t2_ref, s2_ref, zb_ref, cols, z_ref):
    unit = pl.program_id(0)
    images = [slice(COUNT * i, COUNT * (i + 1)) for i in range(x_ref.shape[0] // COUNT)]

    @pl.when(unit == 0)
    def _():
        z_ref[...] = mm(x_ref[...], wre_ref[...])

    inner = []
    for at in images:
        act, slope = gelu_pair(z_ref[at])
        t1_ref[0, at], s1_ref[0, at] = act.astype(BF16), slope.astype(BF16)
        spread(act, cols, at, 1)
        inner.append(mm(cols[at], w_ref[0]))
    for at, value in zip(images, inner):
        act, slope = gelu_pair(value)
        t2_ref[0, at], s2_ref[0, at] = act.astype(BF16), slope.astype(BF16)
        spread(act, cols, at, 1)
        z_ref[at] += mm(cols[at], w_ref[1])

    @pl.when(unit == 1)
    def _():
        zb_ref[...] = z_ref[...].astype(BF16)


def units(x3b, w_re, w_conv):
    rows, ch = x3b.shape[0], w_re.shape[1]
    acts = pl.BlockSpec((1, rows, ch), lambda i: (i, 0, 0))
    return pl.pallas_call(
        units_body,
        grid=(2,),
        in_specs=[whole(x3b.shape), whole(w_re.shape), pl.BlockSpec((2,) + w_conv.shape[1:], lambda i: (i, 0, 0))],
        out_specs=[acts] * 4 + [whole((rows, ch))],
        out_shape=[spec((2, rows, ch))] * 4 + [spec((rows, ch))],
        scratch_shapes=[pltpu.VMEM((rows, 9 * ch), BF16), pltpu.VMEM((rows, ch), F32)],
        compiler_params=params(),
        cost_estimate=lasts(18),
        name="units",
    )(x3b, w_re, w_conv)


def units_back_body(down_ref, scale_ref, gshift_ref, id_ref, z_ref, x3b_ref, gt_ref, count_ref, whead_ref, wre_ref,
                    w_ref, t1_ref, s1_ref, t2_ref, s2_ref,
                    gw_ref, ghead_ref, gre_ref, dm_ref, table_ref, moved_two, turned_two, dz_ref):
    images, _, ch = down_ref.shape

    @pl.when(pl.program_id(0) == 0)
    def _():
        dq = jnp.concatenate([(down_ref[i] * scale_ref[i]).astype(BF16) for i in range(images)], 0)
        ghead_ref[...] = mm_tn(z_ref[...], dq).astype(BF16)
        dz_ref[...] = mm_nt(dq, whead_ref[...])
        table_ref[...] = jnp.zeros_like(table_ref)
        for i in range(images):
            head = mm(z_ref[COUNT * i:COUNT * (i + 1)], whead_ref[...])
            sums = (jnp.sum(head * down_ref[i], 0, keepdims=True), gshift_ref[i])
            for b in range(2 * ch // LANES):
                at, row = SMALL * b, sums[b // (ch // LANES)]
                cols = slice(LANES * (b % (ch // LANES)), LANES * (b % (ch // LANES) + 1))
                hot = lax.broadcasted_iota(jnp.int32, (SMALL, 1), 0) == id_ref[i]
                table_ref[at:at + SMALL] += jnp.where(hot, row[:, cols], 0.0)

    places = [slice(COUNT * i, COUNT * (i + 1)) for i in range(images)]

    def back(index, grads, act_ref, slope_ref):
        moved, turned = moved_two.at[index], turned_two.at[index]
        for b in range(9):
            at = slice(ch * b, ch * (b + 1))
            turned[:, at] = w_ref[index, at, :]
        out = []
        for at, grad in zip(places, grads):
            spread(grad, moved, at, -1)
            out.append(mm_nt(moved[at, :], turned[...]) * slope_ref[0, at].astype(F32))
        g = mm_tn(act_ref[0], moved[...])
        for b in range(9):
            at = slice(ch * b, ch * (b + 1))
            gw_ref[index, at, :] = g[:, at].astype(BF16)
        return out

    grads = back(1, [dz_ref[at] for at in places], t2_ref, s2_ref)
    for at, grad in zip(places, back(0, grads, t1_ref, s1_ref)):
        dz_ref[at] += grad

    @pl.when(pl.program_id(0) == 1)
    def _():
        dr = dz_ref[...].astype(BF16)
        gre_ref[...] = mm_tn(x3b_ref[...], dr).astype(BF16)
        dx3 = mm_nt(dr, wre_ref[...])
        for i in range(images):
            at = slice(COUNT * i, COUNT * (i + 1))
            part = gt_ref[at].astype(F32) * is_live(count_ref, i) + dx3[at]
            dm_ref[at] = part.astype(BF16)


def units_back(down, scale, gshift, ids, z, x3b, gt, live_count, w_head, w_conv, w_re, t1, s1, t2, s2):
    rows, ch = z.shape
    ins = (down, scale, gshift, ids, z, x3b, gt, live_count, w_head, w_re)
    outs = [spec(w_conv.shape), spec(w_head.shape), spec(w_re.shape), spec((rows, D)),
            spec((2 * ch // LANES * SMALL, LANES), F32)]
    kernels = pl.BlockSpec((2,) + w_conv.shape[1:], lambda i: (1 - i, 0, 0))
    act = pl.BlockSpec((1, rows, ch), lambda i: (1 - i, 0, 0))
    return pl.pallas_call(
        units_back_body,
        grid=(2,),
        in_specs=[pl.BlockSpec(memory_space=pltpu.SMEM) if a is live_count or a is ids else whole(a.shape) for a in ins] + [kernels] + [act] * 4,
        out_specs=[kernels] + [whole(a.shape) for a in outs[1:]],
        out_shape=outs,
        scratch_shapes=[pltpu.VMEM((2, rows, 9 * ch), BF16), pltpu.VMEM((2, ch, 9 * ch), BF16), pltpu.VMEM((rows, ch), F32)],
        compiler_params=params(),
        cost_estimate=lasts(30),
        name="units_back",
    )(*ins, w_conv, t1, s1, t2, s2)


def hidden_back(dm, me, u, w2, split, block=512):
    rows, ff = u.shape
    sink = Sink([(ff, D)], split)
    n_out = len(sink.outs)

    def body(dm_ref, me_ref, u_ref, w2_ref, *refs):
        grads, du_ref, held = refs[:n_out], refs[n_out], refs[n_out + 1:]
        step = pl.program_id(0)
        at = pl.ds(pl.multiple_of(step * block, block), block)
        act, slope = gelu_pair(u_ref[...].astype(F32))
        sink.put(grads, held, 0, at, mm_tn(act.astype(BF16), dm_ref[...]))
        du_ref[...] = (mm_nt(dm_ref[...], w2_ref[...]) * slope).astype(BF16)

        @pl.when(step == pl.num_programs(0) - 1)
        def _():
            sink.deliver(me_ref, grads, held)

    cols = pl.BlockSpec((rows, block), lambda i: (0, i))
    out = pl.pallas_call(
        body,
        grid=(ff // block,),
        in_specs=[whole((rows, D)), pl.BlockSpec(memory_space=pltpu.SMEM), cols, pl.BlockSpec((block, D), lambda i: (i, 0))],
        out_specs=sink.out_specs() + [cols],
        out_shape=sink.outs + [spec((rows, ff))],
        scratch_shapes=sink.scratch,
        compiler_params=params(),
        cost_estimate=lasts(20),
        name="hidden_back",
    )(dm, me, u, w2)
    return out[:n_out], out[n_out]


def first_weight_back(du, me, a2, g_re, g_head, table, split, block=512):
    rows, ff = du.shape
    sink = Sink([(D, ff), g_re.shape, g_head.shape], split, True)
    n_out = len(sink.outs)
    half = ff // 2 // block

    def body(du_ref, me_ref, a2_ref, gre_ref, ghead_ref, table_ref, *refs):
        step = pl.program_id(0)
        grads, held = refs[:n_out], refs[n_out:]
        g = mm_tn(a2_ref[...], du_ref[...]).astype(BF16)
        cols = pl.ds(pl.multiple_of(step % half * block, block), block)
        if split == PLAIN:
            grads[0][:, pl.ds(pl.multiple_of(step * block, block), block)] = g
        else:
            held[0][step // half, :, cols] = g

        @pl.when(step == pl.num_programs(0) - 1)
        def _():
            sink.put(grads, held, 1, slice(0, g_re.shape[0]), gre_ref[...])
            sink.put(grads, held, 2, slice(0, g_head.shape[0]), ghead_ref[...])
            if split != PLAIN:
                held[-1][...] = table_ref[...].astype(BF16)
            sink.deliver(me_ref, grads, held)

    return pl.pallas_call(
        body,
        grid=(ff // block,),
        in_specs=[pl.BlockSpec((rows, block), lambda i: (0, i)), pl.BlockSpec(memory_space=pltpu.SMEM), whole((rows, D)),
                  whole(g_re.shape), whole(g_head.shape), whole(table.shape)],
        out_specs=sink.out_specs(),
        out_shape=sink.outs,
        scratch_shapes=sink.scratch,
        compiler_params=params(),
        cost_estimate=lasts(13),
        name="first_weight_back",
    )(du, me, a2, g_re, g_head, table)


def mlp_back_body(du_ref, w1_ref, dm_ref, x2_ref, gains_ref, da_ref):
    n2, rs2 = normalize(x2_ref[...].astype(F32))
    da2 = mm_nt(du_ref[...], w1_ref[...])
    da_ref[...] = (dm_ref[...].astype(F32) + norm_transpose(da2 * gains_ref[1:2], n2, rs2)).astype(BF16)


def mlp_back(du, w1, dm, x2, gains):
    rows, ff = du.shape
    block = rows // 4

    def cols(n):
        return pl.BlockSpec((block, n), lambda i: (i, 0))

    return pl.pallas_call(
        mlp_back_body,
        grid=(4,),
        in_specs=[cols(ff), whole(w1.shape), cols(D), cols(D), whole((2, D))],
        out_specs=cols(D),
        out_shape=spec((rows, D)),
        compiler_params=params(),
        cost_estimate=lasts(13),
        name="mlp_back",
    )(du, w1, dm, x2, gains)


def join_body(z_ref, w_ref, scale_ref, shift_ref, count_ref, out_ref, head_ref):
    step, images, size = pl.program_id(0), out_ref.shape[0], out_ref.shape[1]

    @pl.when(step == 0)
    def _():
        for i in range(images):
            head = mm(z_ref[COUNT * i:COUNT * (i + 1)], w_ref[...])
            head_ref[i] = head.astype(BF16)

    table = bilinear((size, 1), (1, COUNT), step * size)
    for i in range(images):
        out_ref[i] = ((mm(table, head_ref[i]) * scale_ref[i] + shift_ref[i]) * is_live(count_ref, i)).astype(BF16)


def join(z, w_head, scale, shift, live_count):
    images, ch = scale.shape[0], w_head.shape[1]
    one = whole((images, 1, ch))
    return pl.pallas_call(
        join_body,
        grid=(4,),
        in_specs=[whole(z.shape), whole(w_head.shape), one, one, pl.BlockSpec(memory_space=pltpu.SMEM)],
        out_specs=pl.BlockSpec((images, COUNT, ch), lambda i: (0, i, 0)),
        out_shape=spec((images, 4 * COUNT, ch)),
        scratch_shapes=[pltpu.VMEM((images, COUNT, ch), BF16)],
        compiler_params=params(),
        cost_estimate=lasts(7),
        name="join",
    )(z, w_head, scale, shift, live_count)


def shards(tokens, live_count, dataset_id, shift_flag, norm_gains, w_qkv, w_attn_out, w_fc1, w_fc2, w_reassemble,
           conv_kernels, w_head, scale_table, shift_table, d_tokens_out, d_joined):
    slots, count = tokens.shape[:2]
    rows = slots * count
    neighbours = (lax.axis_size("rep"), lax.axis_size("wide")) == (4, 8)
    ch, ff = w_head.shape[1], w_fc1.shape[1]
    wide = lax.axis_size("wide")
    at_wide = lax.axis_index("wide")
    g, t = norm_gains.shape[1], scale_table.shape[1]
    me = bit_vector()
    line = Line()
    r = D // 16

    def gathered(part, axis):
        return lax.all_gather(part, "wide", axis=axis, tiled=True)

    def rows_of(size):
        return lambda shard, y: (shard * 2 + y) * size

    def cols_of(size):
        return lambda x: x * size

    x = tokens.reshape(rows, D)

    if neighbours:
        pieces = line.run(lambda v: prepare(me, v, w_attn_out, w_fc1, w_fc2, w_reassemble, w_head, norm_gains, scale_table,
                                            shift_table), w_qkv)
        zero = Gather(pieces[0], 5 * LANES, 1, True)
    down, g_shift_rows = line.run(bring_down, d_joined, live_count, shift_flag)
    if neighbours:
        together(line, zero)
    n1 = line.run(norm, x)
    if neighbours:
        together(line, zero)
        zero.between_cores()
        one = Gather(line.after(pieces[1]), 9 * LANES, 1)
        f_qkv, small = line.run(lambda v: assemble(me, zero.starting(v), [(D, 3 * D), (wide, SMALL, 3 * LANES)], [
            (0, (0, r), (0, 3 * D // 2), rows_of(r), cols_of(3 * D // 2)), (1, (r, SMALL), (0, 3 * LANES), None, None)]), zero.pieces[0])
        together(line, one)

        def table(lead, start, n):
            return small[:, :lead, start:start + n].transpose(1, 0, 2).reshape(lead, wide * n)

        gains = table(2, 2 * LANES, g)
    else:
        gains, scales, shifts = gathered(norm_gains, 1), gathered(scale_table, 1), gathered(shift_table, 1)
        f_qkv = gathered(w_qkv, 0)

    gains = gains.astype(F32)
    a1 = line.run(lambda n: (n * gains[0:1]).astype(BF16), n1)
    groups = []
    for i in range(GROUPS):
        groups.append(line.run(attention, a1, f_qkv, i))
        if neighbours and i == 0:
            together(line, one)
            own = [swap(one.terms[0], "c"), swap(one.terms[2], "c")]
            two = Gather(line.after(pieces[2]), ff // 32, 0)
        if neighbours and i == 1:
            *one.terms, own_a, own_b = line.touch(*one.terms, *own)
            one.between_cores((own_a, own_b))
            together(line, two)
        if i == 1:
            f_conv = gathered(line.after(conv_kernels), 1)

    def weights_one():
        if not neighbours:
            return gathered(w_attn_out, 0), gathered(w_fc1, 0), gathered(w_reassemble, 0), gathered(w_head, 0)
        rh, at = ch // 16, D // 2 + ff // 2
        return line.run(lambda v: assemble(me, one.starting(v), [(D, D), (D, ff), (D, ch), (ch, ch)], [
            (0, (0, r), (0, D // 2), rows_of(r), cols_of(D // 2)),
            (1, (0, r), (D // 2, ff // 2), rows_of(r), cols_of(ff // 2)),
            (2, (0, r), (at, ch // 2), rows_of(r), cols_of(ch // 2)),
            (3, (0, rh), (at + ch // 2, ch // 2), rows_of(rh), cols_of(ch // 2))]), one.pieces[0])

    def weights_two():
        if not neighbours:
            return gathered(w_fc2, 0)
        n = ff // 16
        return line.run(lambda v: assemble(me, two.starting(v), [(ff, D)], [(0, (0, n), (0, D // 2), rows_of(n), cols_of(D // 2))])[0],
                        two.pieces[0])

    heads_out = [group[1] for group in groups]
    if neighbours:
        scale, shift = line.run(tables, small, dataset_id, shift_flag, ch)
    else:
        onehot = (dataset_id[:, None] == jnp.arange(DATASETS, dtype=jnp.int32)[None, :]).astype(F32)
        scale = jnp.sum(onehot[:, :, None] * scales.astype(F32)[None], 1)[:, None]
        shift = jnp.sum(onehot[:, :, None] * shifts.astype(F32)[None], 1)[:, None] * shift_flag.astype(F32)[:, None, None]
    f_out, f_fc1, f_re, f_head = weights_one()
    if neighbours:
        together(line, two)
        own = [swap(two.terms[0], "c"), swap(two.terms[2], "c")]
    x2, a2, u = line.run(lambda v: mlp_up(v, heads_out, f_out, f_fc1, gains), x)
    if neighbours:
        *two.terms, own_a, own_b = line.touch(*two.terms, *own)
        two.between_cores((own_a, own_b))
    f_fc2 = weights_two()
    x3b, tokens_out = line.run(mlp_down, u, f_fc2, x2, live_count)
    t1, s1, t2, s2, zb = line.run(units, x3b, f_re, f_conv)

    def packed(split):
        return split if neighbours else PLAIN

    def chunk(grads, split):
        return Chunk(line, grads[0], grads[1], split) if neighbours else grads

    def go(*jobs):
        if neighbours:
            together(line, *jobs)

    g_conv, g_head, g_re, dm, small = line.run(
        lambda v: units_back(v, scale, g_shift_rows, dataset_id, zb, x3b, d_tokens_out.reshape(rows, D), live_count, f_head, f_conv, f_re,
                             t1, s1, t2, s2), down)
    s_conv = lax.psum_scatter(g_conv, "wide", scatter_dimension=1, tiled=True)
    split_two, split_one = 3 * ff // 32, 7 * r
    grads, du = line.run(lambda v: hidden_back(v, me, u, f_fc2, packed(split_two)), dm)
    c_two = chunk(grads, split_two)
    grads = line.run(lambda v: first_weight_back(v, me, a2, g_re, g_head, small, packed(split_one)), du)
    go(c_two)
    c_one = chunk(grads, split_one)
    da = line.run(lambda v: mlp_back(v, f_fc1, dm, x2, gains), du)
    go(c_two, c_one)

    def attention_step(i, extra, split):
        qkv, o, e, rs = groups[i]
        return line.run(lambda v: attention_back(v, me, i, qkv, o, e, rs, a1, f_out, extra, packed(split)), da)

    grads, dqkv_0 = attention_step(0, heads_out, ALL_XY)
    if neighbours:
        z_two = Along(c_two)
        together(line, z_two, c_one)
        c_first = Single(line, grads[0], grads[1], XY)
        c_conv = Whole(s_conv)
    else:
        c_first = grads
    (g_second,), dqkv_1 = attention_step(1, None, PLAIN)
    split_last = 3 * r
    if neighbours:
        z_one = Along(c_one)
        together(line, z_two, z_one, c_first, c_conv)
    grads, dqkv_2 = attention_step(2, g_second, split_last)
    if neighbours:
        c_conv.terms = line.touch(*c_conv.terms)
        together(line, z_one, c_first)
        early = Back(line, z_two, z_one)
        c_last = Chunk(line, grads[0], grads[1], split_last)
    else:
        c_last = grads
    joined = line.run(join, zb, f_head, scale, shift, live_count)
    if neighbours:
        together(line, c_last, c_first)
    d_tokens = line.run(lambda v: input_back((dqkv_0, dqkv_1, v), f_qkv, da, x, gains), dqkv_2)

    if neighbours:
        together(line, c_last)
        rh, rows_two, half = ch // 16, ff // 16, D // 2
        blocks, n, quarter = half // LANES, ff // 2 // LANES, TABLE // 4

        def up_to(size):
            return lambda y: size * y

        def across(size):
            return lambda x, b: x * size + b * LANES

        def group_col(i):
            def col(x, b):
                at = blocks * x + b
                return at // 2 * D + WIDTH * i + at % 2 * LANES
            return col

        low = early.rows[0]
        s_fc2, s_fc1, s_re, s_head, small = line.run(lambda m: finish(m, [early], [[
            (0, rows_two, 0, blocks, up_to(rows_two), across(half)),
            (1, r, low, n, up_to(r), across(ff // 2)),
            (2, r, low + r * n, 1, up_to(r), across(ch // 2)),
            (3, rh, low + r * (n + 1), 1, up_to(rh), across(ch // 2)),
            (4, quarter, low + r * (n + 1) + rh, 1, up_to(2 * quarter), lambda x, b: 0)]],
            [w_fc2.shape, w_fc1.shape, w_reassemble.shape, w_head.shape, (TABLE, LANES)]), me)
        z_last = Along(c_first, c_last)
        together(line, z_last)
        s_conv = line.run_all(lambda p, q: p.astype(F32) + q.astype(F32), *c_conv.terms)
        together(line, z_last)
        late = Back(line, z_last)
        s_qkv, s_out = finish(me, [late], [
            [(0, r, 0, blocks, up_to(r), group_col(0)), (1, r, r * blocks, blocks, up_to(r), across(half)),
             (0, r, 2 * r * blocks, blocks, up_to(r), group_col(2)), (0, r, 3 * r * blocks, blocks, up_to(r), group_col(1))]],
            [w_qkv.shape, w_attn_out.shape])
        small = small.reshape(2, ch // LANES, SMALL, LANES).transpose(0, 2, 1, 3).reshape(2, SMALL, ch)
        small = lax.dynamic_slice(small, (0, 0, at_wide * t), (2, DATASETS, t))
        g_scale, g_shift = small[0], small[1]
    else:
        def share(part, axis):
            part = lax.psum_scatter(part.astype(BF16), "wide", scatter_dimension=axis, tiled=True)
            return lax.psum(part, "rep").astype(F32)

        s_conv = lax.psum(s_conv, "rep").astype(F32)
        small = small.reshape(2, ch // LANES, SMALL, LANES).transpose(0, 2, 1, 3).reshape(2, SMALL, ch)[:, :DATASETS]
        g_scale, g_shift = share(small[0], 1), share(small[1], 1)
        s_fc2, s_fc1, s_re, s_head = share(c_two[0], 0), share(c_one[0], 0), share(c_one[1], 0), share(c_one[2], 0)
        s_out = share(c_first[1], 0)
        by_group = (c_first[0], c_last[1], c_last[0])
        s_qkv = share(jnp.concatenate([c[:, WIDTH * p:WIDTH * (p + 1)] for p in range(3) for c in by_group], 1), 0)
    g_gains = jnp.stack([jnp.sum(w_qkv.astype(F32) * s_qkv, 1), jnp.sum(w_fc1.astype(F32) * s_fc1, 1)]) / norm_gains.astype(F32)
    return (tokens_out.reshape(tokens.shape), joined, d_tokens.reshape(tokens.shape), g_gains, s_qkv, s_out, s_fc1, s_fc2,
            s_re, s_conv, s_head, g_scale, g_shift)


def solution(mesh):
    images = P(BOTH, None, None)
    slots = P(BOTH)
    rows = P("wide", None)
    cols = P(None, "wide")
    kernels = P(None, "wide", None)
    return jax.shard_map(
        shards,
        mesh=mesh,
        in_specs=(images, slots, slots, slots, cols, rows, rows, rows, rows, rows, kernels, rows, cols, cols, images, images),
        out_specs=(images, images, images, cols, rows, rows, rows, rows, rows, kernels, rows, cols, cols),
        check_vma=False,
    )
```

```python
import math

import jax
import jax.numpy as jnp
from jax import lax
from jax.experimental import pallas as pl
from jax.experimental.pallas import tpu as pltpu
from jax.sharding import PartitionSpec as P

D = 768
HEADS = 12
HD = 64
GRID = 24
COUNT = GRID * GRID
DATASETS = 10
NH = 4
GROUPS = HEADS // NH
WIDTH = NH * HD
LANES = 128
F32 = jnp.float32
BF16 = jnp.bfloat16
BOTH = ("rep", "wide")
VMEM = 60 << 20


def mm(left, right):
    return jnp.dot(left, right, preferred_element_type=F32)


def mm_tn(left, right):
    return lax.dot_general(left, right, (((0,), (0,)), ((), ())), preferred_element_type=F32)


def mm_nt(left, right):
    return lax.dot_general(left, right, (((1,), (1,)), ((), ())), preferred_element_type=F32)


def spec(shape, dtype=BF16):
    return jax.ShapeDtypeStruct(shape, dtype)


def whole(shape):
    return pl.BlockSpec(shape, lambda *_: (0,) * len(shape), pipeline_mode=pl.Buffered(1))


def params():
    return pltpu.CompilerParams(vmem_limit_bytes=VMEM)


def cost(macs, size):
    return pl.CostEstimate(flops=2 * int(macs), bytes_accessed=int(size), transcendentals=0)


def lasts(microseconds):
    return pl.CostEstimate(flops=int(microseconds * 1.15e9), bytes_accessed=0, transcendentals=0)


FLIP = {"y": 16, "x": 8, "z1": 4, "z0": 2, "c": 1}
XY, YX = ("x", "y"), ("y", "x")


def swap(value, *names):
    flip = sum(FLIP[name] for name in names)
    return lax.ppermute(value, BOTH, [(i, i ^ flip) for i in range(32)])


def bits():
    rep, wide = lax.axis_index("rep"), lax.axis_index("wide")
    return {"y": rep // 2, "x": rep % 2, "z1": wide // 4, "z0": (wide // 2) % 2, "c": wide % 2}


def bit_vector():
    b = bits()
    return jnp.stack([b[k] for k in ("y", "x", "z1", "z0", "c")]).astype(jnp.int32)


def along_z(parts):
    size = lax.axis_size("wide") // 2
    groups = [[2 * z + core for z in range(size)] for core in range(2)]
    return lax.all_to_all(parts, "wide", 0, 0, tiled=True, axis_index_groups=groups)


class Line:
    def __init__(self):
        self.tokens = []

    def after(self, value):
        return lax.optimization_barrier((value, *self.tokens))[0] if self.tokens else value

    def run(self, call, first, *rest):
        out = call(self.after(first), *rest)
        self.tokens = jax.tree.leaves(out)[-1:]
        return out

    def touch(self, *values):
        out = lax.optimization_barrier((*values, *self.tokens))
        self.tokens = list(out[:len(values)])
        return self.tokens

    def run_all(self, call, *values):
        out = call(*(lax.optimization_barrier((*values, *self.tokens))[:len(values)]))
        self.tokens = jax.tree.leaves(out)
        return out


def locate(me, order, plane, z, core):
    place = {order[0]: plane[0], order[1]: plane[1]}
    shard = ((me[2] ^ z[0]) * 2 + (me[3] ^ z[1])) * 2 + (me[4] ^ core)
    return shard, me[0] ^ place["y"], me[1] ^ place["x"]


class Gather:
    def __init__(self, piece, at, axis, swaps=False):
        self.at, self.axis, self.stage = at, axis, 0
        if swaps:
            self.terms = [piece, swap(piece, "z0"), swap(piece, "z1"), swap(piece, "z1", "z0")]
        else:
            self.terms = [along_z(jnp.broadcast_to(piece[None], (4,) + piece.shape))]
        self.relative = swaps

    def add(self, *terms):
        if self.stage == 0:
            value = jnp.stack(terms) if self.relative else terms[0]
            return [lax.slice_in_dim(value, 0, self.at, axis=self.axis + 1),
                    lax.slice_in_dim(value, self.at, value.shape[self.axis + 1], axis=self.axis + 1)]
        return [jnp.concatenate(terms[:2]), jnp.concatenate(terms[2:])]

    def send(self, out):
        one, two = out
        if self.stage == 0:
            self.terms = [one, swap(one, "x"), two, swap(two, "y")]
        else:
            self.terms = [one, swap(one, "y"), two, swap(two, "x")]
        self.stage += 1

    def starting(self, first):
        self.pieces[0] = first
        return self

    def between_cores(self, own=None):
        one, one_y, two, two_x = self.terms
        own = own or (swap(one, "c"), swap(two, "c"))
        self.pieces = [one, one_y, own[0], swap(one_y, "c"), two, two_x, own[1], swap(two_x, "c")]


PLANE = [[(s // 4, a % 2, s // 2 % 2, s % 2, a // 2) for s in range(8)] for a in range(4)]


class Assembly:
    def __init__(self, gathered, shapes, parts):
        self.gathered, self.pieces, self.shapes, self.parts = gathered, gathered.pieces, shapes, parts
        self.count = 64 * len(parts)

    def halves(self, rows, cols):
        at, axis = self.gathered.at, self.gathered.axis
        first, size = (rows, cols)[axis]
        out = []
        for low, high, shift in ((first, min(first + size, at), 0), (max(first, at), first + size, at)):
            span = (low - shift, high - low)
            out.append(None if high <= low else (span, cols, low - first, 0) if axis == 0 else (rows, span, 0, low - first))
        return out

    def start(self, me_ref, ins, outs, sem):
        started, number = [[] for _ in self.shapes], 0
        for k, rows, cols, row, col in self.parts:
            for half, order in enumerate((XY, YX)):
                for a, places in enumerate(PLANE):
                    for s, (first, second, z1, z0, core) in enumerate(places):
                        z = (z1, z0) if self.gathered.relative else (me_ref[2] ^ z1, me_ref[3] ^ z0)
                        shard, y, x = locate(me_ref, order, (first, second), z, core)
                        share = self.halves(rows, cols)[half]
                        if share is None or (row is None and (first or second)):
                            continue
                        (r0, r), (c0, n), down, across = share
                        source = ins[4 * half + a].at[s, pl.ds(r0, r), pl.ds(c0, n)]
                        if row is None:
                            place = outs[k].at[shard, pl.ds(down, r), pl.ds(across, n)]
                        else:
                            place = outs[k].at[pl.ds(pl.multiple_of(row(shard, y) + down, 16), r),
                                               pl.ds(pl.multiple_of(col(x) + across, LANES), n)]
                        copy = pltpu.make_async_copy(source, place, sem.at[number])
                        copy.start()
                        started[k].append(copy)
                        number += 1
        return started


def assemble(me, assembly):
    def body(me_ref, *refs):
        for copies in assembly.start(me_ref, refs[:8], refs[8:-1], refs[-1]):
            for copy in copies:
                copy.wait()

    return pl.pallas_call(
        body,
        grid=(1,),
        in_specs=[pl.BlockSpec(memory_space=pltpu.SMEM)] + [pl.BlockSpec(memory_space=pl.ANY)] * 8,
        out_specs=[whole(s) for s in assembly.shapes],
        out_shape=[spec(s) for s in assembly.shapes],
        scratch_shapes=[pltpu.SemaphoreType.DMA((assembly.count,))],
        compiler_params=params(),
        cost_estimate=lasts(0),
        name="assemble",
    )(me, *assembly.pieces)


class Weights:
    def __init__(self, weights):
        self.assembly = weights if isinstance(weights, Assembly) else None
        if self.assembly:
            shapes = self.assembly.shapes
            self.ins, self.in_specs = self.assembly.pieces, [pl.BlockSpec(memory_space=pl.ANY)] * 8
            self.outs, self.out_specs = [spec(s) for s in shapes], [pl.BlockSpec(memory_space=pl.ANY)] * len(shapes)
            self.scratch = [pltpu.VMEM(s, BF16) for s in shapes] + [
                pltpu.SemaphoreType.DMA((self.assembly.count,)), pltpu.SemaphoreType.DMA((len(shapes),))]
        else:
            self.ins, self.in_specs = list(weights), [whole(w.shape) for w in weights]
            self.outs, self.out_specs, self.scratch = [], [], []

    def bind(self, me_ref, ins, outs, scratch):
        self.me_ref, self.in_refs, self.out_refs, self.held = me_ref, ins, outs, scratch
        self.refs = scratch[:len(outs)] if self.assembly else ins

    def begin(self, *works):
        if not self.assembly:
            for work in works:
                work()
            return
        copies = self.assembly.start(self.me_ref, self.in_refs, self.refs, self.held[-2])
        for k, copy_list in enumerate(copies):
            for copy in copy_list:
                copy.wait()
            self.back(k).start()
            if k < len(works):
                works[k]()

    def back(self, k):
        return pltpu.make_async_copy(self.refs[k], self.out_refs[k], self.held[-1].at[k])

    def end(self):
        for k in range(len(self.out_refs)):
            self.back(k).wait()


def together(line, *jobs):
    counts = [len(job.terms) for job in jobs]

    def call(*terms):
        out = []
        for job, count in zip(jobs, counts):
            out.append(job.add(*terms[:count]))
            terms = terms[count:]
        return out

    for job, out in zip(jobs, line.run_all(call, *[term for job in jobs for term in job.terms])):
        job.send(out)


class Chunk:
    def __init__(self, line, keep, send, split):
        self.split, self.stage = split, 0
        self.terms = [keep, swap(line.after(send), "c")]

    def add(self, *terms):
        if self.stage == 0:
            parts = [(slots, rows) for rows in (slice(0, self.split), slice(self.split, None)) for slots in (slice(0, 8), slice(8, 16))]
            return [terms[0][part] + terms[1][part] for part in parts]
        return [terms[i][part] + terms[i + 1][part] for i in (0, 2) for part in (slice(0, 4), slice(4, 8))]

    def send(self, out):
        one, two = ("x", "y") if self.stage == 0 else ("y", "x")
        self.terms = [out[0], swap(out[1], one), out[2], swap(out[3], two)]
        self.stage += 1


class Single(Chunk):
    def __init__(self, line, keep, send, order):
        super().__init__(line, keep, send, None)
        self.order = order

    def add(self, *terms):
        if self.stage == 2:
            return [terms[0] + terms[1]]
        half = terms[0].shape[0] // 2
        return [terms[0][part] + terms[1][part] for part in (slice(0, half), slice(half, None))]

    def send(self, out):
        self.terms = out if self.stage == 2 else [out[0], swap(out[1], self.order[self.stage])]
        self.stage += 1


class Along:
    def __init__(self, *chunks):
        self.stage, self.terms = 0, [term for chunk in chunks for term in chunk.terms]
        self.done = [len(chunk.terms) == 1 for chunk in chunks for _ in range(max(1, len(chunk.terms) // 2))]

    def add(self, *terms):
        if self.stage:
            return [sum(terms[0][i].astype(F32) for i in range(4)).astype(BF16)]
        terms = list(terms)
        sums = [terms.pop(0) if done else terms.pop(0) + terms.pop(0) for done in self.done]
        return [jnp.concatenate(sums, 1)]

    def send(self, out):
        if self.stage:
            self.total = out[0]
        else:
            self.terms = [along_z(out[0])]
        self.stage += 1


class Back:
    def __init__(self, line, *alongs):
        self.rows = [along.total.shape[0] for along in alongs]
        if len(alongs) > 1:
            (total,) = line.run_all(lambda *parts: [jnp.concatenate(parts)], *[along.total for along in alongs])
        else:
            total = alongs[0].total
        self.terms = [total, swap(total, "x"), swap(total, "y"), swap(total, "x", "y")]


class Whole:
    def __init__(self, value):
        self.terms = [value, swap(value, "x")]

    def add(self, *terms):
        return [terms[0] + terms[1]]

    def send(self, out):
        self.terms = [out[0], swap(out[0], "y")]


def finish(me, backs, places, shapes):
    ins = [t for back in backs for t in back.terms]

    def body(me_ref, *refs):
        outs = refs[len(ins):len(ins) + len(shapes)]
        held = refs[len(ins) + len(shapes):]
        for c, parts in enumerate(places):
            for q in range(4):
                held[c][q] = refs[4 * c + q][...]
            for y in range(2):
                for x in range(2):
                    at = 2 * (me_ref[0] ^ y) + (me_ref[1] ^ x)
                    for k, r, r0, blocks, row, col in parts:
                        for b in range(blocks):
                            at_row = row(y) + (r * x if shapes[k][1] == LANES else 0)
                            outs[k][at_row:at_row + r, col(x, b):col(x, b) + LANES] = (
                                held[c][at, r0 + b * r:r0 + (b + 1) * r, :].astype(F32))

    return pl.pallas_call(
        body,
        grid=(1,),
        in_specs=[pl.BlockSpec(memory_space=pltpu.SMEM)] + [whole(a.shape) for a in ins],
        out_specs=[whole(s) for s in shapes],
        out_shape=[spec(s, F32) for s in shapes],
        scratch_shapes=[pltpu.VMEM((4,) + back.terms[0].shape, BF16) for back in backs],
        compiler_params=params(),
        cost_estimate=lasts(3),
        name="finish",
    )(me, *ins)


PLAIN = "plain"
ALL_XY, ALL_YX = 1 << 30, 0


TABLE = 64


class Sink:
    def __init__(self, shapes, split, table=False):
        self.shapes, self.split, self.table = shapes, split, table
        rows = sum(k // 16 * (n // 2 // LANES) for k, n in shapes) + (TABLE // 4 if table else 0)
        if split == PLAIN:
            self.outs, self.scratch = [spec(s) for s in shapes], []
        else:
            self.outs = [spec((16, rows, LANES))] * 2
            self.scratch = [pltpu.VMEM((2, k, n // 2), BF16) for k, n in shapes]
            self.scratch += [pltpu.VMEM((TABLE, LANES), BF16)] if table else []

    def out_specs(self):
        return [whole(o.shape) for o in self.outs]

    def put(self, outs, held, k, rows, value):
        value = value.astype(BF16)
        half = self.shapes[k][1] // 2
        if self.split == PLAIN:
            outs[k][rows, :] = value
        else:
            held[k][0, rows, :] = value[:, :half]
            held[k][1, rows, :] = value[:, half:]

    def deliver(self, me_ref, outs, held):
        if self.split == PLAIN:
            return
        for core in range(2):
            for s in range(16):
                z = (me_ref[2] ^ (s // 2 % 2), me_ref[3] ^ (s % 2))
                places = [locate(me_ref, order, (s // 8, s // 4 % 2), z, core) for order in (XY, YX)]
                at = 0
                for k, (rows, cols) in enumerate(self.shapes):
                    r = rows // 16
                    size = r // 2 if r > 144 and r % 32 == 0 else r
                    for b in range(cols // 2 // LANES):
                        for part in range(0, r, size):
                            shard, y, x = places[0 if at < self.split else 1]
                            start = pl.multiple_of((shard * 2 + y) * r + part, 16)
                            outs[core][s, at:at + size, :] = held[k][x, pl.ds(start, size), b * LANES:(b + 1) * LANES]
                            at += size
                if self.table:
                    r = TABLE // 4
                    _, y, x = places[0 if at < self.split else 1]
                    outs[core][s, at:at + r, :] = held[-1][pl.ds(pl.multiple_of((2 * y + x) * r, 16), r), :]


def gelu_pair(values):
    cdf = 0.5 + 0.5 * lax.erf(values * 0.7071067811865476)
    pdf = 0.3989422804014327 * jnp.exp(-0.5 * values * values)
    return values * cdf, cdf + values * pdf


def gelu(values):
    return values * (0.5 + 0.5 * lax.erf(values * 0.7071067811865476))


def normalize(values):
    centred = values - jnp.mean(values, -1, keepdims=True)
    recip = lax.rsqrt(jnp.mean(centred * centred, -1, keepdims=True) + 1e-06)
    return centred * recip, recip


def norm_transpose(grad_normed, normed, recip):
    return recip * (
        grad_normed
        - jnp.mean(grad_normed, -1, keepdims=True)
        - normed * jnp.mean(grad_normed * normed, -1, keepdims=True)
    )


SMALL = 16


def prepare(me, w_qkv, w_out, w_fc1, w_fc2, w_re, w_head, gains, scales, shifts):
    ff, ch = w_fc1.shape[1], w_re.shape[1]
    half = w_qkv.shape[0] // 2
    rows_two, rows_head = w_fc2.shape[0] // 2, w_head.shape[0] // 2
    n = w_qkv.shape[1] // 2

    def body(me_ref, qkv_ref, out_ref, fc1_ref, fc2_ref, re_ref, head_ref, gains_ref, scales_ref, shifts_ref,
             zero_ref, one_ref, two_ref):
        zero_ref[:, n:] = jnp.zeros((half, LANES), BF16)
        zero_ref[0:DATASETS, n:n + scales.shape[1]] = scales_ref[...]
        zero_ref[SMALL:SMALL + DATASETS, n:n + shifts.shape[1]] = shifts_ref[...]
        zero_ref[2 * SMALL:2 * SMALL + 2, n:n + gains.shape[1]] = gains_ref[...]
        rows = pl.ds(pl.multiple_of(me_ref[0] * half, 16), half)
        rows_of_two = pl.ds(pl.multiple_of(me_ref[0] * rows_two, 16), rows_two)
        rows_of_head = pl.ds(pl.multiple_of(me_ref[0] * rows_head, 16), rows_head)
        for x in range(2):
            @pl.when(me_ref[1] == x)
            def _():
                zero_ref[:, :n] = qkv_ref[rows, n * x:n * (x + 1)]
                one_ref[:, :D // 2] = out_ref[rows, D // 2 * x:D // 2 * (x + 1)]
                at = D // 2 + ff // 2
                one_ref[:, D // 2:at] = fc1_ref[rows, ff // 2 * x:ff // 2 * (x + 1)]
                one_ref[:, at:at + ch // 2] = re_ref[rows, ch // 2 * x:ch // 2 * (x + 1)]
                one_ref[0:rows_head, at + ch // 2:] = head_ref[rows_of_head, ch // 2 * x:ch // 2 * (x + 1)]
                two_ref[...] = fc2_ref[rows_of_two, D // 2 * x:D // 2 * (x + 1)]
        one_ref[rows_head:, D // 2 + ff // 2 + ch // 2:] = jnp.zeros((half - rows_head, LANES), BF16)

    ins = (w_qkv, w_out, w_fc1, w_fc2, w_re, w_head, gains, scales, shifts)
    outs = [spec((half, n + LANES)), spec((half, D // 2 + ff // 2 + ch // 2 + LANES)), spec((rows_two, D // 2))]
    return pl.pallas_call(
        body,
        grid=(1,),
        in_specs=[pl.BlockSpec(memory_space=pltpu.SMEM)] + [whole(a.shape) for a in ins],
        out_specs=[whole(o.shape) for o in outs],
        out_shape=outs,
        compiler_params=params(),
        cost_estimate=lasts(2.4),
        name="prepare",
    )(me, *ins)


def norm_body(x_ref, out_ref):
    out_ref[...] = normalize(x_ref[...].astype(F32))[0]


def norm(x):
    rows = x.shape[0]
    block = pl.BlockSpec((rows // 4, D), lambda i: (i, 0))
    return pl.pallas_call(
        norm_body,
        grid=(4,),
        in_specs=[block],
        out_specs=block,
        out_shape=spec((rows, D), F32),
        compiler_params=params(),
        cost_estimate=lasts(4.4),
        name="norm",
    )(x)


def bilinear(targets, sources, first):
    size = 2 * GRID
    step = (GRID - 1) / (size - 1)

    def hat(target, source):
        return jnp.maximum(1.0 - jnp.abs(target.astype(F32) * step - source.astype(F32)), 0.0)

    target = lax.broadcasted_iota(jnp.int32, targets, targets.index(max(targets))) + first
    source = lax.broadcasted_iota(jnp.int32, sources, sources.index(max(sources)))
    return (hat(target // size, source // GRID) * hat(target % size, source % GRID)).astype(BF16)


def is_live(count_ref, image):
    return (image < count_ref[0]).astype(F32)


def down_body(dj_ref, count_ref, flag_ref, down_ref, gshift_ref):
    step, images, size = pl.program_id(0), dj_ref.shape[0], dj_ref.shape[1]
    table = bilinear((1, size), (COUNT, 1), step * size)
    for i in range(images):
        part = mm(table, dj_ref[i])
        sums = jnp.sum(dj_ref[i].astype(F32), 0, keepdims=True)

        @pl.when(step == 0)
        def _():
            down_ref[i] = part
            gshift_ref[i] = sums

        @pl.when(step > 0)
        def _():
            down_ref[i] += part
            gshift_ref[i] += sums

        @pl.when(step == pl.num_programs(0) - 1)
        def _():
            down_ref[i] = down_ref[i] * is_live(count_ref, i)
            gshift_ref[i] = gshift_ref[i] * (is_live(count_ref, i) * flag_ref[i].astype(F32))


def bring_down(dj, live_count, flag):
    images, count, ch = dj.shape
    one = whole((images, 1, ch))
    return pl.pallas_call(
        down_body,
        grid=(4,),
        in_specs=[pl.BlockSpec((images, count // 4, ch), lambda i: (0, i, 0))] + [pl.BlockSpec(memory_space=pltpu.SMEM)] * 2,
        out_specs=[whole((images, COUNT, ch)), one],
        out_shape=[spec((images, COUNT, ch), F32), spec((images, 1, ch), F32)],
        compiler_params=params(),
        cost_estimate=lasts(8.9),
        name="bring_down",
    )(dj, live_count, flag)


def tables_body(small_ref, id_ref, flag_ref, scale_ref, shift_ref):
    shards, rows = small_ref.shape[0], SMALL
    ch = scale_ref.shape[2]
    width = ch // shards
    whole_tables = [jnp.zeros((rows, ch), F32), jnp.zeros((rows, ch), F32)]
    lane = lax.broadcasted_iota(jnp.int32, (LANES, ch), 0)
    col = lax.broadcasted_iota(jnp.int32, (LANES, ch), 1)
    for w in range(shards):
        place = ((col == lane + width * w) & (lane < width)).astype(BF16)
        for k in range(2):
            whole_tables[k] = whole_tables[k] + mm(small_ref[w, rows * k:rows * (k + 1), :], place)
    row = lax.broadcasted_iota(jnp.int32, (rows, 1), 0)
    for i in range(scale_ref.shape[0]):
        mask = row == id_ref[i]
        scale_ref[i] = jnp.sum(jnp.where(mask, whole_tables[0], 0.0), 0, keepdims=True)
        shift_ref[i] = jnp.sum(jnp.where(mask, whole_tables[1], 0.0), 0, keepdims=True) * flag_ref[i].astype(F32)


def tables(small, ids, flags, ch):
    out = spec((ids.shape[0], 1, ch), F32)
    return pl.pallas_call(
        tables_body,
        grid=(1,),
        in_specs=[whole(small.shape)] + [pl.BlockSpec(memory_space=pltpu.SMEM)] * 2,
        out_specs=[whole(out.shape)] * 2,
        out_shape=[out] * 2,
        compiler_params=params(),
        cost_estimate=lasts(2),
        name="tables",
    )(small, ids, flags)


def attention_body(a1_ref, wq_ref, wk_ref, wv_ref, qkv_ref, o_ref, e_ref, r_ref):
    for i, ref in enumerate((wq_ref, wk_ref, wv_ref)):
        qkv_ref[:, WIDTH * i:WIDTH * (i + 1)] = mm(a1_ref[...], ref[...]).astype(BF16)
    def part(kind, h):
        return slice(WIDTH * kind + HD * h, WIDTH * kind + HD * (h + 1))

    def scores(h):
        return mm_nt(qkv_ref[:, part(1, h)], qkv_ref[:, part(0, h)] * jnp.asarray(0.125, BF16))

    following = scores(0)
    for h in range(NH):
        s, following = following, scores(h + 1) if h + 1 < NH else None
        e = jnp.exp(s - jnp.max(s, 0, keepdims=True))
        r = 1.0 / jnp.sum(e, 0, keepdims=True)
        low = e.astype(BF16)
        e_ref[h] = low
        o_ref[:, HD * h:HD * (h + 1)] = (mm_tn(qkv_ref[:, part(2, h)], low) * r).T.astype(BF16)
        r_ref[0, h:h + 1, :] = r


def group_specs():
    def cols(n):
        return pl.BlockSpec((COUNT, n), lambda i: (i, 0))

    return cols, pl.BlockSpec((NH, COUNT, COUNT), lambda i: (i, 0, 0)), pl.BlockSpec((1, NH, COUNT), lambda i: (i, 0, 0))


def group_columns(group):
    return [pl.BlockSpec((D, WIDTH), lambda i, p=p: (0, GROUPS * p + group), pipeline_mode=pl.Buffered(1)) for p in range(3)]


def attention(a1, w, group):
    rows = a1.shape[0]
    images = rows // COUNT
    cols, probs, sums = group_specs()
    return pl.pallas_call(
        attention_body,
        grid=(images,),
        in_specs=[cols(D)] + group_columns(group),
        out_specs=[cols(3 * WIDTH), cols(WIDTH), probs, sums],
        out_shape=[spec((rows, 3 * WIDTH)), spec((rows, WIDTH)), spec((images * NH, COUNT, COUNT)),
                   spec((images, NH, COUNT), F32)],
        compiler_params=params(),
        cost_estimate=lasts(11),
        name="attention",
    )(a1, w, w, w)


def attention_back(da, me, group, qkv, o, e, r, a1, w_out, extra, split):
    rows = da.shape[0]
    images = rows // COUNT
    cols, probs, sums = group_specs()
    shape = (D, 3 * WIDTH)
    sink = Sink([shape], PLAIN) if extra is None else Sink([shape, (D, D)], split)
    n_out = len(sink.outs)
    extra = list(extra) if isinstance(extra, (list, tuple)) else [] if extra is None else [extra]

    def body(da_ref, me_ref, qkv_ref, o_ref, e_ref, r_ref, a1_ref, wout_ref, *refs):
        more, refs = refs[:len(extra)], refs[len(extra):]
        grads, dqkv, total, held = refs[:n_out], refs[n_out], refs[n_out + 1], refs[n_out + 2:]
        if len(extra) > 1:
            total_out, held = held[0], held[1:]
        step = pl.program_id(0)
        ones = jnp.ones((8, HD), BF16)
        do_all = mm_nt(da_ref[...], wout_ref[...]).astype(BF16)
        for h in range(NH):
            q, k, v = (slice(WIDTH * i + HD * h, WIDTH * i + HD * (h + 1)) for i in range(3))
            do = do_all[:, HD * h:HD * (h + 1)]
            delta = mm_nt(ones, (do.astype(F32) * o_ref[:, HD * h:HD * (h + 1)].astype(F32)).astype(BF16))[0:1]
            prob = e_ref[h].astype(F32) * r_ref[0, h:h + 1, :]
            dp = mm_nt(qkv_ref[:, v], do)
            ds = (prob * (dp - delta)).astype(BF16)
            dqkv[:, v] = mm(prob.astype(BF16), do).astype(BF16)
            dqkv[:, k] = (mm(ds, qkv_ref[:, q]) * 0.125).astype(BF16)
            dqkv[:, q] = (mm_tn(ds, qkv_ref[:, k]) * 0.125).astype(BF16)
        g = mm_tn(a1_ref[...], dqkv[...])
        g_out = [mm_tn(ref[...], da_ref[...]) for ref in more] if len(extra) > 1 else []

        @pl.when(step == 0)
        def _():
            total[...] = g
            for i, part in enumerate(g_out):
                total_out[WIDTH * i:WIDTH * (i + 1)] = part

        @pl.when(step > 0)
        def _():
            total[...] += g
            for i, part in enumerate(g_out):
                total_out[WIDTH * i:WIDTH * (i + 1)] += part

        @pl.when(step == images - 1)
        def _():
            sink.put(grads, held, 0, slice(0, D), total[...])
            if len(extra) > 1:
                sink.put(grads, held, 1, slice(0, D), total_out[...])
            elif extra:
                sink.put(grads, held, 1, slice(0, D), more[0][...])
            sink.deliver(me_ref, grads, held)

    more_specs = [cols(WIDTH)] * len(extra) if len(extra) > 1 else [whole(a.shape) for a in extra]
    out = pl.pallas_call(
        body,
        grid=(images,),
        in_specs=[cols(D), pl.BlockSpec(memory_space=pltpu.SMEM), cols(3 * WIDTH), cols(WIDTH), probs, sums, cols(D),
                  pl.BlockSpec((WIDTH, D), lambda i: (group, 0))] + more_specs,
        out_specs=sink.out_specs() + [cols(3 * WIDTH)],
        out_shape=sink.outs + [spec((rows, 3 * WIDTH))],
        scratch_shapes=[pltpu.VMEM(shape, F32)] + ([pltpu.VMEM((D, D), F32)] if len(extra) > 1 else []) + sink.scratch,
        compiler_params=params(),
        cost_estimate=lasts(18),
        name="attention_back",
    )(da, me, qkv, o, e, r, a1, w_out, *extra)
    return out[:n_out], out[n_out]


def input_back(dqkv, w, dx2, x, gains):
    rows = x.shape[0]
    block = rows // 4

    def body(*refs):
        (w_ref, dx2_ref, x_ref, gains_ref), out_ref = refs[GROUPS:-1], refs[-1]
        da1 = jnp.zeros((block, D), F32)
        for i, ref in enumerate(refs[:GROUPS]):
            for p in range(3):
                at = D * p + WIDTH * i
                da1 = da1 + mm_nt(ref[:, WIDTH * p:WIDTH * (p + 1)], w_ref[:, at:at + WIDTH])
        n1, rs1 = normalize(x_ref[...].astype(F32))
        out_ref[...] = (dx2_ref[...].astype(F32) + norm_transpose(da1 * gains_ref[0:1], n1, rs1)).astype(BF16)

    def cols(n):
        return pl.BlockSpec((block, n), lambda i: (i, 0))

    return pl.pallas_call(
        body,
        grid=(4,),
        in_specs=[cols(3 * WIDTH)] * GROUPS + [whole(w.shape), cols(D), cols(D), whole(gains.shape)],
        out_specs=cols(D),
        out_shape=spec((rows, D)),
        compiler_params=params(),
        cost_estimate=lasts(9),
        name="input_back",
    )(*dqkv, w, dx2, x, gains)


def mlp_up(x, heads_out, weights, me, gains, block=1024):
    rows = x.shape[0]
    weights = Weights(weights)
    ff = (weights.assembly.shapes[1] if weights.assembly else weights.ins[1].shape)[1]
    n_in, n_out = len(weights.ins), len(weights.outs)
    chunk = rows // 4
    last = ff // block - 1

    def body(me_ref, x_ref, o0_ref, o1_ref, o2_ref, gains_ref, *refs):
        x2_ref, a2_ref, u_ref = refs[n_in:n_in + 3]
        weights.bind(me_ref, refs[:n_in], refs[n_in + 3:n_in + 3 + n_out], refs[n_in + 3 + n_out:])
        wout_ref, w1_ref = weights.refs[:2]
        step = pl.program_id(0)

        def project():
            for p in range(0, rows, chunk):
                at = slice(p, p + chunk)
                x2 = x_ref[at].astype(F32)
                for i, ref in enumerate((o0_ref, o1_ref, o2_ref)):
                    x2 = x2 + mm(ref[at], wout_ref[WIDTH * i:WIDTH * (i + 1), :])
                x2_ref[at] = x2.astype(BF16)
                a2_ref[at] = (normalize(x2)[0] * gains_ref[1:2]).astype(BF16)

        @pl.when(step == 0)
        def _():
            weights.begin(project)

        u_ref[...] = mm(a2_ref[...], w1_ref[:, pl.ds(pl.multiple_of(step * block, LANES), block)]).astype(BF16)

        @pl.when(step == last)
        def _():
            weights.end()

    full, cols = whole((rows, D)), pl.BlockSpec((rows, block), lambda i: (0, i))
    out = pl.pallas_call(
        body,
        grid=(ff // block,),
        in_specs=[pl.BlockSpec(memory_space=pltpu.SMEM), full] + [whole((rows, WIDTH))] * 3 + [whole((2, D))] + weights.in_specs,
        out_specs=[full, full, cols] + weights.out_specs,
        out_shape=[spec((rows, D)), spec((rows, D)), spec((rows, ff))] + weights.outs,
        scratch_shapes=weights.scratch,
        compiler_params=params(),
        cost_estimate=lasts(17),
        name="mlp_up",
    )(me, x, *heads_out, gains, *weights.ins)
    return out[3:], out[:3]


def mlp_down(u, weights, me, x2, live_count):
    rows, ff = u.shape
    weights = Weights(weights)
    n_in, n_out = len(weights.ins), len(weights.outs)
    block = rows // 4

    def body(me_ref, count_ref, u_ref, x2_ref, *refs):
        x3b_ref, out_ref = refs[n_in:n_in + 2]
        weights.bind(me_ref, refs[:n_in], refs[n_in + 2:n_in + 2 + n_out], refs[n_in + 2 + n_out:])
        (w2_ref,) = weights.refs
        step = pl.program_id(0)

        @pl.when(step == 0)
        def _():
            weights.begin()

        x3 = x2_ref[...].astype(F32)
        size = ff // 6
        for k in range(6):
            at = slice(size * k, size * (k + 1))
            x3 = x3 + mm(gelu(u_ref[:, at].astype(F32)).astype(BF16), w2_ref[at, :])
        x3b_ref[...] = x3.astype(BF16)
        image = step * block // COUNT
        out_ref[...] = (x3 * is_live(count_ref, image)).astype(BF16)

        @pl.when(step == 3)
        def _():
            weights.end()

    at = pl.BlockSpec((block, D), lambda i: (i, 0))
    out = pl.pallas_call(
        body,
        grid=(4,),
        in_specs=[pl.BlockSpec(memory_space=pltpu.SMEM)] * 2 + [pl.BlockSpec((block, ff), lambda i: (i, 0)), at] + weights.in_specs,
        out_specs=[at, at] + weights.out_specs,
        out_shape=[spec((rows, D))] * 2 + weights.outs,
        scratch_shapes=weights.scratch,
        compiler_params=params(),
        cost_estimate=lasts(15),
        name="mlp_down",
    )(me, live_count, u, x2, *weights.ins)
    return out[2:], out[:2]


def spread(value, out_ref, rows, sign):
    count, ch = value.shape
    at = lax.broadcasted_iota(jnp.int32, (count, 1), 0)
    col = at % GRID
    gap = jnp.zeros((GRID, ch), F32)
    for dx in (-1, 0, 1):
        step = sign * dx
        moved = value
        if step:
            moved = pltpu.roll(value, (-step) % count, 0)
            moved = jnp.where((col + step >= 0) & (col + step < GRID), moved, 0.0)
        for dy in (-1, 0, 1):
            block = 3 * (dy + 1) + dx + 1
            if sign * dy == 1:
                part = jnp.concatenate([moved[GRID:], gap], 0)
            elif sign * dy == -1:
                part = jnp.concatenate([gap, moved[:-GRID]], 0)
            else:
                part = moved
            out_ref[rows, block * ch:(block + 1) * ch] = part.astype(BF16)


def units_body(x_ref, wre_ref, w_ref, t1_ref, s1_ref, t2_ref, s2_ref, zb_ref, cols, z_ref):
    unit = pl.program_id(0)
    images = [slice(COUNT * i, COUNT * (i + 1)) for i in range(x_ref.shape[0] // COUNT)]

    @pl.when(unit == 0)
    def _():
        z_ref[...] = mm(x_ref[...], wre_ref[...])

    inner = []
    for at in images:
        act, slope = gelu_pair(z_ref[at])
        t1_ref[0, at], s1_ref[0, at] = act.astype(BF16), slope.astype(BF16)
        spread(act, cols, at, 1)
        inner.append(mm(cols[at], w_ref[0]))
    for at, value in zip(images, inner):
        act, slope = gelu_pair(value)
        t2_ref[0, at], s2_ref[0, at] = act.astype(BF16), slope.astype(BF16)
        spread(act, cols, at, 1)
        z_ref[at] += mm(cols[at], w_ref[1])

    @pl.when(unit == 1)
    def _():
        zb_ref[...] = z_ref[...].astype(BF16)


def units(x3b, w_re, w_conv):
    rows, ch = x3b.shape[0], w_re.shape[1]
    acts = pl.BlockSpec((1, rows, ch), lambda i: (i, 0, 0))
    return pl.pallas_call(
        units_body,
        grid=(2,),
        in_specs=[whole(x3b.shape), whole(w_re.shape), pl.BlockSpec((2,) + w_conv.shape[1:], lambda i: (i, 0, 0))],
        out_specs=[acts] * 4 + [whole((rows, ch))],
        out_shape=[spec((2, rows, ch))] * 4 + [spec((rows, ch))],
        scratch_shapes=[pltpu.VMEM((rows, 9 * ch), BF16), pltpu.VMEM((rows, ch), F32)],
        compiler_params=params(),
        cost_estimate=lasts(18),
        name="units",
    )(x3b, w_re, w_conv)


def units_back_body(down_ref, scale_ref, gshift_ref, id_ref, z_ref, x3b_ref, gt_ref, count_ref, whead_ref, wre_ref,
                    w_ref, t1_ref, s1_ref, t2_ref, s2_ref,
                    gw_ref, ghead_ref, gre_ref, dm_ref, table_ref, moved_two, turned_two, dz_ref):
    images, _, ch = down_ref.shape

    @pl.when(pl.program_id(0) == 0)
    def _():
        dq = jnp.concatenate([(down_ref[i] * scale_ref[i]).astype(BF16) for i in range(images)], 0)
        ghead_ref[...] = mm_tn(z_ref[...], dq).astype(BF16)
        dz_ref[...] = mm_nt(dq, whead_ref[...])
        table_ref[...] = jnp.zeros_like(table_ref)
        for i in range(images):
            head = mm(z_ref[COUNT * i:COUNT * (i + 1)], whead_ref[...])
            sums = (jnp.sum(head * down_ref[i], 0, keepdims=True), gshift_ref[i])
            for b in range(2 * ch // LANES):
                at, row = SMALL * b, sums[b // (ch // LANES)]
                cols = slice(LANES * (b % (ch // LANES)), LANES * (b % (ch // LANES) + 1))
                hot = lax.broadcasted_iota(jnp.int32, (SMALL, 1), 0) == id_ref[i]
                table_ref[at:at + SMALL] += jnp.where(hot, row[:, cols], 0.0)

    places = [slice(COUNT * i, COUNT * (i + 1)) for i in range(images)]

    def back(index, grads, act_ref, slope_ref):
        moved, turned = moved_two.at[index], turned_two.at[index]
        for b in range(9):
            at = slice(ch * b, ch * (b + 1))
            turned[:, at] = w_ref[index, at, :]
        out = []
        for at, grad in zip(places, grads):
            spread(grad, moved, at, -1)
            out.append(mm_nt(moved[at, :], turned[...]) * slope_ref[0, at].astype(F32))
        g = mm_tn(act_ref[0], moved[...])
        for b in range(9):
            at = slice(ch * b, ch * (b + 1))
            gw_ref[index, at, :] = g[:, at].astype(BF16)
        return out

    grads = back(1, [dz_ref[at] for at in places], t2_ref, s2_ref)
    for at, grad in zip(places, back(0, grads, t1_ref, s1_ref)):
        dz_ref[at] += grad

    @pl.when(pl.program_id(0) == 1)
    def _():
        dr = dz_ref[...].astype(BF16)
        gre_ref[...] = mm_tn(x3b_ref[...], dr).astype(BF16)
        dx3 = mm_nt(dr, wre_ref[...])
        for i in range(images):
            at = slice(COUNT * i, COUNT * (i + 1))
            part = gt_ref[at].astype(F32) * is_live(count_ref, i) + dx3[at]
            dm_ref[at] = part.astype(BF16)


def units_back(down, scale, gshift, ids, z, x3b, gt, live_count, w_head, w_conv, w_re, t1, s1, t2, s2):
    rows, ch = z.shape
    ins = (down, scale, gshift, ids, z, x3b, gt, live_count, w_head, w_re)
    outs = [spec(w_conv.shape), spec(w_head.shape), spec(w_re.shape), spec((rows, D)),
            spec((2 * ch // LANES * SMALL, LANES), F32)]
    kernels = pl.BlockSpec((2,) + w_conv.shape[1:], lambda i: (1 - i, 0, 0))
    act = pl.BlockSpec((1, rows, ch), lambda i: (1 - i, 0, 0))
    return pl.pallas_call(
        units_back_body,
        grid=(2,),
        in_specs=[pl.BlockSpec(memory_space=pltpu.SMEM) if a is live_count or a is ids else whole(a.shape) for a in ins] + [kernels] + [act] * 4,
        out_specs=[kernels] + [whole(a.shape) for a in outs[1:]],
        out_shape=outs,
        scratch_shapes=[pltpu.VMEM((2, rows, 9 * ch), BF16), pltpu.VMEM((2, ch, 9 * ch), BF16), pltpu.VMEM((rows, ch), F32)],
        compiler_params=params(),
        cost_estimate=lasts(30),
        name="units_back",
    )(*ins, w_conv, t1, s1, t2, s2)


def hidden_back(dm, me, u, w2, split, block=512):
    rows, ff = u.shape
    sink = Sink([(ff, D)], split)
    n_out = len(sink.outs)

    def body(dm_ref, me_ref, u_ref, w2_ref, *refs):
        grads, du_ref, held = refs[:n_out], refs[n_out], refs[n_out + 1:]
        step = pl.program_id(0)
        at = pl.ds(pl.multiple_of(step * block, block), block)
        act, slope = gelu_pair(u_ref[...].astype(F32))
        sink.put(grads, held, 0, at, mm_tn(act.astype(BF16), dm_ref[...]))
        du_ref[...] = (mm_nt(dm_ref[...], w2_ref[...]) * slope).astype(BF16)

        @pl.when(step == pl.num_programs(0) - 1)
        def _():
            sink.deliver(me_ref, grads, held)

    cols = pl.BlockSpec((rows, block), lambda i: (0, i))
    out = pl.pallas_call(
        body,
        grid=(ff // block,),
        in_specs=[whole((rows, D)), pl.BlockSpec(memory_space=pltpu.SMEM), cols, pl.BlockSpec((block, D), lambda i: (i, 0))],
        out_specs=sink.out_specs() + [cols],
        out_shape=sink.outs + [spec((rows, ff))],
        scratch_shapes=sink.scratch,
        compiler_params=params(),
        cost_estimate=lasts(20),
        name="hidden_back",
    )(dm, me, u, w2)
    return out[:n_out], out[n_out]


def first_weight_back(du, me, a2, g_re, g_head, table, split, block=512):
    rows, ff = du.shape
    sink = Sink([(D, ff), g_re.shape, g_head.shape], split, True)
    n_out = len(sink.outs)
    half = ff // 2 // block

    def body(du_ref, me_ref, a2_ref, gre_ref, ghead_ref, table_ref, *refs):
        step = pl.program_id(0)
        grads, held = refs[:n_out], refs[n_out:]
        g = mm_tn(a2_ref[...], du_ref[...]).astype(BF16)
        cols = pl.ds(pl.multiple_of(step % half * block, block), block)
        if split == PLAIN:
            grads[0][:, pl.ds(pl.multiple_of(step * block, block), block)] = g
        else:
            held[0][step // half, :, cols] = g

        @pl.when(step == pl.num_programs(0) - 1)
        def _():
            sink.put(grads, held, 1, slice(0, g_re.shape[0]), gre_ref[...])
            sink.put(grads, held, 2, slice(0, g_head.shape[0]), ghead_ref[...])
            if split != PLAIN:
                held[-1][...] = table_ref[...].astype(BF16)
            sink.deliver(me_ref, grads, held)

    return pl.pallas_call(
        body,
        grid=(ff // block,),
        in_specs=[pl.BlockSpec((rows, block), lambda i: (0, i)), pl.BlockSpec(memory_space=pltpu.SMEM), whole((rows, D)),
                  whole(g_re.shape), whole(g_head.shape), whole(table.shape)],
        out_specs=sink.out_specs(),
        out_shape=sink.outs,
        scratch_shapes=sink.scratch,
        compiler_params=params(),
        cost_estimate=lasts(13),
        name="first_weight_back",
    )(du, me, a2, g_re, g_head, table)


def mlp_back_body(du_ref, w1_ref, dm_ref, x2_ref, gains_ref, da_ref):
    n2, rs2 = normalize(x2_ref[...].astype(F32))
    da2 = mm_nt(du_ref[...], w1_ref[...])
    da_ref[...] = (dm_ref[...].astype(F32) + norm_transpose(da2 * gains_ref[1:2], n2, rs2)).astype(BF16)


def mlp_back(du, w1, dm, x2, gains):
    rows, ff = du.shape
    block = rows // 4

    def cols(n):
        return pl.BlockSpec((block, n), lambda i: (i, 0))

    return pl.pallas_call(
        mlp_back_body,
        grid=(4,),
        in_specs=[cols(ff), whole(w1.shape), cols(D), cols(D), whole((2, D))],
        out_specs=cols(D),
        out_shape=spec((rows, D)),
        compiler_params=params(),
        cost_estimate=lasts(13),
        name="mlp_back",
    )(du, w1, dm, x2, gains)


def join_body(z_ref, w_ref, scale_ref, shift_ref, count_ref, out_ref, head_ref):
    step, images, size = pl.program_id(0), out_ref.shape[0], out_ref.shape[1]

    @pl.when(step == 0)
    def _():
        for i in range(images):
            head = mm(z_ref[COUNT * i:COUNT * (i + 1)], w_ref[...])
            head_ref[i] = head.astype(BF16)

    table = bilinear((size, 1), (1, COUNT), step * size)
    for i in range(images):
        out_ref[i] = ((mm(table, head_ref[i]) * scale_ref[i] + shift_ref[i]) * is_live(count_ref, i)).astype(BF16)


def join(z, w_head, scale, shift, live_count):
    images, ch = scale.shape[0], w_head.shape[1]
    one = whole((images, 1, ch))
    return pl.pallas_call(
        join_body,
        grid=(4,),
        in_specs=[whole(z.shape), whole(w_head.shape), one, one, pl.BlockSpec(memory_space=pltpu.SMEM)],
        out_specs=pl.BlockSpec((images, COUNT, ch), lambda i: (0, i, 0)),
        out_shape=spec((images, 4 * COUNT, ch)),
        scratch_shapes=[pltpu.VMEM((images, COUNT, ch), BF16)],
        compiler_params=params(),
        cost_estimate=lasts(7),
        name="join",
    )(z, w_head, scale, shift, live_count)


def shards(tokens, live_count, dataset_id, shift_flag, norm_gains, w_qkv, w_attn_out, w_fc1, w_fc2, w_reassemble,
           conv_kernels, w_head, scale_table, shift_table, d_tokens_out, d_joined):
    slots, count = tokens.shape[:2]
    rows = slots * count
    neighbours = (lax.axis_size("rep"), lax.axis_size("wide")) == (4, 8)
    ch, ff = w_head.shape[1], w_fc1.shape[1]
    wide = lax.axis_size("wide")
    at_wide = lax.axis_index("wide")
    g, t = norm_gains.shape[1], scale_table.shape[1]
    me = bit_vector()
    line = Line()
    r = D // 16

    def gathered(part, axis):
        return lax.all_gather(part, "wide", axis=axis, tiled=True)

    def rows_of(size):
        return lambda shard, y: (shard * 2 + y) * size

    def cols_of(size):
        return lambda x: x * size

    x = tokens.reshape(rows, D)

    if neighbours:
        pieces = line.run(lambda v: prepare(me, v, w_attn_out, w_fc1, w_fc2, w_reassemble, w_head, norm_gains, scale_table,
                                            shift_table), w_qkv)
        zero = Gather(pieces[0], 5 * LANES, 1, True)
    down, g_shift_rows = line.run(bring_down, d_joined, live_count, shift_flag)
    if neighbours:
        together(line, zero)
    if neighbours:
        one = Gather(line.after(pieces[1]), 9 * LANES, 1)
        together(line, zero)
        zero.between_cores()
    n1 = line.run(norm, x)
    if neighbours:
        f_qkv, small = line.run(lambda v: assemble(me, Assembly(zero.starting(v), [(D, 3 * D), (wide, r, LANES)], [
            (0, (0, r), (0, 3 * D // 2), rows_of(r), cols_of(3 * D // 2)), (1, (0, r), (3 * D // 2, LANES), None, None)])),
            zero.pieces[0])
        together(line, one)

        gains = small[:, 2 * SMALL:2 * SMALL + 2, :g].transpose(1, 0, 2).reshape(2, wide * g)
    else:
        gains, scales, shifts = gathered(norm_gains, 1), gathered(scale_table, 1), gathered(shift_table, 1)
        f_qkv = gathered(w_qkv, 0)

    gains = gains.astype(F32)
    a1 = line.run(lambda n: (n * gains[0:1]).astype(BF16), n1)
    groups = []
    for i in range(GROUPS):
        groups.append(line.run(attention, a1, f_qkv, i))
        if neighbours and i == 0:
            together(line, one)
            own = [swap(one.terms[0], "c"), swap(one.terms[2], "c")]
            two = Gather(line.after(pieces[2]), ff // 32, 0)
        if neighbours and i == 1:
            *one.terms, own_a, own_b = line.touch(*one.terms, *own)
            one.between_cores((own_a, own_b))
            together(line, two)
        if i == 1:
            f_conv = gathered(line.after(conv_kernels), 1)

    heads_out = [group[1] for group in groups]
    if neighbours:
        scale, shift = line.run(tables, small, dataset_id, shift_flag, ch)
    else:
        onehot = (dataset_id[:, None] == jnp.arange(DATASETS, dtype=jnp.int32)[None, :]).astype(F32)
        scale = jnp.sum(onehot[:, :, None] * scales.astype(F32)[None], 1)[:, None]
        shift = jnp.sum(onehot[:, :, None] * shifts.astype(F32)[None], 1)[:, None] * shift_flag.astype(F32)[:, None, None]
    if neighbours:
        rh, at, n = ch // 16, D // 2 + ff // 2, ff // 16
        weights_one = Assembly(one, [(D, D), (D, ff), (D, ch), (ch, ch)], [
            (0, (0, r), (0, D // 2), rows_of(r), cols_of(D // 2)),
            (1, (0, r), (D // 2, ff // 2), rows_of(r), cols_of(ff // 2)),
            (2, (0, r), (at, ch // 2), rows_of(r), cols_of(ch // 2)),
            (3, (0, rh), (at + ch // 2, ch // 2), rows_of(rh), cols_of(ch // 2))])
        together(line, two)
        own = [swap(two.terms[0], "c"), swap(two.terms[2], "c")]
        (f_out, f_fc1, f_re, f_head), (x2, a2, u) = line.run(lambda v: mlp_up(v, heads_out, weights_one, me, gains), x)
        *two.terms, own_a, own_b = line.touch(*two.terms, *own)
        two.between_cores((own_a, own_b))
        weights_two = Assembly(two, [(ff, D)], [(0, (0, n), (0, D // 2), rows_of(n), cols_of(D // 2))])
        (f_fc2,), (x3b, tokens_out) = line.run(lambda v: mlp_down(v, weights_two, me, x2, live_count), u)
    else:
        f_out, f_fc1, f_re, f_head = gathered(w_attn_out, 0), gathered(w_fc1, 0), gathered(w_reassemble, 0), gathered(w_head, 0)
        f_fc2 = gathered(w_fc2, 0)
        _, (x2, a2, u) = mlp_up(x, heads_out, (f_out, f_fc1), me, gains)
        _, (x3b, tokens_out) = mlp_down(u, (f_fc2,), me, x2, live_count)
    t1, s1, t2, s2, zb = line.run(units, x3b, f_re, f_conv)

    def packed(split):
        return split if neighbours else PLAIN

    def chunk(grads, split):
        return Chunk(line, grads[0], grads[1], split) if neighbours else grads

    def go(*jobs):
        if neighbours:
            together(line, *jobs)

    g_conv, g_head, g_re, dm, small = line.run(
        lambda v: units_back(v, scale, g_shift_rows, dataset_id, zb, x3b, d_tokens_out.reshape(rows, D), live_count, f_head, f_conv, f_re,
                             t1, s1, t2, s2), down)
    s_conv = lax.psum_scatter(g_conv, "wide", scatter_dimension=1, tiled=True)
    split_two, split_one = 3 * ff // 32, 7 * r
    grads, du = line.run(lambda v: hidden_back(v, me, u, f_fc2, packed(split_two)), dm)
    c_two = chunk(grads, split_two)
    grads = line.run(lambda v: first_weight_back(v, me, a2, g_re, g_head, small, packed(split_one)), du)
    go(c_two)
    c_one = chunk(grads, split_one)
    da = line.run(lambda v: mlp_back(v, f_fc1, dm, x2, gains), du)
    go(c_two, c_one)

    def attention_step(i, extra, split):
        qkv, o, e, rs = groups[i]
        return line.run(lambda v: attention_back(v, me, i, qkv, o, e, rs, a1, f_out, extra, packed(split)), da)

    grads, dqkv_0 = attention_step(0, heads_out, ALL_XY)
    if neighbours:
        z_two = Along(c_two)
        together(line, z_two, c_one)
        c_first = Single(line, grads[0], grads[1], XY)
        c_conv = Whole(s_conv)
    else:
        c_first = grads
    (g_second,), dqkv_1 = attention_step(1, None, PLAIN)
    split_last = 3 * r
    if neighbours:
        z_one = Along(c_one)
        together(line, z_two, z_one, c_first, c_conv)
    grads, dqkv_2 = attention_step(2, g_second, split_last)
    if neighbours:
        c_conv.terms = line.touch(*c_conv.terms)
        together(line, z_one, c_first)
        c_last = Chunk(line, grads[0], grads[1], split_last)
    else:
        c_last = grads
    joined = line.run(join, zb, f_head, scale, shift, live_count)
    if neighbours:
        together(line, c_last, c_first)
    d_tokens = line.run(lambda v: input_back((dqkv_0, dqkv_1, v), f_qkv, da, x, gains), dqkv_2)

    if neighbours:
        together(line, c_last)
        rh, rows_two, half = ch // 16, ff // 16, D // 2
        blocks, n, quarter = half // LANES, ff // 2 // LANES, TABLE // 4

        def up_to(size):
            return lambda y: size * y

        def across(size):
            return lambda x, b: x * size + b * LANES

        def group_col(i):
            def col(x, b):
                at = blocks * x + b
                return at // 2 * D + WIDTH * i + at % 2 * LANES
            return col

        z_last = Along(c_first, c_last)
        together(line, z_last)
        early = Back(line, z_two, z_one)
        s_conv = line.run_all(lambda p, q: p.astype(F32) + q.astype(F32), *c_conv.terms)
        early.terms = line.touch(*early.terms)
        together(line, z_last)
        late = Back(line, z_last)
        low = early.rows[0]
        s_fc2, s_fc1, s_re, s_head, small = line.run(lambda m: finish(m, [early], [[
            (0, rows_two, 0, blocks, up_to(rows_two), across(half)),
            (1, r, low, n, up_to(r), across(ff // 2)),
            (2, r, low + r * n, 1, up_to(r), across(ch // 2)),
            (3, rh, low + r * (n + 1), 1, up_to(rh), across(ch // 2)),
            (4, quarter, low + r * (n + 1) + rh, 1, up_to(2 * quarter), lambda x, b: 0)]],
            [w_fc2.shape, w_fc1.shape, w_reassemble.shape, w_head.shape, (TABLE, LANES)]), me)
        s_qkv, s_out = finish(me, [late], [
            [(0, r, 0, blocks, up_to(r), group_col(0)), (1, r, r * blocks, blocks, up_to(r), across(half)),
             (0, r, 2 * r * blocks, blocks, up_to(r), group_col(2)), (0, r, 3 * r * blocks, blocks, up_to(r), group_col(1))]],
            [w_qkv.shape, w_attn_out.shape])
        small = small.reshape(2, ch // LANES, SMALL, LANES).transpose(0, 2, 1, 3).reshape(2, SMALL, ch)
        small = lax.dynamic_slice(small, (0, 0, at_wide * t), (2, DATASETS, t))
        g_scale, g_shift = small[0], small[1]
    else:
        def share(part, axis):
            part = lax.psum_scatter(part.astype(BF16), "wide", scatter_dimension=axis, tiled=True)
            return lax.psum(part, "rep").astype(F32)

        s_conv = lax.psum(s_conv, "rep").astype(F32)
        small = small.reshape(2, ch // LANES, SMALL, LANES).transpose(0, 2, 1, 3).reshape(2, SMALL, ch)[:, :DATASETS]
        g_scale, g_shift = share(small[0], 1), share(small[1], 1)
        s_fc2, s_fc1, s_re, s_head = share(c_two[0], 0), share(c_one[0], 0), share(c_one[1], 0), share(c_one[2], 0)
        s_out = share(c_first[1], 0)
        by_group = (c_first[0], c_last[1], c_last[0])
        s_qkv = share(jnp.concatenate([c[:, WIDTH * p:WIDTH * (p + 1)] for p in range(3) for c in by_group], 1), 0)
    g_gains = jnp.stack([jnp.sum(w_qkv.astype(F32) * s_qkv, 1), jnp.sum(w_fc1.astype(F32) * s_fc1, 1)]) / norm_gains.astype(F32)
    return (tokens_out.reshape(tokens.shape), joined, d_tokens.reshape(tokens.shape), g_gains, s_qkv, s_out, s_fc1, s_fc2,
            s_re, s_conv, s_head, g_scale, g_shift)


def solution(mesh):
    images = P(BOTH, None, None)
    slots = P(BOTH)
    rows = P("wide", None)
    cols = P(None, "wide")
    kernels = P(None, "wide", None)
    return jax.shard_map(
        shards,
        mesh=mesh,
        in_specs=(images, slots, slots, slots, cols, rows, rows, rows, rows, rows, kernels, rows, cols, cols, images, images),
        out_specs=(images, images, images, cols, rows, rows, rows, rows, rows, kernels, rows, cols, cols),
        check_vma=False,
    )
```

```python
import math

import jax
import jax.numpy as jnp
from jax import lax
from jax.experimental import pallas as pl
from jax.experimental.pallas import tpu as pltpu
from jax.sharding import PartitionSpec as P

D = 768
HEADS = 12
HD = 64
GRID = 24
COUNT = GRID * GRID
DATASETS = 10
NH = 4
GROUPS = HEADS // NH
WIDTH = NH * HD
LANES = 128
F32 = jnp.float32
BF16 = jnp.bfloat16
BOTH = ("rep", "wide")
VMEM = 60 << 20


def mm(left, right):
    return jnp.dot(left, right, preferred_element_type=F32)


def mm_tn(left, right):
    return lax.dot_general(left, right, (((0,), (0,)), ((), ())), preferred_element_type=F32)


def mm_nt(left, right):
    return lax.dot_general(left, right, (((1,), (1,)), ((), ())), preferred_element_type=F32)


def spec(shape, dtype=BF16):
    return jax.ShapeDtypeStruct(shape, dtype)


def whole(shape):
    return pl.BlockSpec(shape, lambda *_: (0,) * len(shape), pipeline_mode=pl.Buffered(1))


def params():
    return pltpu.CompilerParams(vmem_limit_bytes=VMEM)


def cost(macs, size):
    return pl.CostEstimate(flops=2 * int(macs), bytes_accessed=int(size), transcendentals=0)


def lasts(microseconds):
    return pl.CostEstimate(flops=int(microseconds * 1.15e9), bytes_accessed=0, transcendentals=0)


FLIP = {"y": 16, "x": 8, "z1": 4, "z0": 2, "c": 1}
XY, YX = ("x", "y"), ("y", "x")


def swap(value, *names):
    flip = sum(FLIP[name] for name in names)
    return lax.ppermute(value, BOTH, [(i, i ^ flip) for i in range(32)])


def bits():
    rep, wide = lax.axis_index("rep"), lax.axis_index("wide")
    return {"y": rep // 2, "x": rep % 2, "z1": wide // 4, "z0": (wide // 2) % 2, "c": wide % 2}


def bit_vector():
    b = bits()
    return jnp.stack([b[k] for k in ("y", "x", "z1", "z0", "c")]).astype(jnp.int32)


def along_z(parts):
    size = lax.axis_size("wide") // 2
    groups = [[2 * z + core for z in range(size)] for core in range(2)]
    return lax.all_to_all(parts, "wide", 0, 0, tiled=True, axis_index_groups=groups)


class Line:
    def __init__(self):
        self.tokens = []

    def after(self, value):
        return lax.optimization_barrier((value, *self.tokens))[0] if self.tokens else value

    def run(self, call, first, *rest):
        out = call(self.after(first), *rest)
        self.tokens = jax.tree.leaves(out)[-1:]
        return out

    def touch(self, *values):
        out = lax.optimization_barrier((*values, *self.tokens))
        self.tokens = list(out[:len(values)])
        return self.tokens

    def run_all(self, call, *values):
        out = call(*(lax.optimization_barrier((*values, *self.tokens))[:len(values)]))
        self.tokens = jax.tree.leaves(out)
        return out


def locate(me, order, plane, z, core):
    place = {order[0]: plane[0], order[1]: plane[1]}
    shard = ((me[2] ^ z[0]) * 2 + (me[3] ^ z[1])) * 2 + (me[4] ^ core)
    return shard, me[0] ^ place["y"], me[1] ^ place["x"]


class Gather:
    def __init__(self, piece, at, axis, swaps=False):
        self.at, self.axis, self.stage = at, axis, 0
        if swaps:
            self.terms = [piece, swap(piece, "z0"), swap(piece, "z1"), swap(piece, "z1", "z0")]
        else:
            self.terms = [along_z(jnp.broadcast_to(piece[None], (4,) + piece.shape))]
        self.relative = swaps

    def add(self, *terms):
        if self.stage == 0:
            value = jnp.stack(terms) if self.relative else terms[0]
            return [lax.slice_in_dim(value, 0, self.at, axis=self.axis + 1),
                    lax.slice_in_dim(value, self.at, value.shape[self.axis + 1], axis=self.axis + 1)]
        return [jnp.concatenate(terms[:2]), jnp.concatenate(terms[2:])]

    def send(self, out):
        one, two = out
        if self.stage == 0:
            self.terms = [one, swap(one, "x"), two, swap(two, "y")]
        else:
            self.terms = [one, swap(one, "y"), two, swap(two, "x")]
        self.stage += 1

    def starting(self, first):
        self.pieces[0] = first
        return self

    def between_cores(self, own=None):
        one, one_y, two, two_x = self.terms
        own = own or (swap(one, "c"), swap(two, "c"))
        self.pieces = [one, one_y, own[0], swap(one_y, "c"), two, two_x, own[1], swap(two_x, "c")]


PLANE = [[(s // 4, a % 2, s // 2 % 2, s % 2, a // 2) for s in range(8)] for a in range(4)]


class Assembly:
    def __init__(self, gathered, shapes, parts):
        self.gathered, self.pieces, self.shapes, self.parts = gathered, gathered.pieces, shapes, parts
        self.count = 64 * len(parts)

    def halves(self, rows, cols):
        at, axis = self.gathered.at, self.gathered.axis
        first, size = (rows, cols)[axis]
        out = []
        for low, high, shift in ((first, min(first + size, at), 0), (max(first, at), first + size, at)):
            span = (low - shift, high - low)
            out.append(None if high <= low else (span, cols, low - first, 0) if axis == 0 else (rows, span, 0, low - first))
        return out

    def start(self, me_ref, ins, outs, sem):
        started, number = [[] for _ in self.shapes], 0
        for k, rows, cols, row, col in self.parts:
            for half, order in enumerate((XY, YX)):
                for a, places in enumerate(PLANE):
                    for s, (first, second, z1, z0, core) in enumerate(places):
                        z = (z1, z0) if self.gathered.relative else (me_ref[2] ^ z1, me_ref[3] ^ z0)
                        shard, y, x = locate(me_ref, order, (first, second), z, core)
                        share = self.halves(rows, cols)[half]
                        if share is None or (row is None and (first or second)):
                            continue
                        (r0, r), (c0, n), down, across = share
                        source = ins[4 * half + a].at[s, pl.ds(r0, r), pl.ds(c0, n)]
                        if row is None:
                            place = outs[k].at[shard, pl.ds(down, r), pl.ds(across, n)]
                        else:
                            place = outs[k].at[pl.ds(pl.multiple_of(row(shard, y) + down, 16), r),
                                               pl.ds(pl.multiple_of(col(x) + across, LANES), n)]
                        copy = pltpu.make_async_copy(source, place, sem.at[number])
                        copy.start()
                        started[k].append(copy)
                        number += 1
        return started


def assemble(me, assembly):
    def body(me_ref, *refs):
        for copies in assembly.start(me_ref, refs[:8], refs[8:-1], refs[-1]):
            for copy in copies:
                copy.wait()

    return pl.pallas_call(
        body,
        grid=(1,),
        in_specs=[pl.BlockSpec(memory_space=pltpu.SMEM)] + [pl.BlockSpec(memory_space=pl.ANY)] * 8,
        out_specs=[whole(s) for s in assembly.shapes],
        out_shape=[spec(s) for s in assembly.shapes],
        scratch_shapes=[pltpu.SemaphoreType.DMA((assembly.count,))],
        compiler_params=params(),
        cost_estimate=lasts(0),
        name="assemble",
    )(me, *assembly.pieces)


class Weights:
    def __init__(self, weights):
        self.assembly = weights if isinstance(weights, Assembly) else None
        if self.assembly:
            shapes = self.assembly.shapes
            self.ins, self.in_specs = self.assembly.pieces, [pl.BlockSpec(memory_space=pl.ANY)] * 8
            self.outs, self.out_specs = [spec(s) for s in shapes], [pl.BlockSpec(memory_space=pl.ANY)] * len(shapes)
            self.scratch = [pltpu.VMEM(s, BF16) for s in shapes] + [
                pltpu.SemaphoreType.DMA((self.assembly.count,)), pltpu.SemaphoreType.DMA((len(shapes),))]
        else:
            self.ins, self.in_specs = list(weights), [whole(w.shape) for w in weights]
            self.outs, self.out_specs, self.scratch = [], [], []

    def bind(self, me_ref, ins, outs, scratch):
        self.me_ref, self.in_refs, self.out_refs, self.held = me_ref, ins, outs, scratch
        self.refs = scratch[:len(outs)] if self.assembly else ins

    def begin(self, *works):
        if not self.assembly:
            for work in works:
                work()
            return
        copies = self.assembly.start(self.me_ref, self.in_refs, self.refs, self.held[-2])
        for k, copy_list in enumerate(copies):
            for copy in copy_list:
                copy.wait()
            self.back(k).start()
            if k < len(works):
                works[k]()

    def back(self, k):
        return pltpu.make_async_copy(self.refs[k], self.out_refs[k], self.held[-1].at[k])

    def end(self):
        for k in range(len(self.out_refs)):
            self.back(k).wait()


def together(line, *jobs):
    counts = [len(job.terms) for job in jobs]

    def call(*terms):
        out = []
        for job, count in zip(jobs, counts):
            out.append(job.add(*terms[:count]))
            terms = terms[count:]
        return out

    for job, out in zip(jobs, line.run_all(call, *[term for job in jobs for term in job.terms])):
        job.send(out)


class Chunk:
    def __init__(self, line, keep, send, split):
        self.split, self.stage = split, 0
        self.terms = [keep, swap(line.after(send), "c")]

    def add(self, *terms):
        if self.stage == 0:
            parts = [(slots, rows) for rows in (slice(0, self.split), slice(self.split, None)) for slots in (slice(0, 8), slice(8, 16))]
            return [terms[0][part] + terms[1][part] for part in parts]
        return [terms[i][part] + terms[i + 1][part] for i in (0, 2) for part in (slice(0, 4), slice(4, 8))]

    def send(self, out):
        one, two = ("x", "y") if self.stage == 0 else ("y", "x")
        self.terms = [out[0], swap(out[1], one), out[2], swap(out[3], two)]
        self.stage += 1


class Single(Chunk):
    def __init__(self, line, keep, send, order):
        super().__init__(line, keep, send, None)
        self.order = order

    def add(self, *terms):
        if self.stage == 2:
            return [terms[0] + terms[1]]
        half = terms[0].shape[0] // 2
        return [terms[0][part] + terms[1][part] for part in (slice(0, half), slice(half, None))]

    def send(self, out):
        self.terms = out if self.stage == 2 else [out[0], swap(out[1], self.order[self.stage])]
        self.stage += 1


class Along:
    def __init__(self, *chunks):
        self.stage, self.terms = 0, [term for chunk in chunks for term in chunk.terms]
        self.done = [len(chunk.terms) == 1 for chunk in chunks for _ in range(max(1, len(chunk.terms) // 2))]

    def add(self, *terms):
        if self.stage:
            return [sum(terms[0][i].astype(F32) for i in range(4)).astype(BF16)]
        terms = list(terms)
        sums = [terms.pop(0) if done else terms.pop(0) + terms.pop(0) for done in self.done]
        return [jnp.concatenate(sums, 1)]

    def send(self, out):
        if self.stage:
            self.total = out[0]
        else:
            self.terms = [along_z(out[0])]
        self.stage += 1


class Back:
    def __init__(self, line, *alongs):
        self.rows = [along.total.shape[0] for along in alongs]
        if len(alongs) > 1:
            (total,) = line.run_all(lambda *parts: [jnp.concatenate(parts)], *[along.total for along in alongs])
        else:
            total = alongs[0].total
        self.terms = [total, swap(total, "x"), swap(total, "y"), swap(total, "x", "y")]


class Whole:
    def __init__(self, value):
        self.terms = [value, swap(value, "x")]

    def add(self, *terms):
        return [terms[0] + terms[1]]

    def send(self, out):
        self.terms = [out[0], swap(out[0], "y")]


def finish(me, backs, places, shapes):
    ins = [t for back in backs for t in back.terms]

    def body(me_ref, *refs):
        outs = refs[len(ins):len(ins) + len(shapes)]
        held = refs[len(ins) + len(shapes):]
        for c, parts in enumerate(places):
            for q in range(4):
                held[c][q] = refs[4 * c + q][...]
            for y in range(2):
                for x in range(2):
                    at = 2 * (me_ref[0] ^ y) + (me_ref[1] ^ x)
                    for k, r, r0, blocks, row, col in parts:
                        for b in range(blocks):
                            at_row = row(y) + (r * x if shapes[k][1] == LANES else 0)
                            outs[k][at_row:at_row + r, col(x, b):col(x, b) + LANES] = (
                                held[c][at, r0 + b * r:r0 + (b + 1) * r, :].astype(F32))

    return pl.pallas_call(
        body,
        grid=(1,),
        in_specs=[pl.BlockSpec(memory_space=pltpu.SMEM)] + [whole(a.shape) for a in ins],
        out_specs=[whole(s) for s in shapes],
        out_shape=[spec(s, F32) for s in shapes],
        scratch_shapes=[pltpu.VMEM((4,) + back.terms[0].shape, BF16) for back in backs],
        compiler_params=params(),
        cost_estimate=lasts(3),
        name="finish",
    )(me, *ins)


PLAIN = "plain"
ALL_XY, ALL_YX = 1 << 30, 0


TABLE = 64


class Sink:
    def __init__(self, shapes, split, table=False):
        self.shapes, self.split, self.table = shapes, split, table
        rows = sum(k // 16 * (n // 2 // LANES) for k, n in shapes) + (TABLE // 4 if table else 0)
        if split == PLAIN:
            self.outs, self.scratch = [spec(s) for s in shapes], []
        else:
            self.outs = [spec((16, rows, LANES))] * 2
            self.scratch = [pltpu.VMEM((2, k, n // 2), BF16) for k, n in shapes]
            self.scratch += [pltpu.VMEM((TABLE, LANES), BF16)] if table else []

    def out_specs(self):
        return [whole(o.shape) for o in self.outs]

    def put(self, outs, held, k, rows, value):
        value = value.astype(BF16)
        half = self.shapes[k][1] // 2
        if self.split == PLAIN:
            outs[k][rows, :] = value
        else:
            held[k][0, rows, :] = value[:, :half]
            held[k][1, rows, :] = value[:, half:]

    def deliver(self, me_ref, outs, held):
        if self.split == PLAIN:
            return
        for core in range(2):
            for s in range(16):
                z = (me_ref[2] ^ (s // 2 % 2), me_ref[3] ^ (s % 2))
                places = [locate(me_ref, order, (s // 8, s // 4 % 2), z, core) for order in (XY, YX)]
                at = 0
                for k, (rows, cols) in enumerate(self.shapes):
                    r = rows // 16
                    size = r // 2 if r > 144 and r % 32 == 0 else r
                    for b in range(cols // 2 // LANES):
                        for part in range(0, r, size):
                            shard, y, x = places[0 if at < self.split else 1]
                            start = pl.multiple_of((shard * 2 + y) * r + part, 16)
                            outs[core][s, at:at + size, :] = held[k][x, pl.ds(start, size), b * LANES:(b + 1) * LANES]
                            at += size
                if self.table:
                    r = TABLE // 4
                    _, y, x = places[0 if at < self.split else 1]
                    outs[core][s, at:at + r, :] = held[-1][pl.ds(pl.multiple_of((2 * y + x) * r, 16), r), :]


def gelu_pair(values):
    cdf = 0.5 + 0.5 * lax.erf(values * 0.7071067811865476)
    pdf = 0.3989422804014327 * jnp.exp(-0.5 * values * values)
    return values * cdf, cdf + values * pdf


def gelu(values):
    return values * (0.5 + 0.5 * lax.erf(values * 0.7071067811865476))


def normalize(values):
    centred = values - jnp.mean(values, -1, keepdims=True)
    recip = lax.rsqrt(jnp.mean(centred * centred, -1, keepdims=True) + 1e-06)
    return centred * recip, recip


def norm_transpose(grad_normed, normed, recip):
    return recip * (
        grad_normed
        - jnp.mean(grad_normed, -1, keepdims=True)
        - normed * jnp.mean(grad_normed * normed, -1, keepdims=True)
    )


SMALL = 16


def prepare(me, w_qkv, w_out, w_fc1, w_fc2, w_re, w_head, gains, scales, shifts):
    ff, ch = w_fc1.shape[1], w_re.shape[1]
    half = w_qkv.shape[0] // 2
    rows_two, rows_head = w_fc2.shape[0] // 2, w_head.shape[0] // 2
    n = w_qkv.shape[1] // 2

    def body(me_ref, qkv_ref, out_ref, fc1_ref, fc2_ref, re_ref, head_ref, gains_ref, scales_ref, shifts_ref,
             zero_ref, one_ref, two_ref):
        zero_ref[:, n:] = jnp.zeros((half, LANES), BF16)
        zero_ref[0:DATASETS, n:n + scales.shape[1]] = scales_ref[...]
        zero_ref[SMALL:SMALL + DATASETS, n:n + shifts.shape[1]] = shifts_ref[...]
        zero_ref[2 * SMALL:2 * SMALL + 2, n:n + gains.shape[1]] = gains_ref[...]
        rows = pl.ds(pl.multiple_of(me_ref[0] * half, 16), half)
        rows_of_two = pl.ds(pl.multiple_of(me_ref[0] * rows_two, 16), rows_two)
        rows_of_head = pl.ds(pl.multiple_of(me_ref[0] * rows_head, 16), rows_head)
        for x in range(2):
            @pl.when(me_ref[1] == x)
            def _():
                zero_ref[:, :n] = qkv_ref[rows, n * x:n * (x + 1)]
                one_ref[:, :D // 2] = out_ref[rows, D // 2 * x:D // 2 * (x + 1)]
                at = D // 2 + ff // 2
                one_ref[:, D // 2:at] = fc1_ref[rows, ff // 2 * x:ff // 2 * (x + 1)]
                one_ref[:, at:at + ch // 2] = re_ref[rows, ch // 2 * x:ch // 2 * (x + 1)]
                one_ref[0:rows_head, at + ch // 2:] = head_ref[rows_of_head, ch // 2 * x:ch // 2 * (x + 1)]
                two_ref[...] = fc2_ref[rows_of_two, D // 2 * x:D // 2 * (x + 1)]
        one_ref[rows_head:, D // 2 + ff // 2 + ch // 2:] = jnp.zeros((half - rows_head, LANES), BF16)

    ins = (w_qkv, w_out, w_fc1, w_fc2, w_re, w_head, gains, scales, shifts)
    outs = [spec((half, n + LANES)), spec((half, D // 2 + ff // 2 + ch // 2 + LANES)), spec((rows_two, D // 2))]
    return pl.pallas_call(
        body,
        grid=(1,),
        in_specs=[pl.BlockSpec(memory_space=pltpu.SMEM)] + [whole(a.shape) for a in ins],
        out_specs=[whole(o.shape) for o in outs],
        out_shape=outs,
        compiler_params=params(),
        cost_estimate=lasts(2.4),
        name="prepare",
    )(me, *ins)


def norm_body(x_ref, out_ref):
    out_ref[...] = normalize(x_ref[...].astype(F32))[0]


def norm(x):
    rows = x.shape[0]
    block = pl.BlockSpec((rows // 4, D), lambda i: (i, 0))
    return pl.pallas_call(
        norm_body,
        grid=(4,),
        in_specs=[block],
        out_specs=block,
        out_shape=spec((rows, D), F32),
        compiler_params=params(),
        cost_estimate=lasts(0),
        name="norm",
    )(x)


def bilinear(targets, sources, first):
    size = 2 * GRID
    step = (GRID - 1) / (size - 1)

    def hat(target, source):
        return jnp.maximum(1.0 - jnp.abs(target.astype(F32) * step - source.astype(F32)), 0.0)

    target = lax.broadcasted_iota(jnp.int32, targets, targets.index(max(targets))) + first
    source = lax.broadcasted_iota(jnp.int32, sources, sources.index(max(sources)))
    return (hat(target // size, source // GRID) * hat(target % size, source % GRID)).astype(BF16)


def is_live(count_ref, image):
    return (image < count_ref[0]).astype(F32)


def down_body(dj_ref, count_ref, flag_ref, down_ref, gshift_ref):
    step, images, size = pl.program_id(0), dj_ref.shape[0], dj_ref.shape[1]
    table = bilinear((1, size), (COUNT, 1), step * size)
    for i in range(images):
        part = mm(table, dj_ref[i])
        sums = jnp.sum(dj_ref[i].astype(F32), 0, keepdims=True)

        @pl.when(step == 0)
        def _():
            down_ref[i] = part
            gshift_ref[i] = sums

        @pl.when(step > 0)
        def _():
            down_ref[i] += part
            gshift_ref[i] += sums

        @pl.when(step == pl.num_programs(0) - 1)
        def _():
            down_ref[i] = down_ref[i] * is_live(count_ref, i)
            gshift_ref[i] = gshift_ref[i] * (is_live(count_ref, i) * flag_ref[i].astype(F32))


def bring_down(dj, live_count, flag):
    images, count, ch = dj.shape
    one = whole((images, 1, ch))
    return pl.pallas_call(
        down_body,
        grid=(4,),
        in_specs=[pl.BlockSpec((images, count // 4, ch), lambda i: (0, i, 0))] + [pl.BlockSpec(memory_space=pltpu.SMEM)] * 2,
        out_specs=[whole((images, COUNT, ch)), one],
        out_shape=[spec((images, COUNT, ch), F32), spec((images, 1, ch), F32)],
        compiler_params=params(),
        cost_estimate=lasts(8.9),
        name="bring_down",
    )(dj, live_count, flag)


def tables_body(small_ref, id_ref, flag_ref, scale_ref, shift_ref):
    shards, rows = small_ref.shape[0], SMALL
    ch = scale_ref.shape[2]
    width = ch // shards
    whole_tables = [jnp.zeros((rows, ch), F32), jnp.zeros((rows, ch), F32)]
    lane = lax.broadcasted_iota(jnp.int32, (LANES, ch), 0)
    col = lax.broadcasted_iota(jnp.int32, (LANES, ch), 1)
    for w in range(shards):
        place = ((col == lane + width * w) & (lane < width)).astype(BF16)
        for k in range(2):
            whole_tables[k] = whole_tables[k] + mm(small_ref[w, rows * k:rows * (k + 1), :], place)
    row = lax.broadcasted_iota(jnp.int32, (rows, 1), 0)
    for i in range(scale_ref.shape[0]):
        mask = row == id_ref[i]
        scale_ref[i] = jnp.sum(jnp.where(mask, whole_tables[0], 0.0), 0, keepdims=True)
        shift_ref[i] = jnp.sum(jnp.where(mask, whole_tables[1], 0.0), 0, keepdims=True) * flag_ref[i].astype(F32)


def tables(small, ids, flags, ch):
    out = spec((ids.shape[0], 1, ch), F32)
    return pl.pallas_call(
        tables_body,
        grid=(1,),
        in_specs=[whole(small.shape)] + [pl.BlockSpec(memory_space=pltpu.SMEM)] * 2,
        out_specs=[whole(out.shape)] * 2,
        out_shape=[out] * 2,
        compiler_params=params(),
        cost_estimate=lasts(2),
        name="tables",
    )(small, ids, flags)


def attention_body(a1_ref, wq_ref, wk_ref, wv_ref, qkv_ref, o_ref, e_ref, r_ref):
    for i, ref in enumerate((wq_ref, wk_ref, wv_ref)):
        qkv_ref[:, WIDTH * i:WIDTH * (i + 1)] = mm(a1_ref[...], ref[...]).astype(BF16)
    def part(kind, h):
        return slice(WIDTH * kind + HD * h, WIDTH * kind + HD * (h + 1))

    def scores(h):
        return mm_nt(qkv_ref[:, part(1, h)], qkv_ref[:, part(0, h)] * jnp.asarray(0.125, BF16))

    following = scores(0)
    for h in range(NH):
        s, following = following, scores(h + 1) if h + 1 < NH else None
        e = jnp.exp(s - jnp.max(s, 0, keepdims=True))
        r = 1.0 / jnp.sum(e, 0, keepdims=True)
        low = e.astype(BF16)
        e_ref[h] = low
        o_ref[:, HD * h:HD * (h + 1)] = (mm_tn(qkv_ref[:, part(2, h)], low) * r).T.astype(BF16)
        r_ref[0, h:h + 1, :] = r


def group_specs():
    def cols(n):
        return pl.BlockSpec((COUNT, n), lambda i: (i, 0))

    return cols, pl.BlockSpec((NH, COUNT, COUNT), lambda i: (i, 0, 0)), pl.BlockSpec((1, NH, COUNT), lambda i: (i, 0, 0))


def group_columns(group):
    return [pl.BlockSpec((D, WIDTH), lambda i, p=p: (0, GROUPS * p + group), pipeline_mode=pl.Buffered(1)) for p in range(3)]


def attention(a1, w, group):
    rows = a1.shape[0]
    images = rows // COUNT
    cols, probs, sums = group_specs()
    return pl.pallas_call(
        attention_body,
        grid=(images,),
        in_specs=[cols(D)] + group_columns(group),
        out_specs=[cols(3 * WIDTH), cols(WIDTH), probs, sums],
        out_shape=[spec((rows, 3 * WIDTH)), spec((rows, WIDTH)), spec((images * NH, COUNT, COUNT)),
                   spec((images, NH, COUNT), F32)],
        compiler_params=params(),
        cost_estimate=lasts(11),
        name="attention",
    )(a1, w, w, w)


def attention_back(da, me, group, qkv, o, e, r, a1, w_out, extra, split):
    rows = da.shape[0]
    images = rows // COUNT
    cols, probs, sums = group_specs()
    shape = (D, 3 * WIDTH)
    sink = Sink([shape], PLAIN) if extra is None else Sink([shape, (D, D)], split)
    n_out = len(sink.outs)
    extra = list(extra) if isinstance(extra, (list, tuple)) else [] if extra is None else [extra]

    def body(da_ref, me_ref, qkv_ref, o_ref, e_ref, r_ref, a1_ref, wout_ref, *refs):
        more, refs = refs[:len(extra)], refs[len(extra):]
        grads, dqkv, held = refs[:n_out], refs[n_out], refs[n_out + 1:]
        step = pl.program_id(0)
        at = pl.ds(pl.multiple_of(step * COUNT, COUNT), COUNT)
        ones = jnp.ones((8, HD), BF16)
        do_all = mm_nt(da_ref[at, :], wout_ref[...]).astype(BF16)
        for h in range(NH):
            q, k, v = (slice(WIDTH * i + HD * h, WIDTH * i + HD * (h + 1)) for i in range(3))
            do = do_all[:, HD * h:HD * (h + 1)]
            delta = mm_nt(ones, (do.astype(F32) * o_ref[:, HD * h:HD * (h + 1)].astype(F32)).astype(BF16))[0:1]
            prob = e_ref[h].astype(F32) * r_ref[0, h:h + 1, :]
            dp = mm_nt(qkv_ref[:, v], do)
            ds = (prob * (dp - delta)).astype(BF16)
            dqkv[at, v] = mm(prob.astype(BF16), do).astype(BF16)
            dqkv[at, k] = (mm(ds, qkv_ref[:, q]) * 0.125).astype(BF16)
            dqkv[at, q] = (mm_tn(ds, qkv_ref[:, k]) * 0.125).astype(BF16)

        @pl.when(step == images - 1)
        def _():
            sink.put(grads, held, 0, slice(0, D), mm_tn(a1_ref[...], dqkv[...]))
            if len(extra) > 1:
                for i, ref in enumerate(more):
                    sink.put(grads, held, 1, slice(WIDTH * i, WIDTH * (i + 1)), mm_tn(ref[...], da_ref[...]))
            elif extra:
                sink.put(grads, held, 1, slice(0, D), more[0][...])
            sink.deliver(me_ref, grads, held)

    more_specs = [whole(a.shape) for a in extra]
    out = pl.pallas_call(
        body,
        grid=(images,),
        in_specs=[whole(da.shape), pl.BlockSpec(memory_space=pltpu.SMEM), cols(3 * WIDTH), cols(WIDTH), probs, sums, whole(a1.shape),
                  pl.BlockSpec((WIDTH, D), lambda i: (group, 0))] + more_specs,
        out_specs=sink.out_specs() + [whole((rows, 3 * WIDTH))],
        out_shape=sink.outs + [spec((rows, 3 * WIDTH))],
        scratch_shapes=sink.scratch,
        compiler_params=params(),
        cost_estimate=lasts(18),
        name="attention_back",
    )(da, me, qkv, o, e, r, a1, w_out, *extra)
    return out[:n_out], out[n_out]


def input_back(dqkv, w, dx2, x, gains):
    rows = x.shape[0]
    block = rows // 4

    def body(*refs):
        (w_ref, dx2_ref, x_ref, gains_ref), out_ref = refs[GROUPS:-1], refs[-1]
        da1 = jnp.zeros((block, D), F32)
        for i, ref in enumerate(refs[:GROUPS]):
            for p in range(3):
                at = D * p + WIDTH * i
                da1 = da1 + mm_nt(ref[:, WIDTH * p:WIDTH * (p + 1)], w_ref[:, at:at + WIDTH])
        n1, rs1 = normalize(x_ref[...].astype(F32))
        out_ref[...] = (dx2_ref[...].astype(F32) + norm_transpose(da1 * gains_ref[0:1], n1, rs1)).astype(BF16)

    def cols(n):
        return pl.BlockSpec((block, n), lambda i: (i, 0))

    return pl.pallas_call(
        body,
        grid=(4,),
        in_specs=[cols(3 * WIDTH)] * GROUPS + [whole(w.shape), cols(D), cols(D), whole(gains.shape)],
        out_specs=cols(D),
        out_shape=spec((rows, D)),
        compiler_params=params(),
        cost_estimate=lasts(9),
        name="input_back",
    )(*dqkv, w, dx2, x, gains)


def mlp_up(x, heads_out, weights, me, gains, block=1024):
    rows = x.shape[0]
    weights = Weights(weights)
    ff = (weights.assembly.shapes[1] if weights.assembly else weights.ins[1].shape)[1]
    n_in, n_out = len(weights.ins), len(weights.outs)
    chunk = rows // 4
    last = ff // block - 1

    def body(me_ref, x_ref, o0_ref, o1_ref, o2_ref, gains_ref, *refs):
        x2_ref, a2_ref, u_ref = refs[n_in:n_in + 3]
        weights.bind(me_ref, refs[:n_in], refs[n_in + 3:n_in + 3 + n_out], refs[n_in + 3 + n_out:])
        wout_ref, w1_ref = weights.refs[:2]
        step = pl.program_id(0)

        def project():
            for p in range(0, rows, chunk):
                at = slice(p, p + chunk)
                x2 = x_ref[at].astype(F32)
                for i, ref in enumerate((o0_ref, o1_ref, o2_ref)):
                    x2 = x2 + mm(ref[at], wout_ref[WIDTH * i:WIDTH * (i + 1), :])
                x2_ref[at] = x2.astype(BF16)
                a2_ref[at] = (normalize(x2)[0] * gains_ref[1:2]).astype(BF16)

        @pl.when(step == 0)
        def _():
            weights.begin(project)

        u_ref[...] = mm(a2_ref[...], w1_ref[:, pl.ds(pl.multiple_of(step * block, LANES), block)]).astype(BF16)

        @pl.when(step == last)
        def _():
            weights.end()

    full, cols = whole((rows, D)), pl.BlockSpec((rows, block), lambda i: (0, i))
    out = pl.pallas_call(
        body,
        grid=(ff // block,),
        in_specs=[pl.BlockSpec(memory_space=pltpu.SMEM), full] + [whole((rows, WIDTH))] * 3 + [whole((2, D))] + weights.in_specs,
        out_specs=[full, full, cols] + weights.out_specs,
        out_shape=[spec((rows, D)), spec((rows, D)), spec((rows, ff))] + weights.outs,
        scratch_shapes=weights.scratch,
        compiler_params=params(),
        cost_estimate=lasts(17),
        name="mlp_up",
    )(me, x, *heads_out, gains, *weights.ins)
    return out[3:], out[:3]


def mlp_down(u, weights, me, x2, live_count):
    rows, ff = u.shape
    weights = Weights(weights)
    n_in, n_out = len(weights.ins), len(weights.outs)
    block = rows // 4

    def body(me_ref, count_ref, u_ref, x2_ref, *refs):
        x3b_ref, out_ref = refs[n_in:n_in + 2]
        weights.bind(me_ref, refs[:n_in], refs[n_in + 2:n_in + 2 + n_out], refs[n_in + 2 + n_out:])
        (w2_ref,) = weights.refs
        step = pl.program_id(0)

        @pl.when(step == 0)
        def _():
            weights.begin()

        x3 = x2_ref[...].astype(F32)
        size = ff // 6
        for k in range(6):
            at = slice(size * k, size * (k + 1))
            x3 = x3 + mm(gelu(u_ref[:, at].astype(F32)).astype(BF16), w2_ref[at, :])
        x3b_ref[...] = x3.astype(BF16)
        image = step * block // COUNT
        out_ref[...] = (x3 * is_live(count_ref, image)).astype(BF16)

        @pl.when(step == 3)
        def _():
            weights.end()

    at = pl.BlockSpec((block, D), lambda i: (i, 0))
    out = pl.pallas_call(
        body,
        grid=(4,),
        in_specs=[pl.BlockSpec(memory_space=pltpu.SMEM)] * 2 + [pl.BlockSpec((block, ff), lambda i: (i, 0)), at] + weights.in_specs,
        out_specs=[at, at] + weights.out_specs,
        out_shape=[spec((rows, D))] * 2 + weights.outs,
        scratch_shapes=weights.scratch,
        compiler_params=params(),
        cost_estimate=lasts(15),
        name="mlp_down",
    )(me, live_count, u, x2, *weights.ins)
    return out[2:], out[:2]


def spread(value, out_ref, rows, sign):
    count, ch = value.shape
    at = lax.broadcasted_iota(jnp.int32, (count, 1), 0)
    col = at % GRID
    gap = jnp.zeros((GRID, ch), F32)
    for dx in (-1, 0, 1):
        step = sign * dx
        moved = value
        if step:
            moved = pltpu.roll(value, (-step) % count, 0)
            moved = jnp.where((col + step >= 0) & (col + step < GRID), moved, 0.0)
        for dy in (-1, 0, 1):
            block = 3 * (dy + 1) + dx + 1
            if sign * dy == 1:
                part = jnp.concatenate([moved[GRID:], gap], 0)
            elif sign * dy == -1:
                part = jnp.concatenate([gap, moved[:-GRID]], 0)
            else:
                part = moved
            out_ref[rows, block * ch:(block + 1) * ch] = part.astype(BF16)


def units_body(x_ref, wre_ref, w_ref, t1_ref, s1_ref, t2_ref, s2_ref, zb_ref, cols, z_ref):
    unit = pl.program_id(0)
    images = [slice(COUNT * i, COUNT * (i + 1)) for i in range(x_ref.shape[0] // COUNT)]

    @pl.when(unit == 0)
    def _():
        z_ref[...] = mm(x_ref[...], wre_ref[...])

    inner = []
    for at in images:
        act, slope = gelu_pair(z_ref[at])
        t1_ref[0, at], s1_ref[0, at] = act.astype(BF16), slope.astype(BF16)
        spread(act, cols, at, 1)
        inner.append(mm(cols[at], w_ref[0]))
    for at, value in zip(images, inner):
        act, slope = gelu_pair(value)
        t2_ref[0, at], s2_ref[0, at] = act.astype(BF16), slope.astype(BF16)
        spread(act, cols, at, 1)
        z_ref[at] += mm(cols[at], w_ref[1])

    @pl.when(unit == 1)
    def _():
        zb_ref[...] = z_ref[...].astype(BF16)


def units(x3b, w_re, w_conv):
    rows, ch = x3b.shape[0], w_re.shape[1]
    acts = pl.BlockSpec((1, rows, ch), lambda i: (i, 0, 0))
    return pl.pallas_call(
        units_body,
        grid=(2,),
        in_specs=[whole(x3b.shape), whole(w_re.shape), pl.BlockSpec((2,) + w_conv.shape[1:], lambda i: (i, 0, 0))],
        out_specs=[acts] * 4 + [whole((rows, ch))],
        out_shape=[spec((2, rows, ch))] * 4 + [spec((rows, ch))],
        scratch_shapes=[pltpu.VMEM((rows, 9 * ch), BF16), pltpu.VMEM((rows, ch), F32)],
        compiler_params=params(),
        cost_estimate=lasts(18),
        name="units",
    )(x3b, w_re, w_conv)


def units_back_body(down_ref, scale_ref, gshift_ref, id_ref, z_ref, x3b_ref, gt_ref, count_ref, whead_ref, wre_ref,
                    w_ref, t1_ref, s1_ref, t2_ref, s2_ref,
                    gw_ref, ghead_ref, gre_ref, dm_ref, table_ref, moved_two, turned_two, dz_ref):
    images, _, ch = down_ref.shape

    @pl.when(pl.program_id(0) == 0)
    def _():
        dq = jnp.concatenate([(down_ref[i] * scale_ref[i]).astype(BF16) for i in range(images)], 0)
        ghead_ref[...] = mm_tn(z_ref[...], dq).astype(BF16)
        dz_ref[...] = mm_nt(dq, whead_ref[...])
        table_ref[...] = jnp.zeros_like(table_ref)
        for i in range(images):
            head = mm(z_ref[COUNT * i:COUNT * (i + 1)], whead_ref[...])
            sums = (jnp.sum(head * down_ref[i], 0, keepdims=True), gshift_ref[i])
            for b in range(2 * ch // LANES):
                at, row = SMALL * b, sums[b // (ch // LANES)]
                cols = slice(LANES * (b % (ch // LANES)), LANES * (b % (ch // LANES) + 1))
                hot = lax.broadcasted_iota(jnp.int32, (SMALL, 1), 0) == id_ref[i]
                table_ref[at:at + SMALL] += jnp.where(hot, row[:, cols], 0.0)

    places = [slice(COUNT * i, COUNT * (i + 1)) for i in range(images)]

    def back(index, grads, act_ref, slope_ref):
        moved, turned = moved_two.at[index], turned_two.at[index]
        for b in range(9):
            at = slice(ch * b, ch * (b + 1))
            turned[:, at] = w_ref[index, at, :]
        out = []
        for at, grad in zip(places, grads):
            spread(grad, moved, at, -1)
            out.append(mm_nt(moved[at, :], turned[...]) * slope_ref[0, at].astype(F32))
        g = mm_tn(act_ref[0], moved[...])
        for b in range(9):
            at = slice(ch * b, ch * (b + 1))
            gw_ref[index, at, :] = g[:, at].astype(BF16)
        return out

    grads = back(1, [dz_ref[at] for at in places], t2_ref, s2_ref)
    for at, grad in zip(places, back(0, grads, t1_ref, s1_ref)):
        dz_ref[at] += grad

    @pl.when(pl.program_id(0) == 1)
    def _():
        dr = dz_ref[...].astype(BF16)
        gre_ref[...] = mm_tn(x3b_ref[...], dr).astype(BF16)
        dx3 = mm_nt(dr, wre_ref[...])
        for i in range(images):
            at = slice(COUNT * i, COUNT * (i + 1))
            part = gt_ref[at].astype(F32) * is_live(count_ref, i) + dx3[at]
            dm_ref[at] = part.astype(BF16)


def units_back(down, scale, gshift, ids, z, x3b, gt, live_count, w_head, w_conv, w_re, t1, s1, t2, s2):
    rows, ch = z.shape
    ins = (down, scale, gshift, ids, z, x3b, gt, live_count, w_head, w_re)
    outs = [spec(w_conv.shape), spec(w_head.shape), spec(w_re.shape), spec((rows, D)),
            spec((2 * ch // LANES * SMALL, LANES), F32)]
    kernels = pl.BlockSpec((2,) + w_conv.shape[1:], lambda i: (1 - i, 0, 0))
    act = pl.BlockSpec((1, rows, ch), lambda i: (1 - i, 0, 0))
    return pl.pallas_call(
        units_back_body,
        grid=(2,),
        in_specs=[pl.BlockSpec(memory_space=pltpu.SMEM) if a is live_count or a is ids else whole(a.shape) for a in ins] + [kernels] + [act] * 4,
        out_specs=[kernels] + [whole(a.shape) for a in outs[1:]],
        out_shape=outs,
        scratch_shapes=[pltpu.VMEM((2, rows, 9 * ch), BF16), pltpu.VMEM((2, ch, 9 * ch), BF16), pltpu.VMEM((rows, ch), F32)],
        compiler_params=params(),
        cost_estimate=lasts(30),
        name="units_back",
    )(*ins, w_conv, t1, s1, t2, s2)


def hidden_back(dm, me, u, w2, split, block=512):
    rows, ff = u.shape
    sink = Sink([(ff, D)], split)
    n_out = len(sink.outs)

    def body(dm_ref, me_ref, u_ref, w2_ref, *refs):
        grads, du_ref, held = refs[:n_out], refs[n_out], refs[n_out + 1:]
        step = pl.program_id(0)
        at = pl.ds(pl.multiple_of(step * block, block), block)
        act, slope = gelu_pair(u_ref[...].astype(F32))
        sink.put(grads, held, 0, at, mm_tn(act.astype(BF16), dm_ref[...]))
        du_ref[...] = (mm_nt(dm_ref[...], w2_ref[...]) * slope).astype(BF16)

        @pl.when(step == pl.num_programs(0) - 1)
        def _():
            sink.deliver(me_ref, grads, held)

    cols = pl.BlockSpec((rows, block), lambda i: (0, i))
    out = pl.pallas_call(
        body,
        grid=(ff // block,),
        in_specs=[whole((rows, D)), pl.BlockSpec(memory_space=pltpu.SMEM), cols, pl.BlockSpec((block, D), lambda i: (i, 0))],
        out_specs=sink.out_specs() + [cols],
        out_shape=sink.outs + [spec((rows, ff))],
        scratch_shapes=sink.scratch,
        compiler_params=params(),
        cost_estimate=lasts(20),
        name="hidden_back",
    )(dm, me, u, w2)
    return out[:n_out], out[n_out]


def first_weight_back(du, me, a2, g_re, g_head, table, split, block=768):
    rows, ff = du.shape
    sink = Sink([(D, ff), g_re.shape, g_head.shape], split, True)
    n_out = len(sink.outs)
    half = ff // 2 // block

    def body(du_ref, me_ref, a2_ref, gre_ref, ghead_ref, table_ref, *refs):
        step = pl.program_id(0)
        grads, held = refs[:n_out], refs[n_out:]
        g = mm_tn(a2_ref[...], du_ref[...]).astype(BF16)
        cols = pl.ds(pl.multiple_of(step % half * block, block), block)
        if split == PLAIN:
            grads[0][:, pl.ds(pl.multiple_of(step * block, block), block)] = g
        else:
            held[0][step // half, :, cols] = g

        @pl.when(step == pl.num_programs(0) - 1)
        def _():
            sink.put(grads, held, 1, slice(0, g_re.shape[0]), gre_ref[...])
            sink.put(grads, held, 2, slice(0, g_head.shape[0]), ghead_ref[...])
            if split != PLAIN:
                held[-1][...] = table_ref[...].astype(BF16)
            sink.deliver(me_ref, grads, held)

    return pl.pallas_call(
        body,
        grid=(ff // block,),
        in_specs=[pl.BlockSpec((rows, block), lambda i: (0, i)), pl.BlockSpec(memory_space=pltpu.SMEM), whole((rows, D)),
                  whole(g_re.shape), whole(g_head.shape), whole(table.shape)],
        out_specs=sink.out_specs(),
        out_shape=sink.outs,
        scratch_shapes=sink.scratch,
        compiler_params=params(),
        cost_estimate=lasts(13),
        name="first_weight_back",
    )(du, me, a2, g_re, g_head, table)


def mlp_back_body(du_ref, w1_ref, dm_ref, x2_ref, gains_ref, da_ref):
    n2, rs2 = normalize(x2_ref[...].astype(F32))
    da2 = mm_nt(du_ref[...], w1_ref[...])
    da_ref[...] = (dm_ref[...].astype(F32) + norm_transpose(da2 * gains_ref[1:2], n2, rs2)).astype(BF16)


def mlp_back(du, w1, dm, x2, gains):
    rows, ff = du.shape
    block = rows // 4

    def cols(n):
        return pl.BlockSpec((block, n), lambda i: (i, 0))

    return pl.pallas_call(
        mlp_back_body,
        grid=(4,),
        in_specs=[cols(ff), whole(w1.shape), cols(D), cols(D), whole((2, D))],
        out_specs=cols(D),
        out_shape=spec((rows, D)),
        compiler_params=params(),
        cost_estimate=lasts(13),
        name="mlp_back",
    )(du, w1, dm, x2, gains)


def join_body(z_ref, w_ref, scale_ref, shift_ref, count_ref, out_ref, head_ref):
    step, images, size = pl.program_id(0), out_ref.shape[0], out_ref.shape[1]

    @pl.when(step == 0)
    def _():
        for i in range(images):
            head = mm(z_ref[COUNT * i:COUNT * (i + 1)], w_ref[...])
            head_ref[i] = head.astype(BF16)

    table = bilinear((size, 1), (1, COUNT), step * size)
    for i in range(images):
        out_ref[i] = ((mm(table, head_ref[i]) * scale_ref[i] + shift_ref[i]) * is_live(count_ref, i)).astype(BF16)


def join(z, w_head, scale, shift, live_count):
    images, ch = scale.shape[0], w_head.shape[1]
    one = whole((images, 1, ch))
    return pl.pallas_call(
        join_body,
        grid=(4,),
        in_specs=[whole(z.shape), whole(w_head.shape), one, one, pl.BlockSpec(memory_space=pltpu.SMEM)],
        out_specs=pl.BlockSpec((images, COUNT, ch), lambda i: (0, i, 0)),
        out_shape=spec((images, 4 * COUNT, ch)),
        scratch_shapes=[pltpu.VMEM((images, COUNT, ch), BF16)],
        compiler_params=params(),
        cost_estimate=lasts(7),
        name="join",
    )(z, w_head, scale, shift, live_count)


def shards(tokens, live_count, dataset_id, shift_flag, norm_gains, w_qkv, w_attn_out, w_fc1, w_fc2, w_reassemble,
           conv_kernels, w_head, scale_table, shift_table, d_tokens_out, d_joined):
    slots, count = tokens.shape[:2]
    rows = slots * count
    neighbours = (lax.axis_size("rep"), lax.axis_size("wide")) == (4, 8)
    ch, ff = w_head.shape[1], w_fc1.shape[1]
    wide = lax.axis_size("wide")
    at_wide = lax.axis_index("wide")
    g, t = norm_gains.shape[1], scale_table.shape[1]
    me = bit_vector()
    line = Line()
    r = D // 16

    def gathered(part, axis):
        return lax.all_gather(part, "wide", axis=axis, tiled=True)

    def rows_of(size):
        return lambda shard, y: (shard * 2 + y) * size

    def cols_of(size):
        return lambda x: x * size

    x = tokens.reshape(rows, D)

    if neighbours:
        pieces = line.run(lambda v: prepare(me, v, w_attn_out, w_fc1, w_fc2, w_reassemble, w_head, norm_gains, scale_table,
                                            shift_table), w_qkv)
        zero = Gather(pieces[0], 5 * LANES, 1, True)
    down, g_shift_rows = line.run(bring_down, d_joined, live_count, shift_flag)
    if neighbours:
        together(line, zero)
    if neighbours:
        one = Gather(line.after(pieces[1]), 9 * LANES, 1)
        together(line, zero)
        zero.between_cores()
    n1 = line.run(norm, x)
    if neighbours:
        f_qkv, small = line.run(lambda v: assemble(me, Assembly(zero.starting(v), [(D, 3 * D), (wide, r, LANES)], [
            (0, (0, r), (0, 3 * D // 2), rows_of(r), cols_of(3 * D // 2)), (1, (0, r), (3 * D // 2, LANES), None, None)])),
            zero.pieces[0])
        together(line, one)

        gains = small[:, 2 * SMALL:2 * SMALL + 2, :g].transpose(1, 0, 2).reshape(2, wide * g)
    else:
        gains, scales, shifts = gathered(norm_gains, 1), gathered(scale_table, 1), gathered(shift_table, 1)
        f_qkv = gathered(w_qkv, 0)

    gains = gains.astype(F32)
    a1 = line.run(lambda n: (n * gains[0:1]).astype(BF16), n1)
    groups = []
    for i in range(GROUPS):
        groups.append(line.run(attention, a1, f_qkv, i))
        if neighbours and i == 0:
            together(line, one)
            own = [swap(one.terms[0], "c"), swap(one.terms[2], "c")]
            two = Gather(line.after(pieces[2]), ff // 32, 0)
        if neighbours and i == 1:
            scale, shift = line.run(tables, small, dataset_id, shift_flag, ch)
            *one.terms, own_a, own_b = line.touch(*one.terms, *own)
            one.between_cores((own_a, own_b))
            together(line, two)
        if i == 1:
            f_conv = gathered(line.after(conv_kernels), 1)

    heads_out = [group[1] for group in groups]
    if not neighbours:
        onehot = (dataset_id[:, None] == jnp.arange(DATASETS, dtype=jnp.int32)[None, :]).astype(F32)
        scale = jnp.sum(onehot[:, :, None] * scales.astype(F32)[None], 1)[:, None]
        shift = jnp.sum(onehot[:, :, None] * shifts.astype(F32)[None], 1)[:, None] * shift_flag.astype(F32)[:, None, None]
    if neighbours:
        rh, at, n = ch // 16, D // 2 + ff // 2, ff // 16
        weights_one = Assembly(one, [(D, D), (D, ff), (D, ch), (ch, ch)], [
            (0, (0, r), (0, D // 2), rows_of(r), cols_of(D // 2)),
            (1, (0, r), (D // 2, ff // 2), rows_of(r), cols_of(ff // 2)),
            (2, (0, r), (at, ch // 2), rows_of(r), cols_of(ch // 2)),
            (3, (0, rh), (at + ch // 2, ch // 2), rows_of(rh), cols_of(ch // 2))])
        together(line, two)
        own = [swap(two.terms[0], "c"), swap(two.terms[2], "c")]
        (f_out, f_fc1, f_re, f_head), (x2, a2, u) = line.run(lambda v: mlp_up(v, heads_out, weights_one, me, gains), x)
        *two.terms, own_a, own_b = line.touch(*two.terms, *own)
        two.between_cores((own_a, own_b))
        weights_two = Assembly(two, [(ff, D)], [(0, (0, n), (0, D // 2), rows_of(n), cols_of(D // 2))])
        (f_fc2,), (x3b, tokens_out) = line.run(lambda v: mlp_down(v, weights_two, me, x2, live_count), u)
    else:
        f_out, f_fc1, f_re, f_head = gathered(w_attn_out, 0), gathered(w_fc1, 0), gathered(w_reassemble, 0), gathered(w_head, 0)
        f_fc2 = gathered(w_fc2, 0)
        _, (x2, a2, u) = mlp_up(x, heads_out, (f_out, f_fc1), me, gains)
        _, (x3b, tokens_out) = mlp_down(u, (f_fc2,), me, x2, live_count)
    t1, s1, t2, s2, zb = line.run(units, x3b, f_re, f_conv)

    def packed(split):
        return split if neighbours else PLAIN

    def chunk(grads, split):
        return Chunk(line, grads[0], grads[1], split) if neighbours else grads

    def go(*jobs):
        if neighbours:
            together(line, *jobs)

    g_conv, g_head, g_re, dm, small = line.run(
        lambda v: units_back(v, scale, g_shift_rows, dataset_id, zb, x3b, d_tokens_out.reshape(rows, D), live_count, f_head, f_conv, f_re,
                             t1, s1, t2, s2), down)
    s_conv = lax.psum_scatter(g_conv, "wide", scatter_dimension=1, tiled=True)
    split_two, split_one = 3 * ff // 32, 7 * r
    grads, du = line.run(lambda v: hidden_back(v, me, u, f_fc2, packed(split_two)), dm)
    c_two = chunk(grads, split_two)
    grads = line.run(lambda v: first_weight_back(v, me, a2, g_re, g_head, small, packed(split_one)), du)
    go(c_two)
    c_one = chunk(grads, split_one)
    da = line.run(lambda v: mlp_back(v, f_fc1, dm, x2, gains), du)
    go(c_two, c_one)

    def attention_step(i, extra, split):
        qkv, o, e, rs = groups[i]
        return line.run(lambda v: attention_back(v, me, i, qkv, o, e, rs, a1, f_out, extra, packed(split)), da)

    grads, dqkv_0 = attention_step(0, heads_out, ALL_XY)
    if neighbours:
        z_two = Along(c_two)
        together(line, z_two, c_one)
        c_first = Single(line, grads[0], grads[1], XY)
        c_conv = Whole(s_conv)
    else:
        c_first = grads
    (g_second,), dqkv_1 = attention_step(1, None, PLAIN)
    split_last = 3 * r
    if neighbours:
        z_one = Along(c_one)
        together(line, z_two, z_one, c_first, c_conv)
    grads, dqkv_2 = attention_step(2, g_second, split_last)
    if neighbours:
        c_conv.terms = line.touch(*c_conv.terms)
        together(line, z_one, c_first)
        c_last = Chunk(line, grads[0], grads[1], split_last)
    else:
        c_last = grads
    joined = line.run(join, zb, f_head, scale, shift, live_count)
    if neighbours:
        together(line, c_last, c_first)
    d_tokens = line.run(lambda v: input_back((dqkv_0, dqkv_1, v), f_qkv, da, x, gains), dqkv_2)

    if neighbours:
        together(line, c_last)
        rh, rows_two, half = ch // 16, ff // 16, D // 2
        blocks, n, quarter = half // LANES, ff // 2 // LANES, TABLE // 4

        def up_to(size):
            return lambda y: size * y

        def across(size):
            return lambda x, b: x * size + b * LANES

        def group_col(i):
            def col(x, b):
                at = blocks * x + b
                return at // 2 * D + WIDTH * i + at % 2 * LANES
            return col

        z_last = Along(c_first, c_last)
        together(line, z_last)
        early = Back(line, z_two, z_one)
        s_conv = line.run_all(lambda p, q: p.astype(F32) + q.astype(F32), *c_conv.terms)
        early.terms = line.touch(*early.terms)
        together(line, z_last)
        late = Back(line, z_last)
        low = early.rows[0]
        s_fc2, s_fc1, s_re, s_head, small = line.run(lambda m: finish(m, [early], [[
            (0, rows_two, 0, blocks, up_to(rows_two), across(half)),
            (1, r, low, n, up_to(r), across(ff // 2)),
            (2, r, low + r * n, 1, up_to(r), across(ch // 2)),
            (3, rh, low + r * (n + 1), 1, up_to(rh), across(ch // 2)),
            (4, quarter, low + r * (n + 1) + rh, 1, up_to(2 * quarter), lambda x, b: 0)]],
            [w_fc2.shape, w_fc1.shape, w_reassemble.shape, w_head.shape, (TABLE, LANES)]), me)
        s_qkv, s_out = finish(me, [late], [
            [(0, r, 0, blocks, up_to(r), group_col(0)), (1, r, r * blocks, blocks, up_to(r), across(half)),
             (0, r, 2 * r * blocks, blocks, up_to(r), group_col(2)), (0, r, 3 * r * blocks, blocks, up_to(r), group_col(1))]],
            [w_qkv.shape, w_attn_out.shape])
        small = small.reshape(2, ch // LANES, SMALL, LANES).transpose(0, 2, 1, 3).reshape(2, SMALL, ch)
        small = lax.dynamic_slice(small, (0, 0, at_wide * t), (2, DATASETS, t))
        g_scale, g_shift = small[0], small[1]
    else:
        def share(part, axis):
            part = lax.psum_scatter(part.astype(BF16), "wide", scatter_dimension=axis, tiled=True)
            return lax.psum(part, "rep").astype(F32)

        s_conv = lax.psum(s_conv, "rep").astype(F32)
        small = small.reshape(2, ch // LANES, SMALL, LANES).transpose(0, 2, 1, 3).reshape(2, SMALL, ch)[:, :DATASETS]
        g_scale, g_shift = share(small[0], 1), share(small[1], 1)
        s_fc2, s_fc1, s_re, s_head = share(c_two[0], 0), share(c_one[0], 0), share(c_one[1], 0), share(c_one[2], 0)
        s_out = share(c_first[1], 0)
        by_group = (c_first[0], c_last[1], c_last[0])
        s_qkv = share(jnp.concatenate([c[:, WIDTH * p:WIDTH * (p + 1)] for p in range(3) for c in by_group], 1), 0)
    g_gains = jnp.stack([jnp.sum(w_qkv.astype(F32) * s_qkv, 1), jnp.sum(w_fc1.astype(F32) * s_fc1, 1)]) / norm_gains.astype(F32)
    return (tokens_out.reshape(tokens.shape), joined, d_tokens.reshape(tokens.shape), g_gains, s_qkv, s_out, s_fc1, s_fc2,
            s_re, s_conv, s_head, g_scale, g_shift)


def solution(mesh):
    images = P(BOTH, None, None)
    slots = P(BOTH)
    rows = P("wide", None)
    cols = P(None, "wide")
    kernels = P(None, "wide", None)
    return jax.shard_map(
        shards,
        mesh=mesh,
        in_specs=(images, slots, slots, slots, cols, rows, rows, rows, rows, rows, kernels, rows, cols, cols, images, images),
        out_specs=(images, images, images, cols, rows, rows, rows, rows, rows, kernels, rows, cols, cols),
        check_vma=False,
    )
```
